32 devices in a mesh: dp: 4 (over y, core), frame: 2 (over x), tensor: 4 (over z).
Axes of the slice: x: 2, y: 2, z: 4, core: 2. Of those that a mesh axis runs over, the one named last changes fastest.
Arguments:
- latent: bfloat16 [12, 16, 32, 128], P('dp', 'frame', 'tensor'), may hold values from -5 to 5
- noise_draw: bfloat16 [12, 16, 32, 128], P('dp', 'frame', 'tensor'), may hold values from -5 to 5
- levels: int32 [12, 16], P('dp', 'frame'), may hold values from 1 to 999
- context: int32 [12], replicated, may hold values from 1 to 15
- step_count: int32 [1], replicated, may hold values from 1 to 20
- w_in: float32 [1024, 7168], P(('dp', 'frame'), 'tensor'), may hold values from -0.1875 to 0.1875
- w_outs: float32 [5120, 1024], P('tensor', ('dp', 'frame')), may hold values from -2 to 2, as said below
- w_cond: float32 [1024, 8192], P(('dp', 'frame'), 'tensor'), may hold values from -0.1875 to 0.1875
- w_time: float32 [1280, 1024], P(('dp', 'frame')), may hold values from -0.5 to 0.5
- w_patch: float32 [2, 16, 1024], P(None, None, ('dp', 'frame')), may hold values from -0.75 to 0.75
- m_in: float32 [1024, 7168], P(('dp', 'frame'), 'tensor'), may hold values from -0.00012207031 to 0.00012207031
- m_outs: float32 [5120, 1024], P('tensor', ('dp', 'frame')), may hold values from -3.8146973e-05 to 3.8146973e-05
- m_cond: float32 [1024, 8192], P(('dp', 'frame'), 'tensor'), may hold values from -0.00012207031 to 0.00012207031
- m_time: float32 [1280, 1024], P(('dp', 'frame')), may hold values from -0.00012207031 to 0.00012207031
- m_patch: float32 [2, 16, 1024], P(None, None, ('dp', 'frame')), may hold values from -0.00012207031 to 0.00012207031
- v_in: float32 [1024, 7168], P(('dp', 'frame'), 'tensor'), may hold values from 4.481289e-10 to 1.7925156e-09
- v_outs: float32 [5120, 1024], P('tensor', ('dp', 'frame')), may hold values from 4.481289e-11 to 1.7925156e-10
- v_cond: float32 [1024, 8192], P(('dp', 'frame'), 'tensor'), may hold values from 4.481289e-10 to 1.7925156e-09
- v_time: float32 [1280, 1024], P(('dp', 'frame')), may hold values from 4.481289e-10 to 1.7925156e-09
- v_patch: float32 [2, 16, 1024], P(None, None, ('dp', 'frame')), may hold values from 4.481289e-10 to 1.7925156e-09
Outputs:
- loss_value: float32 [], replicated
- grad_norm: float32 [], replicated
- new_in: float32 [1024, 7168], P(('dp', 'frame'), 'tensor')
- new_outs: float32 [5120, 1024], P('tensor', ('dp', 'frame'))
- new_cond: float32 [1024, 8192], P(('dp', 'frame'), 'tensor')
- new_time: float32 [1280, 1024], P(('dp', 'frame'))
- new_patch: float32 [2, 16, 1024], P(None, None, ('dp', 'frame'))
- first_in: float32 [1024, 7168], P(('dp', 'frame'), 'tensor')
- first_outs: float32 [5120, 1024], P('tensor', ('dp', 'frame'))
- first_cond: float32 [1024, 8192], P(('dp', 'frame'), 'tensor')
- first_time: float32 [1280, 1024], P(('dp', 'frame'))
- first_patch: float32 [2, 16, 1024], P(None, None, ('dp', 'frame'))
- second_in: float32 [1024, 7168], P(('dp', 'frame'), 'tensor')
- second_outs: float32 [5120, 1024], P('tensor', ('dp', 'frame'))
- second_cond: float32 [1024, 8192], P(('dp', 'frame'), 'tensor')
- second_time: float32 [1280, 1024], P(('dp', 'frame'))
- second_patch: float32 [2, 16, 1024], P(None, None, ('dp', 'frame'))
- half_in: bfloat16 [1024, 7168], P(('dp', 'frame'), 'tensor')
- half_outs: bfloat16 [5120, 1024], P('tensor', ('dp', 'frame'))
- half_cond: bfloat16 [1024, 8192], P(('dp', 'frame'), 'tensor')
- half_time: bfloat16 [1280, 1024], P(('dp', 'frame'))
- half_patch: bfloat16 [2, 16, 1024], P(None, None, ('dp', 'frame'))
The draws below stay inside these ranges and needn't reach their ends.
Inputs may be any that keep to these rules, and one draw needn't show every extreme that they name: `w_outs`: output-projection and down-projection weights.
All inputs are finite; a program needn't handle non-finite values.
Results may differ from the reference program's by a relative error of at most 0.017.
Values may be sent and summed in bfloat16 or wider, within the bound.
A program may use at most 512 MiB of HBM per device.

```python
import math
import jax
import jax.numpy as jnp
from jax import lax

D = 1024
HEADS = 16
HD = 64
FF = 4096
TEMB = 256
CHANNELS = 4
PATCH = 2
PD = 16
HL = 32
WL = 32
TOKF = 256
FRAMES = 16
NLEV = 1000
CLIPS = 12
NPARAM = 22315008
N_TENSOR = 4


def draw_w_outs(key, part):
    head_cols = D // N_TENSOR
    hidden_cols = FF // N_TENSOR
    block_rows = head_cols + hidden_cols
    row_place = jnp.arange(N_TENSOR * block_rows) % block_rows
    scales = jnp.where(row_place < head_cols, 0.5, FF ** (-0.5)).astype(jnp.float32)
    values = jax.random.truncated_normal(key, -4.0, 4.0, (D + FF, D), jnp.float32)
    return values * scales[:, None]


def touch_ends(result, key, low, high):
    place = [jax.random.randint(jax.random.fold_in(key, axis), (), 0, length) for axis, length in enumerate(result.shape)]
    longest = result.shape.index(max(result.shape))
    neighbour = place[:longest] + [(place[longest] + 1) % result.shape[longest]] + place[longest + 1:]
    return result.at[tuple(place)].set(low).at[tuple(neighbour)].set(high)


def block_scale(rng, shape, cuts, low, high):
    gain = 1.0
    for dim, blocks in cuts:
        draws = jax.random.uniform(jax.random.fold_in(jax.random.fold_in(rng, 6), dim), (blocks,), jnp.float32, low / len(cuts), high / len(cuts))
        gain = gain * jnp.repeat(jnp.exp(draws), shape[dim] // blocks).reshape((-1,) + (1,) * (len(shape) - 1 - dim))
    return gain


def normal_values(own_key, shape, width, limit, split=(), held_as=jnp.bfloat16):
    values = jax.random.normal(own_key, shape, jnp.float32) * width
    if len(split) > 0:
        values = block_scale(own_key, shape, split, -0.22, 0.18) * values
    return jnp.clip(values, min=-limit, max=limit).astype(held_as)


def setup_inputs(seed: int = 0) -> dict:
    splits = jax.random.split(jax.random.key(seed), 21)
    return {
        "latent": normal_values(splits[0], (CLIPS, FRAMES, HL, WL * CHANNELS), 1.0, 5.0, ((0, 4), (1, 2), (2, 4))),
        "noise_draw": normal_values(splits[1], (CLIPS, FRAMES, HL, WL * CHANNELS), 1.0, 5.0, ((0, 4), (1, 2), (2, 4))),
        "levels": touch_ends(jax.random.randint(splits[2], (CLIPS, FRAMES), 1, NLEV), jax.random.fold_in(splits[2], 1), 1, NLEV - 1).astype(jnp.int32),
        "context": touch_ends(jax.random.randint(splits[3], (CLIPS,), 1, FRAMES), jax.random.fold_in(splits[3], 1), 1, FRAMES - 1).astype(jnp.int32),
        "step_count": jax.random.randint(splits[4], (1,), 1, 21).astype(jnp.int32),
        "w_in": normal_values(splits[5], (D, 3 * D + FF), D ** -0.5, 0.1875, ((0, 8), (1, 4)), jnp.float32),
        "w_outs": draw_w_outs(jax.random.fold_in(splits[20], 71), 0),
        "w_cond": normal_values(splits[7], (D, 8 * D), D ** -0.5, 0.1875, ((0, 8), (1, 4)), jnp.float32),
        "w_time": normal_values(splits[8], (TEMB + D, D), (TEMB // 2) ** -0.5, 0.5, ((0, 8),), jnp.float32),
        "w_patch": normal_values(splits[9], (2, PD, D), (D // 16) ** -0.5, 0.75, ((2, 8),), jnp.float32),
        "m_in": normal_values(splits[10], (D, 3 * D + FF), (0.1 * NPARAM ** -0.5), 0.00012207031, ((0, 8), (1, 4)), jnp.float32),
        "m_outs": normal_values(splits[11], (D + FF, D), (0.03 * NPARAM ** -0.5), 3.814697265625e-05, ((0, 4), (1, 8)), jnp.float32),
        "m_cond": normal_values(splits[12], (D, 8 * D), (0.1 * NPARAM ** -0.5), 0.00012207031, ((0, 8), (1, 4)), jnp.float32),
        "m_time": normal_values(splits[13], (TEMB + D, D), (0.1 * NPARAM ** -0.5), 0.00012207031, ((0, 8),), jnp.float32),
        "m_patch": normal_values(splits[14], (2, PD, D), (0.1 * NPARAM ** -0.5), 0.00012207031, ((2, 8),), jnp.float32),
        "v_in": jnp.clip(jnp.exp(math.log(1.7925155804121573e-09) - 1.3862944 * jax.random.uniform(splits[15], (D, 3 * D + FF), jnp.float32) ** block_scale(splits[15], (D, 3 * D + FF), ((0, 8), (1, 4)), -0.2, 0.2)), 4.4812889510303933e-10, 1.7925155804121573e-09),
        "v_outs": jnp.clip(jnp.exp(math.log(1.7925155804121573e-10) - 1.3862944 * jax.random.uniform(splits[16], (D + FF, D), jnp.float32) ** block_scale(splits[16], (D + FF, D), ((0, 4), (1, 8)), -0.2, 0.2)), 4.481288951030393e-11, 1.7925155804121573e-10),
        "v_cond": jnp.clip(jnp.exp(math.log(1.7925155804121573e-09) - 1.3862944 * jax.random.uniform(splits[17], (D, 8 * D), jnp.float32) ** block_scale(splits[17], (D, 8 * D), ((0, 8), (1, 4)), -0.2, 0.2)), 4.4812889510303933e-10, 1.7925155804121573e-09),
        "v_time": jnp.clip(jnp.exp(math.log(1.7925155804121573e-09) - 1.3862944 * jax.random.uniform(splits[18], (TEMB + D, D), jnp.float32) ** block_scale(splits[18], (TEMB + D, D), ((0, 8),), -0.2, 0.2)), 4.4812889510303933e-10, 1.7925155804121573e-09),
        "v_patch": jnp.clip(jnp.exp(math.log(1.7925155804121573e-09) - 1.3862944 * jax.random.uniform(splits[19], (2, PD, D), jnp.float32) ** block_scale(splits[19], (2, PD, D), ((2, 8),), -0.2, 0.2)), 4.4812889510303933e-10, 1.7925155804121573e-09),
    }


EPS_NORM = 1e-06
MAX_NORM = 0.1
LEARN_RATE = 0.08
WEIGHT_DECAY = 0.1
BETA_FIRST = 0.5
BETA_SECOND = 0.5
ADAM_EPS = 1e-08

@jax.custom_vjp
def low(v):
    return lax.optimization_barrier(v.astype(jnp.bfloat16)).astype(jnp.float32)

@jax.custom_vjp
def low_back(v):
    return v

def low_keep(v):
    return (low(v), None)

def low_pass(kept, grad):
    return (grad,)

def back_keep(v):
    return (v, None)

def back_low(kept, grad):
    return (low(grad),)
low.defvjp(low_keep, low_pass)
low_back.defvjp(back_keep, back_low)

def matmul(left_mat, right_mat):
    return jnp.dot(left_mat, right_mat, precision=lax.Precision.HIGHEST)

def frequency_table(level_values):
    half_width = TEMB // 2
    rate_table = jnp.exp(-math.log(10000.0) * jnp.arange(half_width, dtype=jnp.float32) / half_width)
    angles = level_values[..., None] * rate_table
    return jnp.concatenate([jnp.cos(angles), jnp.sin(angles)], axis=-1)

def noise_terms(level_values):
    angles = level_values * (0.5 * math.pi / NLEV)
    return (jnp.cos(angles), jnp.sin(angles))

def modulate(residual, shift_rows, scale_rows):
    centre = residual - lax.optimization_barrier(jnp.mean(residual, axis=-1, keepdims=True))
    spread = lax.optimization_barrier(jnp.mean(centre * centre, axis=-1, keepdims=True))
    return centre * lax.rsqrt(spread + EPS_NORM) * (1.0 + scale_rows) + shift_rows

def patchify(field_in):
    lead_shape = field_in.shape[:-2]
    rows_here = field_in.shape[-2]
    width_cells = field_in.shape[-1] // CHANNELS
    lead_rank = len(lead_shape)
    blocks_view = field_in.reshape(lead_shape + (rows_here // PATCH, PATCH, width_cells // PATCH, PATCH, CHANNELS))
    order_axes = tuple(range(lead_rank)) + (lead_rank, lead_rank + 2, lead_rank + 1, lead_rank + 3, lead_rank + 4)
    return jnp.transpose(blocks_view, order_axes).reshape(lead_shape + (rows_here // PATCH * (width_cells // PATCH), PATCH * PATCH * CHANNELS))

def unpack_weights(w_in, w_outs, w_cond, w_time, w_patch):
    head_cols = D // N_TENSOR
    hidden_cols = FF // N_TENSOR
    col_blocks = w_in.reshape(D, N_TENSOR, 3 * head_cols + hidden_cols)
    w_query = col_blocks[:, :, :head_cols].reshape(D, D)
    w_key = col_blocks[:, :, head_cols:2 * head_cols].reshape(D, D)
    w_value = col_blocks[:, :, 2 * head_cols:3 * head_cols].reshape(D, D)
    w_up = col_blocks[:, :, 3 * head_cols:].reshape(D, FF)
    row_blocks = w_outs.reshape(N_TENSOR, head_cols + hidden_cols, D)
    w_out = row_blocks[:, :head_cols].reshape(D, D)
    w_down = row_blocks[:, head_cols:].reshape(FF, D)
    return (w_query, w_key, w_value, w_up, w_out, w_down, w_cond, w_time[:TEMB], w_time[TEMB:], w_patch[0], w_patch[1])

def attention(query_rows, key_rows, value_rows):
    tokens_all = query_rows.shape[0]
    block_rows = min(512, tokens_all)
    scale_value = HD ** (-0.5)
    query_blocks = query_rows.reshape(tokens_all // block_rows, block_rows, HEADS, HD)
    key_heads = key_rows.reshape(tokens_all, HEADS, HD)
    value_heads = value_rows.reshape(tokens_all, HEADS, HD)

    def one_block(query_block):
        scores = low_back(jnp.einsum('qhe,khe->hqk', query_block, key_heads, precision=lax.Precision.HIGHEST) * scale_value)
        soft_probs = low(jax.nn.softmax(scores, axis=-1))
        return jnp.einsum('hqk,khe->qhe', soft_probs, value_heads, precision=lax.Precision.HIGHEST)
    return lax.map(jax.checkpoint(one_block), query_blocks).reshape(tokens_all, HEADS * HD)

def clip_loss(params, latent_clip, noise_clip, level_clip, context_one, token_total):
    w_query, w_key, w_value, w_up, w_out, w_down, w_cond, w_first, w_second, w_embed, w_head = params
    clean_frames = jnp.arange(FRAMES) < context_one
    level_values = jnp.where(clean_frames, 0, level_clip).astype(jnp.float32)
    alpha_coef, sigma_coef = noise_terms(level_values)
    hidden_time = low_back(matmul(low(frequency_table(level_values)), w_first))
    cond_vec = low_back(matmul(low(jax.nn.silu(hidden_time)), w_second))
    modulation = low_back(matmul(low(jax.nn.silu(cond_vec)), w_cond))
    pieces = [modulation[:, None, which_piece * D:(which_piece + 1) * D] for which_piece in range(8)]
    alpha_field = alpha_coef[:, None, None]
    sigma_field = sigma_coef[:, None, None]
    noisy_field = alpha_field * latent_clip + sigma_field * noise_clip
    target = alpha_field * noise_clip - sigma_field * latent_clip
    patches = patchify(noisy_field)
    goal_rows = patchify(target)
    residual = low_back(matmul(low(patches.reshape(-1, PD)), w_embed)).reshape(FRAMES, TOKF, D)
    normed = low(modulate(residual, pieces[0], pieces[1])).reshape(-1, D)
    query_rows = low(low_back(matmul(normed, w_query)))
    key_rows = low(low_back(matmul(normed, w_key)))
    value_rows = low(low_back(matmul(normed, w_value)))
    mixed_rows = low(low_back(attention(query_rows, key_rows, value_rows)))
    branch = low_back(matmul(mixed_rows, w_out)).reshape(FRAMES, TOKF, D)
    residual = residual + pieces[2] * branch
    normed = low(modulate(residual, pieces[3], pieces[4])).reshape(-1, D)
    hidden = low_back(matmul(normed, w_up))
    branch = low_back(matmul(low(jax.nn.gelu(hidden, approximate=True)), w_down)).reshape(FRAMES, TOKF, D)
    residual = residual + pieces[5] * branch
    final_rows = low(modulate(residual, pieces[6], pieces[7])).reshape(-1, D)
    predicted = low_back(matmul(final_rows, w_head.T)).reshape(FRAMES, TOKF, PD)
    error_rows = predicted - goal_rows
    weight_rows = (1.0 - clean_frames.astype(jnp.float32))[:, None, None]
    return jnp.sum(weight_rows * error_rows * error_rows) / token_total

def adam_update(master, first_old, second_old, grad_in, factor, fix_first, fix_second):
    clipped = grad_in * factor
    first_new = BETA_FIRST * first_old + (1.0 - BETA_FIRST) * clipped
    second_new = BETA_SECOND * second_old + (1.0 - BETA_SECOND) * clipped * clipped
    step_dir = first_new / fix_first / (jnp.sqrt(second_new / fix_second) + ADAM_EPS)
    master_new = master - LEARN_RATE * (step_dir + WEIGHT_DECAY * master)
    return (master_new, first_new, second_new)

def reference(latent, noise_draw, levels, context, step_count, w_in, w_outs, w_cond, w_time, w_patch, m_in, m_outs, m_cond, m_time, m_patch, v_in, v_outs, v_cond, v_time, v_patch):
    masters = (w_in, w_outs, w_cond, w_time, w_patch)
    token_total = (TOKF * jnp.sum(FRAMES - context)).astype(jnp.float32)
    latent_full = latent.astype(jnp.float32)
    noise_full = noise_draw.astype(jnp.float32)

    def total_loss(weights):
        params = unpack_weights(low(weights[0]), low(weights[1]), low(weights[2]), low(weights[3]), low(weights[4]))

        def one_clip(loss_acc, inputs):
            return (loss_acc + clip_loss(params, inputs[0], inputs[1], inputs[2], inputs[3], token_total), None)
        loss_total, unused = lax.scan(one_clip, jnp.zeros((), jnp.float32), (latent_full, noise_full, levels, context))
        return loss_total
    loss_value, pullback = jax.vjp(total_loss, masters)
    grad_set = pullback(jnp.ones((), jnp.float32))[0]
    grad_norm = jnp.sqrt(sum((jnp.sum(grad_in * grad_in) for grad_in in grad_set)))
    factor = jnp.minimum(1.0, MAX_NORM / (grad_norm + 1e-06))
    steps_done = step_count[0].astype(jnp.float32)
    fix_first = 1.0 - BETA_FIRST ** steps_done
    fix_second = 1.0 - BETA_SECOND ** steps_done
    firsts = (m_in, m_outs, m_cond, m_time, m_patch)
    seconds = (v_in, v_outs, v_cond, v_time, v_patch)
    results = [adam_update(masters[which], firsts[which], seconds[which], grad_set[which], factor, fix_first, fix_second) for which in range(5)]
    return (loss_value, grad_norm, results[0][0], results[1][0], results[2][0], results[3][0], results[4][0], results[0][1], results[1][1], results[2][1], results[3][1], results[4][1], results[0][2], results[1][2], results[2][2], results[3][2], results[4][2], results[0][0].astype(jnp.bfloat16), results[1][0].astype(jnp.bfloat16), results[2][0].astype(jnp.bfloat16), results[3][0].astype(jnp.bfloat16), results[4][0].astype(jnp.bfloat16))
```

```python
from functools import partial
import math

import jax
import jax.numpy as jnp
from jax import lax
from jax.experimental import pallas as pl
from jax.experimental.pallas import tpu as pltpu
from jax.sharding import PartitionSpec as P

D = 1024
HD = 64
TEMB = 256
CHANNELS = 4
PATCH = 2
PD = 16
TOKF = 256
FRAMES = 16
NLEV = 1000
PAIR = 2 * HD
PLANE = ("dp", "frame")
EVERY = ("tensor", "dp", "frame")
SCORE_SCALE = HD ** (-0.5) * math.log2(math.e)
TOTAL_LOW = 2.0**-40
TOTAL_HIGH = 2.0**70


EPS_NORM = 1e-06
MAX_NORM = 0.1
LEARN_RATE = 0.08
WEIGHT_DECAY = 0.1
BETA_FIRST = 0.5
BETA_SECOND = 0.5
ADAM_EPS = 1e-08


def to_half(array_in):
    return array_in.astype(jnp.bfloat16)


def product(left_mat, right_mat):
    return jnp.dot(left_mat, right_mat, preferred_element_type=jnp.float32)


def rows_product(left_mat, right_mat):
    return lax.dot_general(
        left_mat, right_mat, (((0,), (0,)), ((), ())), preferred_element_type=jnp.float32
    )


def cols_product(left_mat, right_mat):
    return lax.dot_general(
        left_mat, right_mat, (((1,), (1,)), ((), ())), preferred_element_type=jnp.float32
    )


def frequency_table(level_values):
    half_width = TEMB // 2
    rate_table = jnp.exp(
        -math.log(10000.0) * jnp.arange(half_width, dtype=jnp.float32) / half_width
    )
    angles = level_values[..., None] * rate_table
    return jnp.concatenate([jnp.cos(angles), jnp.sin(angles)], axis=-1)


def noise_terms(level_values):
    angles = level_values * (0.5 * math.pi / NLEV)
    return (jnp.cos(angles), jnp.sin(angles))


def modulate(residual, shift_rows, scale_rows):
    centre = residual - jnp.mean(residual, axis=-1, keepdims=True)
    spread = jnp.mean(centre * centre, axis=-1, keepdims=True)
    return centre * lax.rsqrt(spread + EPS_NORM) * (1.0 + scale_rows) + shift_rows


def modulate_back(residual, shift_rows, scale_rows, grad_out):
    unused, pullback = jax.vjp(modulate, residual, shift_rows, scale_rows)
    return pullback(grad_out)


def patchify(field_in):
    lead_shape = field_in.shape[:-2]
    rows_here = field_in.shape[-2]
    width_cells = field_in.shape[-1] // CHANNELS
    lead_rank = len(lead_shape)
    blocks_view = field_in.reshape(
        lead_shape + (rows_here // PATCH, PATCH, width_cells // PATCH, PATCH, CHANNELS)
    )
    order_axes = tuple(range(lead_rank)) + (
        lead_rank,
        lead_rank + 2,
        lead_rank + 1,
        lead_rank + 3,
        lead_rank + 4,
    )
    return jnp.transpose(blocks_view, order_axes).reshape(
        lead_shape + (rows_here // PATCH * (width_cells // PATCH), PATCH * PATCH * CHANNELS)
    )


def contract(left_mat, right_mat, left_dim, right_dim):
    return lax.dot_general(
        left_mat,
        right_mat,
        (((left_dim,), (right_dim,)), ((), ())),
        preferred_element_type=jnp.float32,
    )


def head_lanes(head):
    return lax.broadcasted_iota(jnp.int32, (1, PAIR), 1) // HD == head


def attend_kernel(chunk, query_ref, key_ref, value_ref, exps_ref, low_ref, mixed_ref, inverse_ref):
    key_total = key_ref.shape[1]
    block_rows = query_ref.shape[1]
    query_pair = query_ref[0]
    mixed_parts = []
    inverse_parts = []
    for head in range(2):
        lanes = head_lanes(head)
        query_head = jnp.where(lanes, query_pair, jnp.zeros_like(query_pair))

        def scores_of(rows):
            return contract(key_ref[0, rows, :], query_head, 1, 1) * SCORE_SCALE

        def add_chunk(rows, scores, total):
            exps = jnp.exp2(scores).astype(jnp.bfloat16)
            exps_ref[0, head, :, rows] = exps.T
            values = value_ref[0, rows, :]
            values = jnp.where(lanes, values, jnp.ones_like(values))
            return total + contract(values, exps, 0, 0)

        zeros = jnp.zeros((PAIR, block_rows), jnp.float32)
        total = zeros
        for start in range(0, key_total, chunk):
            rows = slice(start, start + chunk)
            total = add_chunk(rows, scores_of(rows), total)
        sum_rows = total[(1 - head) * HD : (1 - head) * HD + 8]
        outside = jnp.max(
            jnp.where((sum_rows > TOTAL_LOW) & (sum_rows < TOTAL_HIGH), 0.0, 1.0)
        )

        def shifted(unused):
            def chunk_rows(step):
                return pl.ds(pl.multiple_of(step * chunk, chunk), chunk)

            def highest(step, top):
                return jnp.maximum(
                    top, jnp.max(scores_of(chunk_rows(step)), axis=0, keepdims=True)
                )

            top = lax.fori_loop(
                0, key_total // chunk, highest, jnp.full((1, block_rows), -jnp.inf, jnp.float32)
            )

            def one_chunk(step, total):
                rows = chunk_rows(step)
                return add_chunk(rows, scores_of(rows) - top, total)

            return lax.fori_loop(0, key_total // chunk, one_chunk, zeros)

        total = lax.cond(outside > 0.0, shifted, lambda kept: kept, total)
        inverse = 1.0 / total[(1 - head) * HD : (2 - head) * HD]
        mixed_parts.append(total[head * HD : (head + 1) * HD] * inverse)
        inverse_parts.append(inverse)
    mixed = jnp.concatenate(mixed_parts, axis=0).T
    mixed_ref[0] = mixed
    low_ref[0] = mixed.astype(jnp.bfloat16)
    inverse_ref[0] = jnp.concatenate(inverse_parts, axis=0).T


def attend(query_in, key_value, key_place):
    units, query_total = query_in.shape[:2]
    key_total = key_value.shape[1]
    block_rows = min(1024, query_total)
    chunk = min(1024, key_total)

    def query_map(unit, step):
        return (unit, step, 0)

    query_spec = pl.BlockSpec((1, block_rows, PAIR), query_map)
    shape_rows = (units, query_total, PAIR)
    products = 4 * units * query_total * key_total * PAIR
    return pl.pallas_call(
        partial(attend_kernel, chunk),
        grid=(units, query_total // block_rows),
        in_specs=[
            query_spec,
            pl.BlockSpec((1, key_total, PAIR), lambda unit, step: (unit, 0, key_place)),
            pl.BlockSpec((1, key_total, PAIR), lambda unit, step: (unit, 0, key_place + 1)),
        ],
        out_specs=[
            pl.BlockSpec((1, 2, block_rows, key_total), lambda unit, step: (unit, 0, step, 0)),
            query_spec,
            query_spec,
            query_spec,
        ],
        out_shape=[
            jax.ShapeDtypeStruct((units, 2, query_total, key_total), jnp.bfloat16),
            jax.ShapeDtypeStruct(shape_rows, jnp.bfloat16),
            jax.ShapeDtypeStruct(shape_rows, jnp.float32),
            jax.ShapeDtypeStruct(shape_rows, jnp.float32),
        ],
        cost_estimate=pl.CostEstimate(
            flops=4 * products,
            bytes_accessed=4 * units * query_total * key_total,
            transcendentals=2 * units * query_total * key_total,
        ),
        compiler_params=pltpu.CompilerParams(vmem_limit_bytes=62 << 20),
    )(query_in, key_value, key_value)


def attend_back_kernel(
    chunk,
    exps_ref,
    query_ref,
    key_ref,
    value_ref,
    grad_ref,
    mixed_ref,
    inverse_ref,
    grad_query_ref,
    grad_key_ref,
    grad_value_ref,
    key_sums,
    value_sums,
):
    step = pl.program_id(1)
    head = pl.program_id(2)
    key_total = key_ref.shape[1]
    block_rows = query_ref.shape[1]
    lane = lax.broadcasted_iota(jnp.int32, (1, PAIR), 1)
    lanes = head_lanes(head)
    grad_low = jnp.where(lanes, grad_ref[0].astype(jnp.float32) * inverse_ref[0], 0.0).astype(
        jnp.bfloat16
    )
    row_terms = jnp.sum(grad_low.astype(jnp.float32) * mixed_ref[0], axis=1, keepdims=True)
    term_high = row_terms.astype(jnp.bfloat16).astype(jnp.float32)
    term_rest = row_terms - term_high
    term_lanes = jnp.where(lane == 0, -term_high, jnp.where(lane == 1, -term_rest, 0.0))
    grad_wide = jnp.concatenate([grad_low, term_lanes.astype(jnp.bfloat16)], axis=1)
    query_pair = query_ref[0]
    query_columns = jnp.where(lanes, query_pair, jnp.zeros_like(query_pair)).T
    grad_columns = grad_low.T
    term_ones = jnp.broadcast_to(jnp.where(lane < 2, 1.0, 0.0).astype(jnp.bfloat16), (chunk, PAIR))

    @pl.when((step == 0) & (head == 0))
    def start_sums():
        key_sums[...] = jnp.zeros_like(key_sums)
        value_sums[...] = jnp.zeros_like(value_sums)

    grad_query = jnp.zeros((block_rows, PAIR), jnp.float32)
    for start in range(0, key_total, chunk):
        rows = slice(start, start + chunk)
        values_wide = jnp.concatenate([value_ref[0, rows, :], term_ones], axis=1)
        grad_probs = contract(grad_wide, values_wide, 1, 1).astype(jnp.bfloat16)
        exps = exps_ref[0, 0, :, rows]
        grad_scores = exps * grad_probs
        value_sums[:, rows] += contract(grad_columns, exps, 1, 0)
        key_sums[:, rows] += contract(query_columns, grad_scores, 1, 0)
        keys = key_ref[0, rows, :]
        keys = jnp.where(lanes, keys, jnp.zeros_like(keys))
        grad_query = grad_query + contract(grad_scores, keys, 1, 0)
    grad_query_low = (grad_query * HD ** (-0.5)).astype(jnp.bfloat16)

    @pl.when(head == 0)
    def first_head():
        grad_query_ref[0] = grad_query_low

    @pl.when(head == 1)
    def second_head():
        grad_query_ref[0] = jnp.where(lanes, grad_query_low, grad_query_ref[0])

    @pl.when((step == pl.num_programs(1) - 1) & (head == 1))
    def write_sums():
        grad_key_ref[0] = (key_sums[...].T * HD ** (-0.5)).astype(jnp.bfloat16)
        grad_value_ref[0] = value_sums[...].T.astype(jnp.bfloat16)


def attend_back(exps, query_in, key_value, key_place, grad_mixed, mixed, inverse):
    units, query_total = mixed.shape[:2]
    key_total = key_value.shape[1]
    block_rows = min(1024, query_total)
    chunk = min(1024, key_total)
    query_spec = pl.BlockSpec((1, block_rows, PAIR), lambda unit, step, head: (unit, step, 0))
    whole_spec = pl.BlockSpec((1, key_total, PAIR), lambda unit, step, head: (unit, 0, 0))
    products = 8 * units * query_total * key_total * PAIR
    return pl.pallas_call(
        partial(attend_back_kernel, chunk),
        grid=(units, query_total // block_rows, 2),
        in_specs=[
            pl.BlockSpec(
                (1, 1, block_rows, key_total), lambda unit, step, head: (unit, head, step, 0)
            ),
            query_spec,
            pl.BlockSpec((1, key_total, PAIR), lambda unit, step, head: (unit, 0, key_place)),
            pl.BlockSpec((1, key_total, PAIR), lambda unit, step, head: (unit, 0, key_place + 1)),
            query_spec,
            query_spec,
            query_spec,
        ],
        out_specs=[query_spec, whole_spec, whole_spec],
        out_shape=[
            jax.ShapeDtypeStruct((units, query_total, PAIR), jnp.bfloat16),
            jax.ShapeDtypeStruct((units, key_total, PAIR), jnp.bfloat16),
            jax.ShapeDtypeStruct((units, key_total, PAIR), jnp.bfloat16),
        ],
        scratch_shapes=[pltpu.VMEM((PAIR, key_total), jnp.float32)] * 2,
        cost_estimate=pl.CostEstimate(
            flops=4 * products,
            bytes_accessed=4 * units * query_total * key_total,
            transcendentals=0,
        ),
        compiler_params=pltpu.CompilerParams(vmem_limit_bytes=62 << 20),
    )(exps, query_in, key_value, key_value, grad_mixed, mixed, inverse)


def swap_groups(array_in):
    dp_size = lax.axis_size("dp")
    tensor_size = lax.axis_size("tensor")
    pairs = [
        (row * tensor_size + column, column * dp_size + row)
        for row in range(dp_size)
        for column in range(tensor_size)
    ]
    return lax.ppermute(array_in, ("dp", "tensor"), pairs)


def spread_heads():
    return (D // PAIR) % (lax.axis_size("dp") * lax.axis_size("frame")) == 0


def to_heads(rows_in):
    tokens, pairs, columns = rows_in.shape
    axes = PLANE if spread_heads() else ("dp",)
    parts = math.prod(lax.axis_size(axis) for axis in axes)
    by_pair = jnp.transpose(rows_in, (1, 0, 2)).reshape(parts, pairs // parts, tokens, columns)
    moved = lax.all_to_all(by_pair, axes, 0, 0, tiled=True)
    return jnp.transpose(moved, (1, 0, 2, 3)).reshape(pairs // parts, parts * tokens, columns)


def to_tokens(units_in):
    axes = PLANE if spread_heads() else ("dp",)
    parts = math.prod(lax.axis_size(axis) for axis in axes)
    units, tokens_all, columns = units_in.shape
    by_place = jnp.transpose(
        units_in.reshape(units, parts, tokens_all // parts, columns), (1, 0, 2, 3)
    )
    moved = lax.all_to_all(by_place, axes, 0, 0, tiled=True)
    return jnp.transpose(
        moved.reshape(parts * units, tokens_all // parts, columns), (1, 0, 2)
    )


def gather_in(shard):
    tensor_size = lax.axis_size("tensor")
    whole = lax.all_gather(shard, EVERY, axis=0, tiled=True)
    return jnp.transpose(whole.reshape(tensor_size, D, -1), (1, 0, 2)).reshape(D, -1)


def gather_outs(shard):
    tensor_size = lax.axis_size("tensor")
    rows, columns = shard.shape
    whole = lax.all_gather(shard, EVERY, axis=0, tiled=True)
    return jnp.transpose(
        whole.reshape(tensor_size, D // columns, rows, columns), (0, 2, 1, 3)
    ).reshape(tensor_size * rows, D)


def scatter_in(grad_whole):
    tensor_size = lax.axis_size("tensor")
    stacked = jnp.transpose(
        to_half(grad_whole).reshape(D, tensor_size, -1), (1, 0, 2)
    ).reshape(tensor_size * D, -1)
    return lax.psum_scatter(stacked, EVERY, scatter_dimension=0, tiled=True).astype(jnp.float32)


def scatter_outs(grad_whole, columns):
    tensor_size = lax.axis_size("tensor")
    rows = grad_whole.shape[0] // tensor_size
    stacked = jnp.transpose(
        to_half(grad_whole).reshape(tensor_size, rows, D // columns, columns), (0, 2, 1, 3)
    ).reshape(-1, columns)
    return lax.psum_scatter(stacked, EVERY, scatter_dimension=0, tiled=True).astype(jnp.float32)


def swap_qkv(columns_in, outer, inner):
    rows = columns_in.shape[0]
    return jnp.transpose(
        columns_in.reshape(rows, outer, inner, PAIR), (0, 2, 1, 3)
    ).reshape(rows, outer * inner * PAIR)


def adam_update(master, first_old, second_old, grad_in, factor, fix_first, fix_second):
    clipped = grad_in * factor
    first_new = BETA_FIRST * first_old + (1.0 - BETA_FIRST) * clipped
    second_new = BETA_SECOND * second_old + (1.0 - BETA_SECOND) * clipped * clipped
    step_dir = first_new / fix_first / (jnp.sqrt(second_new / fix_second) + ADAM_EPS)
    master_new = master - LEARN_RATE * (step_dir + WEIGHT_DECAY * master)
    return (master_new, first_new, second_new)


def shards(
    latent,
    noise_draw,
    levels,
    context,
    step_count,
    w_in,
    w_outs,
    w_cond,
    w_time,
    w_patch,
    m_in,
    m_outs,
    m_cond,
    m_time,
    m_patch,
    v_in,
    v_outs,
    v_cond,
    v_time,
    v_patch,
):
    head_cols = D // lax.axis_size("tensor")
    pairs_block = head_cols // PAIR
    pairs_all = D // PAIR
    masters = (w_in, w_outs, w_cond, w_time, w_patch)
    clips, frames_here, patch_rows, width = latent.shape
    groups = clips * frames_here
    plane_index = lax.axis_index(PLANE)
    half_in, half_outs, half_cond, half_time, half_patch = [to_half(m) for m in masters]

    time_whole = lax.all_gather(half_time, PLANE, axis=0, tiled=True)
    levels_all = lax.all_gather(levels, PLANE, axis=0, tiled=False)
    fields = swap_groups(jnp.stack([latent, noise_draw]))
    patch_whole = lax.all_gather(half_patch, PLANE, axis=2, tiled=True)
    cond_whole = lax.all_gather(half_cond, PLANE, axis=0, tiled=True)
    w_qkv = gather_in(swap_qkv(half_in[:, : 3 * head_cols], 3, pairs_block))
    w_out = gather_outs(half_outs[:head_cols])
    w_up = gather_in(half_in[:, 3 * head_cols :])
    w_down = gather_outs(half_outs[head_cols:])
    w_first = time_whole[:TEMB]
    w_second = time_whole[TEMB:]
    w_embed = patch_whole[0]
    w_head = patch_whole[1]

    token_total = (TOKF * jnp.sum(FRAMES - context)).astype(jnp.float32)
    dp_size = lax.axis_size("dp")
    frame_size = lax.axis_size("frame")
    clip_ids = jnp.arange(dp_size * clips, dtype=jnp.int32).reshape(dp_size, 1, clips, 1)
    frame_ids = jnp.arange(FRAMES, dtype=jnp.int32).reshape(1, frame_size, 1, frames_here)
    clean_all = frame_ids < context[clip_ids]
    level_all = jnp.where(
        clean_all, 0, levels_all.reshape(dp_size, frame_size, clips, frames_here)
    ).astype(jnp.float32)
    embed_low = to_half(frequency_table(level_all.reshape(-1)))
    hidden_time = product(embed_low, w_first)
    first_low = to_half(jax.nn.silu(hidden_time))
    cond_vec = product(first_low, w_second)
    cond_low = to_half(jax.nn.silu(cond_vec))
    frame_index = lax.axis_index("frame")
    tensor_index = lax.axis_index("tensor")
    cond_frame = lax.dynamic_index_in_dim(
        cond_low.reshape(dp_size, frame_size, groups, D), frame_index, 1, keepdims=False
    )
    mod_blocks = product(cond_frame.reshape(dp_size * groups, D), cond_whole)
    mod_moved = lax.all_to_all(
        mod_blocks.reshape(dp_size, groups, -1), "tensor", 0, 0, tiled=True
    )
    modulation = jnp.transpose(mod_moved, (1, 0, 2)).reshape(groups, -1)
    pieces = [modulation[:, None, place * D : (place + 1) * D] for place in range(8)]

    def own_part(whole):
        part = lax.dynamic_index_in_dim(whole, tensor_index, 0, keepdims=False)
        return lax.dynamic_index_in_dim(part, frame_index, 0, keepdims=False)

    clean_frames = own_part(clean_all).reshape(groups)
    alpha_coef, sigma_coef = noise_terms(own_part(level_all))
    alpha_field = alpha_coef[:, :, None, None]
    sigma_field = sigma_coef[:, :, None, None]
    clean_field = fields[0].astype(jnp.float32)
    noise_field = fields[1].astype(jnp.float32)
    noisy_field = alpha_field * clean_field + sigma_field * noise_field
    target = alpha_field * noise_field - sigma_field * clean_field
    patch_low = to_half(patchify(noisy_field).reshape(groups, -1, PD))
    goal_rows = patchify(target).reshape(groups, -1, PD)
    rows_local = patch_low.shape[1]
    tokens = groups * rows_local

    residual_in = product(patch_low.reshape(-1, PD), w_embed).reshape(groups, rows_local, D)
    flat_one = to_half(modulate(residual_in, pieces[0], pieces[1])).reshape(tokens, D)
    qkv_rows = to_half(product(flat_one, w_qkv)).reshape(clips, -1, pairs_all, 3 * PAIR)
    spread = spread_heads()
    kept = []
    mixed_tokens = []
    for clip in range(clips):
        qkv_heads = to_heads(qkv_rows[clip])
        if spread:
            key_value, key_place = qkv_heads, 1
        else:
            key_value = lax.all_gather(qkv_heads[..., PAIR:], "frame", axis=1, tiled=True)
            key_place = 0
        exps, mixed_low, mixed, inverse = attend(qkv_heads, key_value, key_place)
        kept.append((exps, qkv_heads, key_value, key_place, mixed, inverse))
        mixed_tokens.append(to_tokens(mixed_low))
    mixed_flat = jnp.stack(mixed_tokens).reshape(tokens, D)
    attn_out = product(mixed_flat, w_out).reshape(groups, rows_local, D)
    residual_mid = residual_in + pieces[2] * attn_out
    flat_two = to_half(modulate(residual_mid, pieces[3], pieces[4])).reshape(tokens, D)
    hidden = product(flat_two, w_up)
    act_low = to_half(jax.nn.gelu(hidden, approximate=True))
    mlp_out = product(act_low, w_down).reshape(groups, rows_local, D)
    residual_out = residual_mid + pieces[5] * mlp_out
    final_low = to_half(modulate(residual_out, pieces[6], pieces[7])).reshape(tokens, D)
    predicted = cols_product(final_low, w_head).reshape(groups, rows_local, PD)
    weight_rows = (1.0 - clean_frames.astype(jnp.float32)).reshape(groups, 1, 1)
    error_rows = predicted - goal_rows
    loss_part = jnp.sum(weight_rows * error_rows * error_rows) / token_total

    grad_pred = to_half(2.0 * weight_rows * error_rows / token_total).reshape(tokens, PD)
    grad_head = rows_product(grad_pred, final_low)
    grad_final = product(grad_pred, w_head).reshape(groups, rows_local, D)
    grad_residual, grad_six, grad_seven = modulate_back(
        residual_out, pieces[6], pieces[7], grad_final
    )
    grad_five = jnp.sum(mlp_out * grad_residual, axis=1, keepdims=True)
    grad_mlp = to_half(pieces[5] * grad_residual).reshape(tokens, D)
    grad_down = rows_product(act_low, grad_mlp)
    final_down = scatter_outs(grad_down, half_outs.shape[1])
    grad_act = cols_product(grad_mlp, w_down)
    unused, gelu_back = jax.vjp(partial(jax.nn.gelu, approximate=True), hidden)
    grad_hidden = to_half(gelu_back(grad_act)[0])
    grad_up = rows_product(flat_two, grad_hidden)
    final_up = scatter_in(grad_up)
    grad_normed = cols_product(grad_hidden, w_up).reshape(groups, rows_local, D)
    grad_branch, grad_three, grad_four = modulate_back(
        residual_mid, pieces[3], pieces[4], grad_normed
    )
    grad_residual = grad_residual + grad_branch
    grad_two = jnp.sum(attn_out * grad_residual, axis=1, keepdims=True)
    grad_attn = to_half(pieces[2] * grad_residual).reshape(tokens, D)
    grad_mixed = to_half(cols_product(grad_attn, w_out)).reshape(clips, -1, pairs_all, PAIR)
    grad_out = rows_product(mixed_flat, grad_attn)
    final_out = scatter_outs(grad_out, half_outs.shape[1])
    grad_qkv_parts = []
    for clip in range(clips):
        exps, qkv_heads, key_value, key_place, mixed, inverse = kept[clip]
        grad_heads = to_heads(grad_mixed[clip])
        grad_query, grad_key, grad_value = attend_back(
            exps, qkv_heads, key_value, key_place, grad_heads, mixed, inverse
        )
        if not spread:
            grad_key, grad_value = [
                lax.psum_scatter(grad, "frame", scatter_dimension=1, tiled=True)
                for grad in (grad_key, grad_value)
            ]
        grad_qkv_parts.append(
            to_tokens(jnp.concatenate([grad_query, grad_key, grad_value], axis=-1))
        )
    grad_qkv = jnp.stack(grad_qkv_parts).reshape(tokens, 3 * D)
    grad_wqkv = rows_product(flat_one, grad_qkv)
    final_qkv = swap_qkv(scatter_in(grad_wqkv), pairs_block, 3)
    grad_normed = cols_product(grad_qkv, w_qkv).reshape(groups, rows_local, D)
    grad_branch, grad_zero, grad_one = modulate_back(residual_in, pieces[0], pieces[1], grad_normed)
    grad_residual = grad_residual + grad_branch
    grad_embed = rows_product(patch_low.reshape(-1, PD), to_half(grad_residual).reshape(-1, D))
    patch_sum = lax.psum(jnp.stack([grad_embed, grad_head]), EVERY)
    patch_cols = half_patch.shape[2]
    final_patch = lax.dynamic_slice_in_dim(patch_sum, plane_index * patch_cols, patch_cols, 2)
    grad_mod = jnp.concatenate(
        [grad_zero, grad_one, grad_two, grad_three, grad_four, grad_five, grad_six, grad_seven],
        axis=-1,
    )[:, 0, :]
    grad_mod_part = lax.psum_scatter(grad_mod, "dp", scatter_dimension=1, tiled=True)
    grad_mod_low = lax.all_gather(swap_groups(to_half(grad_mod_part)), PLANE, axis=0, tiled=True)
    cond_rows = half_cond.shape[0]
    cond_own = lax.dynamic_slice_in_dim(cond_low, plane_index * cond_rows, cond_rows, 1)
    final_cond = rows_product(cond_own, grad_mod_low)
    grad_cond_all = lax.psum(cols_product(grad_mod_low, cond_whole), "tensor")
    unused, silu_cond = jax.vjp(jax.nn.silu, cond_vec)
    grad_cond_low = to_half(silu_cond(grad_cond_all)[0])
    grad_second = rows_product(first_low, grad_cond_low)
    grad_first_act = cols_product(grad_cond_low, w_second)
    unused, silu_first = jax.vjp(jax.nn.silu, hidden_time)
    grad_hidden_time = to_half(silu_first(grad_first_act)[0])
    grad_first = rows_product(embed_low, grad_hidden_time)
    time_rows = half_time.shape[0]
    final_time = lax.dynamic_slice_in_dim(
        jnp.concatenate([grad_first, grad_second], axis=0), plane_index * time_rows, time_rows, 0
    )
    final_grads = (
        jnp.concatenate([final_qkv, final_up], axis=1),
        jnp.concatenate([final_out, final_down], axis=0),
        final_cond,
        final_time,
        final_patch,
    )
    split_square = sum((jnp.sum(grad_in * grad_in) for grad_in in final_grads[:3]))
    shared_square = sum(
        (jnp.sum(grad_in * grad_in) for grad_in in final_grads[3:])
    ) / lax.axis_size("tensor")
    totals = lax.psum((loss_part, split_square + shared_square), ("dp", "frame", "tensor"))
    loss_value = totals[0]
    grad_norm = jnp.sqrt(totals[1])
    factor = jnp.minimum(1.0, MAX_NORM / (grad_norm + 1e-06))
    steps_done = step_count[0].astype(jnp.float32)
    fix_first = 1.0 - BETA_FIRST**steps_done
    fix_second = 1.0 - BETA_SECOND**steps_done
    firsts = (m_in, m_outs, m_cond, m_time, m_patch)
    seconds = (v_in, v_outs, v_cond, v_time, v_patch)
    results = [
        adam_update(
            masters[which],
            firsts[which],
            seconds[which],
            final_grads[which],
            factor,
            fix_first,
            fix_second,
        )
        for which in range(5)
    ]
    return (
        loss_value,
        grad_norm,
        results[0][0],
        results[1][0],
        results[2][0],
        results[3][0],
        results[4][0],
        results[0][1],
        results[1][1],
        results[2][1],
        results[3][1],
        results[4][1],
        results[0][2],
        results[1][2],
        results[2][2],
        results[3][2],
        results[4][2],
        to_half(results[0][0]),
        to_half(results[1][0]),
        to_half(results[2][0]),
        to_half(results[3][0]),
        to_half(results[4][0]),
    )


def solution(mesh):
    placed = (
        P("dp", "frame", "tensor", None),
        P("dp", "frame", "tensor", None),
        P("dp", "frame"),
        P(),
        P(),
        P(("dp", "frame"), "tensor"),
        P("tensor", ("dp", "frame")),
        P(("dp", "frame"), "tensor"),
        P(("dp", "frame"), None),
        P(None, None, ("dp", "frame")),
        P(("dp", "frame"), "tensor"),
        P("tensor", ("dp", "frame")),
        P(("dp", "frame"), "tensor"),
        P(("dp", "frame"), None),
        P(None, None, ("dp", "frame")),
        P(("dp", "frame"), "tensor"),
        P("tensor", ("dp", "frame")),
        P(("dp", "frame"), "tensor"),
        P(("dp", "frame"), None),
        P(None, None, ("dp", "frame")),
    )
    return jax.shard_map(
        shards,
        mesh=mesh,
        in_specs=placed,
        out_specs=(
            P(),
            P(),
            P(("dp", "frame"), "tensor"),
            P("tensor", ("dp", "frame")),
            P(("dp", "frame"), "tensor"),
            P(("dp", "frame"), None),
            P(None, None, ("dp", "frame")),
            P(("dp", "frame"), "tensor"),
            P("tensor", ("dp", "frame")),
            P(("dp", "frame"), "tensor"),
            P(("dp", "frame"), None),
            P(None, None, ("dp", "frame")),
            P(("dp", "frame"), "tensor"),
            P("tensor", ("dp", "frame")),
            P(("dp", "frame"), "tensor"),
            P(("dp", "frame"), None),
            P(None, None, ("dp", "frame")),
            P(("dp", "frame"), "tensor"),
            P("tensor", ("dp", "frame")),
            P(("dp", "frame"), "tensor"),
            P(("dp", "frame"), None),
            P(None, None, ("dp", "frame")),
        ),
        check_vma=False,
    )
```

```python
from functools import partial
import math

import jax
import jax.numpy as jnp
from jax import lax
from jax.experimental import pallas as pl
from jax.experimental.pallas import tpu as pltpu
from jax.sharding import PartitionSpec as P

D = 1024
HD = 64
TEMB = 256
CHANNELS = 4
PATCH = 2
PD = 16
TOKF = 256
FRAMES = 16
NLEV = 1000
PAIR = 2 * HD
PLANE = ("dp", "frame")
EVERY = ("tensor", "dp", "frame")
SCORE_SCALE = HD ** (-0.5) * math.log2(math.e)
TOTAL_LOW = 2.0**-40
TOTAL_HIGH = 2.0**70


EPS_NORM = 1e-06
MAX_NORM = 0.1
LEARN_RATE = 0.08
WEIGHT_DECAY = 0.1
BETA_FIRST = 0.5
BETA_SECOND = 0.5
ADAM_EPS = 1e-08


def to_half(array_in):
    return array_in.astype(jnp.bfloat16)


def product(left_mat, right_mat):
    return jnp.dot(left_mat, right_mat, preferred_element_type=jnp.float32)


def rows_product(left_mat, right_mat):
    return lax.dot_general(
        left_mat, right_mat, (((0,), (0,)), ((), ())), preferred_element_type=jnp.float32
    )


def cols_product(left_mat, right_mat):
    return lax.dot_general(
        left_mat, right_mat, (((1,), (1,)), ((), ())), preferred_element_type=jnp.float32
    )


def frequency_table(level_values):
    half_width = TEMB // 2
    rate_table = jnp.exp(
        -math.log(10000.0) * jnp.arange(half_width, dtype=jnp.float32) / half_width
    )
    angles = level_values[..., None] * rate_table
    return jnp.concatenate([jnp.cos(angles), jnp.sin(angles)], axis=-1)


def noise_terms(level_values):
    angles = level_values * (0.5 * math.pi / NLEV)
    return (jnp.cos(angles), jnp.sin(angles))


def patchify(field_in):
    lead_shape = field_in.shape[:-2]
    rows_here = field_in.shape[-2]
    width_cells = field_in.shape[-1] // CHANNELS
    lead_rank = len(lead_shape)
    blocks_view = field_in.reshape(
        lead_shape + (rows_here // PATCH, PATCH, width_cells // PATCH, PATCH, CHANNELS)
    )
    order_axes = tuple(range(lead_rank)) + (
        lead_rank,
        lead_rank + 2,
        lead_rank + 1,
        lead_rank + 3,
        lead_rank + 4,
    )
    return jnp.transpose(blocks_view, order_axes).reshape(
        lead_shape + (rows_here // PATCH * (width_cells // PATCH), PATCH * PATCH * CHANNELS)
    )


def contract(left_mat, right_mat, left_dim, right_dim):
    return lax.dot_general(
        left_mat,
        right_mat,
        (((left_dim,), (right_dim,)), ((), ())),
        preferred_element_type=jnp.float32,
    )


def head_lanes(head):
    return lax.broadcasted_iota(jnp.int32, (1, PAIR), 1) // HD == head


def attend_kernel(chunk, query_ref, key_ref, value_ref, exps_ref, low_ref, mixed_ref, inverse_ref):
    key_total = key_ref.shape[1]
    block_rows = query_ref.shape[1]
    query_pair = query_ref[0]
    mixed_parts = []
    inverse_parts = []
    for head in range(2):
        lanes = head_lanes(head)
        query_head = jnp.where(lanes, query_pair, jnp.zeros_like(query_pair))

        def scores_of(rows):
            return contract(key_ref[0, rows, :], query_head, 1, 1) * SCORE_SCALE

        def add_chunk(rows, scores, total):
            exps = jnp.exp2(scores).astype(jnp.bfloat16)
            exps_ref[0, head, :, rows] = exps.T
            values = value_ref[0, rows, :]
            values = jnp.where(lanes, values, jnp.ones_like(values))
            return total + contract(values, exps, 0, 0)

        zeros = jnp.zeros((PAIR, block_rows), jnp.float32)
        total = zeros
        for start in range(0, key_total, chunk):
            rows = slice(start, start + chunk)
            total = add_chunk(rows, scores_of(rows), total)
        sum_rows = total[(1 - head) * HD : (1 - head) * HD + 8]
        outside = jnp.max(
            jnp.where((sum_rows > TOTAL_LOW) & (sum_rows < TOTAL_HIGH), 0.0, 1.0)
        )

        def shifted(unused):
            def chunk_rows(step):
                return pl.ds(pl.multiple_of(step * chunk, chunk), chunk)

            def highest(step, top):
                return jnp.maximum(
                    top, jnp.max(scores_of(chunk_rows(step)), axis=0, keepdims=True)
                )

            top = lax.fori_loop(
                0, key_total // chunk, highest, jnp.full((1, block_rows), -jnp.inf, jnp.float32)
            )

            def one_chunk(step, total):
                rows = chunk_rows(step)
                return add_chunk(rows, scores_of(rows) - top, total)

            return lax.fori_loop(0, key_total // chunk, one_chunk, zeros)

        total = lax.cond(outside > 0.0, shifted, lambda kept: kept, total)
        inverse = 1.0 / total[(1 - head) * HD : (2 - head) * HD]
        mixed_parts.append(total[head * HD : (head + 1) * HD] * inverse)
        inverse_parts.append(inverse)
    mixed = jnp.concatenate(mixed_parts, axis=0).T
    mixed_ref[0] = mixed
    low_ref[0] = mixed.astype(jnp.bfloat16)
    inverse_ref[0] = jnp.concatenate(inverse_parts, axis=0).T


def attend(query_in, key_value, key_place):
    units, query_total = query_in.shape[:2]
    key_total = key_value.shape[1]
    block_rows = min(1024, query_total)
    chunk = min(1024, key_total)

    def query_map(unit, step):
        return (unit, step, 0)

    query_spec = pl.BlockSpec((1, block_rows, PAIR), query_map)
    shape_rows = (units, query_total, PAIR)
    products = 4 * units * query_total * key_total * PAIR
    return pl.pallas_call(
        partial(attend_kernel, chunk),
        grid=(units, query_total // block_rows),
        in_specs=[
            query_spec,
            pl.BlockSpec((1, key_total, PAIR), lambda unit, step: (unit, 0, key_place)),
            pl.BlockSpec((1, key_total, PAIR), lambda unit, step: (unit, 0, key_place + 1)),
        ],
        out_specs=[
            pl.BlockSpec((1, 2, block_rows, key_total), lambda unit, step: (unit, 0, step, 0)),
            query_spec,
            query_spec,
            query_spec,
        ],
        out_shape=[
            jax.ShapeDtypeStruct((units, 2, query_total, key_total), jnp.bfloat16),
            jax.ShapeDtypeStruct(shape_rows, jnp.bfloat16),
            jax.ShapeDtypeStruct(shape_rows, jnp.float32),
            jax.ShapeDtypeStruct(shape_rows, jnp.float32),
        ],
        cost_estimate=pl.CostEstimate(
            flops=4 * products,
            bytes_accessed=4 * units * query_total * key_total,
            transcendentals=2 * units * query_total * key_total,
        ),
        compiler_params=pltpu.CompilerParams(vmem_limit_bytes=62 << 20),
    )(query_in, key_value, key_value)


def attend_back_kernel(
    chunk,
    exps_ref,
    query_ref,
    key_ref,
    value_ref,
    grad_ref,
    mixed_ref,
    inverse_ref,
    *grads_and_sums,
):
    *grad_refs, key_sums, value_sums = grads_and_sums
    step = pl.program_id(1)
    head = pl.program_id(2)
    key_total = key_ref.shape[1]
    block_rows = query_ref.shape[1]
    lane = lax.broadcasted_iota(jnp.int32, (1, PAIR), 1)
    lanes = head_lanes(head)
    grad_low = jnp.where(lanes, grad_ref[0].astype(jnp.float32) * inverse_ref[0], 0.0).astype(
        jnp.bfloat16
    )
    row_terms = jnp.sum(grad_low.astype(jnp.float32) * mixed_ref[0], axis=1, keepdims=True)
    term_high = row_terms.astype(jnp.bfloat16).astype(jnp.float32)
    term_rest = row_terms - term_high
    term_lanes = jnp.where(lane == 0, -term_high, jnp.where(lane == 1, -term_rest, 0.0))
    grad_wide = jnp.concatenate([grad_low, term_lanes.astype(jnp.bfloat16)], axis=1)
    query_pair = query_ref[0]
    query_columns = jnp.where(lanes, query_pair, jnp.zeros_like(query_pair)).T
    grad_columns = grad_low.T
    term_ones = jnp.broadcast_to(jnp.where(lane < 2, 1.0, 0.0).astype(jnp.bfloat16), (chunk, PAIR))

    @pl.when((step == 0) & (head == 0))
    def start_sums():
        key_sums[...] = jnp.zeros_like(key_sums)
        value_sums[...] = jnp.zeros_like(value_sums)

    grad_query = jnp.zeros((block_rows, PAIR), jnp.float32)
    for start in range(0, key_total, chunk):
        rows = slice(start, start + chunk)
        values_wide = jnp.concatenate([value_ref[0, rows, :], term_ones], axis=1)
        grad_probs = contract(grad_wide, values_wide, 1, 1).astype(jnp.bfloat16)
        exps = exps_ref[0, 0, :, rows]
        grad_scores = exps * grad_probs
        value_sums[:, rows] += contract(grad_columns, exps, 1, 0)
        key_sums[:, rows] += contract(query_columns, grad_scores, 1, 0)
        keys = key_ref[0, rows, :]
        keys = jnp.where(lanes, keys, jnp.zeros_like(keys))
        grad_query = grad_query + contract(grad_scores, keys, 1, 0)
    grad_query_low = (grad_query * HD ** (-0.5)).astype(jnp.bfloat16)

    fused = len(grad_refs) == 1
    first_row = pl.multiple_of(step * block_rows, block_rows) if fused else 0
    query_place = (0, pl.ds(first_row, block_rows), slice(0, PAIR))

    @pl.when(head == 0)
    def first_head():
        grad_refs[0][query_place] = grad_query_low

    @pl.when(head == 1)
    def second_head():
        grad_refs[0][query_place] = jnp.where(lanes, grad_query_low, grad_refs[0][query_place])

    @pl.when((step == pl.num_programs(1) - 1) & (head == 1))
    def write_sums():
        grad_key = (key_sums[...].T * HD ** (-0.5)).astype(jnp.bfloat16)
        grad_value = value_sums[...].T.astype(jnp.bfloat16)
        if fused:
            grad_refs[0][0, :, PAIR : 2 * PAIR] = grad_key
            grad_refs[0][0, :, 2 * PAIR :] = grad_value
        else:
            grad_refs[1][0] = grad_key
            grad_refs[2][0] = grad_value


def attend_back(exps, query_in, key_value, key_place, grad_mixed, mixed, inverse):
    units, query_total = mixed.shape[:2]
    key_total = key_value.shape[1]
    block_rows = min(1024, query_total)
    chunk = min(1024, key_total)
    query_spec = pl.BlockSpec((1, block_rows, PAIR), lambda unit, step, head: (unit, step, 0))
    whole_spec = pl.BlockSpec((1, key_total, PAIR), lambda unit, step, head: (unit, 0, 0))
    if query_total == key_total:
        out_sizes = [(key_total, 3 * PAIR)]
        out_specs = [
            pl.BlockSpec((1, key_total, 3 * PAIR), lambda unit, step, head: (unit, 0, 0))
        ]
    else:
        out_sizes = [(query_total, PAIR), (key_total, PAIR), (key_total, PAIR)]
        out_specs = [query_spec, whole_spec, whole_spec]
    products = 8 * units * query_total * key_total * PAIR
    return pl.pallas_call(
        partial(attend_back_kernel, chunk),
        grid=(units, query_total // block_rows, 2),
        in_specs=[
            pl.BlockSpec(
                (1, 1, block_rows, key_total), lambda unit, step, head: (unit, head, step, 0)
            ),
            query_spec,
            pl.BlockSpec((1, key_total, PAIR), lambda unit, step, head: (unit, 0, key_place)),
            pl.BlockSpec((1, key_total, PAIR), lambda unit, step, head: (unit, 0, key_place + 1)),
            query_spec,
            query_spec,
            query_spec,
        ],
        out_specs=out_specs,
        out_shape=[
            jax.ShapeDtypeStruct((units, rows, columns), jnp.bfloat16)
            for rows, columns in out_sizes
        ],
        scratch_shapes=[pltpu.VMEM((PAIR, key_total), jnp.float32)] * 2,
        cost_estimate=pl.CostEstimate(
            flops=4 * products,
            bytes_accessed=4 * units * query_total * key_total,
            transcendentals=0,
        ),
        compiler_params=pltpu.CompilerParams(vmem_limit_bytes=62 << 20),
    )(exps, query_in, key_value, key_value, grad_mixed, mixed, inverse)


def normalize(rows_in):
    centre = rows_in - jnp.mean(rows_in, axis=-1, keepdims=True)
    spread = jnp.mean(centre * centre, axis=-1, keepdims=True)
    inverse = lax.rsqrt(spread + EPS_NORM)
    return (centre * inverse, inverse)


def normalize_back(normed, inverse, scale_row, grad_out):
    grad_shift = jnp.sum(grad_out, axis=0, keepdims=True)
    grad_scale = jnp.sum(grad_out * normed, axis=0, keepdims=True)
    grad_normed = grad_out * (1.0 + scale_row)
    grad_rows = inverse * (
        grad_normed
        - jnp.mean(grad_normed, axis=-1, keepdims=True)
        - normed * jnp.mean(grad_normed * normed, axis=-1, keepdims=True)
    )
    return (grad_rows, grad_shift, grad_scale)


def mod_row(mods_ref, place, group):
    return mods_ref[pl.ds(group, 1), place * D : (place + 1) * D]


def group_rows(group, rows_group):
    return pl.ds(pl.multiple_of(group * rows_group, rows_group), rows_group)


def open_kernel(patch_ref, embed_ref, mods_ref, weight_ref, rows_ref, normed_ref, send_ref):
    groups = mods_ref.shape[0]
    rows_group = rows_ref.shape[0] // groups

    @pl.when(pl.program_id(0) == 0)
    def embed_rows():
        def one_group(group, unused):
            rows = group_rows(group, rows_group)
            residual = product(patch_ref[rows, :], embed_ref[...])
            rows_ref[rows, :] = residual
            normed, unused_inverse = normalize(residual)
            normed_ref[rows, :] = to_half(
                normed * (1.0 + mod_row(mods_ref, 1, group)) + mod_row(mods_ref, 0, group)
            )
            return unused

        lax.fori_loop(0, groups, one_group, 0)

    columns = send_ref.shape[2]
    for place in range(send_ref.shape[0]):
        send_ref[place] = to_half(
            product(
                normed_ref[...], weight_ref[0, :, place * columns : (place + 1) * columns]
            )
        )


def open_layer(patch_rows, w_embed, mods, w_qkv):
    tokens = patch_rows.shape[0]
    blocks, unused, columns = w_qkv.shape
    per_block = columns // (3 * PAIR)
    whole = pl.BlockSpec((tokens, D), lambda step: (0, 0))
    return pl.pallas_call(
        open_kernel,
        grid=(blocks,),
        in_specs=[
            pl.BlockSpec(patch_rows.shape, lambda step: (0, 0)),
            pl.BlockSpec(w_embed.shape, lambda step: (0, 0)),
            pl.BlockSpec(mods.shape, lambda step: (0, 0)),
            pl.BlockSpec((1, D, columns), lambda step: (step, 0, 0)),
        ],
        out_specs=[
            whole,
            whole,
            pl.BlockSpec((per_block, tokens, 3 * PAIR), lambda step: (step, 0, 0)),
        ],
        out_shape=[
            jax.ShapeDtypeStruct((tokens, D), jnp.float32),
            jax.ShapeDtypeStruct((tokens, D), jnp.bfloat16),
            jax.ShapeDtypeStruct((blocks * per_block, tokens, 3 * PAIR), jnp.bfloat16),
        ],
        cost_estimate=pl.CostEstimate(
            flops=2 * tokens * D * blocks * columns,
            bytes_accessed=2 * blocks * D * columns + 12 * tokens * D,
            transcendentals=0,
        ),
        compiler_params=pltpu.CompilerParams(vmem_limit_bytes=60 << 20),
    )(patch_rows, w_embed, mods, w_qkv)


GELU_RATE = math.sqrt(2.0 / math.pi)
GELU_CUBE = 0.044715


def middle_kernel(
    head_cols,
    hidden_cols,
    mixed_ref,
    rows_ref,
    mods_ref,
    goal_ref,
    coef_ref,
    head_ref,
    weights_hbm,
    normed_hbm,
    act_hbm,
    grad_mlp_hbm,
    grad_hidden_hbm,
    grad_attn_hbm,
    grad_rows_hbm,
    send_ref,
    grad_mods_ref,
    grad_head_ref,
    loss_ref,
    weights,
    normed_low,
    act_low,
    grad_mlp_low,
    grad_hidden_low,
    grad_attn_low,
    grad_rows,
    attn_sum,
    middle,
    mlp_sum,
    slopes,
    out_sems,
    wide_sems,
    act_sems,
    hidden_sems,
    row_sems,
):
    blocks = weights.shape[0]
    groups = mods_ref.shape[0]
    rows_group = rows_ref.shape[0] // groups
    per_block = head_cols // PAIR
    wide = 2 * hidden_cols
    up_columns = slice(0, hidden_cols)
    down_columns = slice(hidden_cols, wide)
    out_columns = slice(wide, wide + head_cols)

    def fetch_out(block):
        return pltpu.make_async_copy(
            weights_hbm.at[block, :, out_columns],
            weights.at[block, :, out_columns],
            out_sems.at[block],
        )

    def fetch_wide(block):
        return pltpu.make_async_copy(
            weights_hbm.at[block, :, 0:wide], weights.at[block, :, 0:wide], wide_sems.at[block]
        )

    def put_act(block):
        columns = pl.ds(pl.multiple_of(block * hidden_cols, hidden_cols), hidden_cols)
        return pltpu.make_async_copy(
            act_low.at[block], act_hbm.at[:, columns], act_sems.at[block]
        )

    def put_hidden(block):
        columns = pl.ds(pl.multiple_of(block * hidden_cols, hidden_cols), hidden_cols)
        return pltpu.make_async_copy(
            grad_hidden_low.at[block], grad_hidden_hbm.at[:, columns], hidden_sems.at[block]
        )

    put_normed = pltpu.make_async_copy(normed_low, normed_hbm, row_sems.at[0])
    put_grad_mlp = pltpu.make_async_copy(grad_mlp_low, grad_mlp_hbm, row_sems.at[1])
    put_grad_attn = pltpu.make_async_copy(grad_attn_low, grad_attn_hbm, row_sems.at[2])
    put_grad_rows = pltpu.make_async_copy(grad_rows, grad_rows_hbm, row_sems.at[3])

    def each_block(one_block):
        def step(block, unused):
            one_block(block)
            return unused

        lax.fori_loop(0, blocks, step, 0)

    def each_group(one_group):
        def step(group, unused):
            one_group(group, group_rows(group, rows_group))
            return unused

        lax.fori_loop(0, groups, step, 0)

    each_block(lambda block: fetch_out(block).start())
    each_block(lambda block: fetch_wide(block).start())
    attn_sum[...] = jnp.zeros_like(attn_sum)
    mlp_sum[...] = jnp.zeros_like(mlp_sum)

    def attn_out(block):
        fetch_out(block).wait()
        mixed = jnp.concatenate(
            [mixed_ref[block * per_block + place] for place in range(per_block)], axis=1
        )
        attn_sum[...] += contract(mixed, weights[block, :, out_columns], 1, 1)

    each_block(attn_out)

    def to_middle(group, rows):
        residual = rows_ref[rows, :] + mod_row(mods_ref, 2, group) * attn_sum[rows, :]
        middle[rows, :] = residual
        normed, unused_inverse = normalize(residual)
        normed_low[rows, :] = to_half(
            normed * (1.0 + mod_row(mods_ref, 4, group)) + mod_row(mods_ref, 3, group)
        )

    each_group(to_middle)
    put_normed.start()

    def forward_mlp(block):
        fetch_wide(block).wait()
        hidden = product(normed_low[...], weights[block, :, up_columns])
        square = hidden * hidden
        bend = jnp.tanh(GELU_RATE * hidden * (1.0 + GELU_CUBE * square))
        half_open = 0.5 * (1.0 + bend)
        act = to_half(hidden * half_open)
        act_low[block] = act
        slope = half_open + 0.5 * hidden * (1.0 - bend * bend) * (
            GELU_RATE * (1.0 + 3.0 * GELU_CUBE * square)
        )
        slopes[block] = to_half(slope)
        put_act(block).start()
        mlp_sum[...] += contract(act, weights[block, :, down_columns], 1, 1)

    each_block(forward_mlp)
    grad_head_ref[...] = jnp.zeros_like(grad_head_ref)
    loss_ref[...] = jnp.zeros_like(loss_ref)

    def turn(group, rows):
        mlp_out = mlp_sum[rows, :]
        gate = mod_row(mods_ref, 5, group)
        normed, inverse = normalize(middle[rows, :] + gate * mlp_out)
        scale_row = mod_row(mods_ref, 7, group)
        final_low = to_half(normed * (1.0 + scale_row) + mod_row(mods_ref, 6, group))
        error_rows = contract(final_low, head_ref[...], 1, 1) - goal_ref[rows, :]
        weighted = coef_ref[pl.ds(group, 1), :] * error_rows
        loss_ref[pl.ds(0, 1), :] += jnp.sum(weighted * error_rows, axis=0, keepdims=True)
        grad_pred = to_half(2.0 * weighted)
        grad_head_ref[...] += contract(grad_pred, final_low, 0, 0)
        grad_final = product(grad_pred, head_ref[...])
        grad_residual, grad_six, grad_seven = normalize_back(
            normed, inverse, scale_row, grad_final
        )
        grad_mods_ref[4, pl.ds(group, 1), :] = grad_six
        grad_mods_ref[5, pl.ds(group, 1), :] = grad_seven
        grad_mods_ref[3, pl.ds(group, 1), :] = jnp.sum(
            mlp_out * grad_residual, axis=0, keepdims=True
        )
        grad_rows[rows, :] = grad_residual
        grad_mlp_low[rows, :] = to_half(gate * grad_residual)

    each_group(turn)
    put_grad_mlp.start()
    mlp_sum[...] = jnp.zeros_like(mlp_sum)

    def backward_mlp(block):
        grad_act = product(grad_mlp_low[...], weights[block, :, down_columns])
        grad_hidden = to_half(grad_act * slopes[block].astype(jnp.float32))
        grad_hidden_low[block] = grad_hidden
        put_hidden(block).start()
        mlp_sum[...] += contract(grad_hidden, weights[block, :, up_columns], 1, 1)

    each_block(backward_mlp)

    def from_middle(group, rows):
        normed, inverse = normalize(middle[rows, :])
        grad_branch, grad_three, grad_four = normalize_back(
            normed, inverse, mod_row(mods_ref, 4, group), mlp_sum[rows, :]
        )
        grad_residual = grad_rows[rows, :] + grad_branch
        grad_mods_ref[1, pl.ds(group, 1), :] = grad_three
        grad_mods_ref[2, pl.ds(group, 1), :] = grad_four
        grad_mods_ref[0, pl.ds(group, 1), :] = jnp.sum(
            attn_sum[rows, :] * grad_residual, axis=0, keepdims=True
        )
        grad_rows[rows, :] = grad_residual
        grad_attn_low[rows, :] = to_half(mod_row(mods_ref, 2, group) * grad_residual)

    each_group(from_middle)
    put_grad_rows.start()
    put_grad_attn.start()

    def to_send(block):
        grad_mixed = to_half(product(grad_attn_low[...], weights[block, :, out_columns]))
        for place in range(per_block):
            send_ref[block * per_block + place] = grad_mixed[
                :, place * PAIR : (place + 1) * PAIR
            ]

    each_block(to_send)
    put_normed.wait()
    put_grad_mlp.wait()
    put_grad_rows.wait()
    put_grad_attn.wait()
    each_block(lambda block: put_act(block).wait())
    each_block(lambda block: put_hidden(block).wait())


def middle_layer(mixed_pairs, rows_in, mods, goal, coef, w_head, weights, head_cols, hidden_cols):
    blocks = weights.shape[0]
    tokens = rows_in.shape[0]
    groups = mods.shape[0]
    in_vmem = pl.BlockSpec(memory_space=pltpu.VMEM)
    in_hbm = pl.BlockSpec(memory_space=pl.ANY)
    rows_low = pltpu.VMEM((tokens, D), jnp.bfloat16)
    rows_full = pltpu.VMEM((tokens, D), jnp.float32)
    wide_low = pltpu.VMEM((blocks, tokens, hidden_cols), jnp.bfloat16)
    block_sems = pltpu.SemaphoreType.DMA((blocks,))
    return pl.pallas_call(
        partial(middle_kernel, head_cols, hidden_cols),
        in_specs=[in_vmem] * 6 + [in_hbm],
        out_specs=[in_hbm] * 6 + [in_vmem] * 4,
        out_shape=[
            jax.ShapeDtypeStruct((tokens, D), jnp.bfloat16),
            jax.ShapeDtypeStruct((tokens, blocks * hidden_cols), jnp.bfloat16),
            jax.ShapeDtypeStruct((tokens, D), jnp.bfloat16),
            jax.ShapeDtypeStruct((tokens, blocks * hidden_cols), jnp.bfloat16),
            jax.ShapeDtypeStruct((tokens, D), jnp.bfloat16),
            jax.ShapeDtypeStruct((tokens, D), jnp.float32),
            jax.ShapeDtypeStruct(mixed_pairs.shape, jnp.bfloat16),
            jax.ShapeDtypeStruct((6, groups, D), jnp.float32),
            jax.ShapeDtypeStruct(w_head.shape, jnp.float32),
            jax.ShapeDtypeStruct((8, PAIR), jnp.float32),
        ],
        scratch_shapes=[
            pltpu.VMEM(weights.shape, jnp.bfloat16),
            rows_low,
            wide_low,
            rows_low,
            wide_low,
            rows_low,
            rows_full,
            rows_full,
            rows_full,
            rows_full,
            wide_low,
            block_sems,
            block_sems,
            block_sems,
            block_sems,
            pltpu.SemaphoreType.DMA((4,)),
        ],
        cost_estimate=pl.CostEstimate(
            flops=4 * tokens * D * blocks * (2 * hidden_cols + head_cols),
            bytes_accessed=2 * weights.size + 30 * tokens * D,
            transcendentals=tokens * blocks * hidden_cols,
        ),
        compiler_params=pltpu.CompilerParams(vmem_limit_bytes=62 << 20),
    )(mixed_pairs, rows_in, mods, goal, coef, w_head, weights)


def close_kernel(
    blocks,
    grad_ref,
    rows_ref,
    grad_rows_ref,
    mods_ref,
    patch_ref,
    weight_ref,
    grad_mods_ref,
    grad_embed_ref,
    total,
):
    step = pl.program_id(0)
    groups = mods_ref.shape[0]
    rows_group = rows_ref.shape[0] // groups
    columns = grad_ref.shape[2]
    part = jnp.zeros(total.shape, jnp.float32)
    for place in range(grad_ref.shape[0]):
        part = part + contract(
            grad_ref[place], weight_ref[0, :, place * columns : (place + 1) * columns], 1, 1
        )

    @pl.when(step == 0)
    def first():
        total[...] = part

    @pl.when(step > 0)
    def later():
        total[...] += part

    @pl.when(step == blocks - 1)
    def finish():
        grad_embed_ref[...] = jnp.zeros_like(grad_embed_ref)

        def one_group(group, unused):
            rows = group_rows(group, rows_group)
            normed, inverse = normalize(rows_ref[rows, :])
            grad_branch, grad_zero, grad_one = normalize_back(
                normed, inverse, mod_row(mods_ref, 1, group), total[rows, :]
            )
            grad_mods_ref[0, pl.ds(group, 1), :] = grad_zero
            grad_mods_ref[1, pl.ds(group, 1), :] = grad_one
            grad_low = to_half(grad_rows_ref[rows, :] + grad_branch)
            grad_embed_ref[...] += contract(patch_ref[rows, :], grad_low, 0, 0)
            return unused

        lax.fori_loop(0, groups, one_group, 0)


def close_layer(grad_pairs, rows_in, grad_rows, mods, patch_rows, w_qkv):
    tokens = rows_in.shape[0]
    groups = mods.shape[0]
    blocks, unused, columns = w_qkv.shape
    per_block = columns // (3 * PAIR)

    def whole(shape):
        return pl.BlockSpec(shape, lambda step: (0,) * len(shape))

    return pl.pallas_call(
        partial(close_kernel, blocks),
        grid=(blocks,),
        in_specs=[
            pl.BlockSpec((per_block, tokens, 3 * PAIR), lambda step: (step, 0, 0)),
            whole(rows_in.shape),
            whole(grad_rows.shape),
            whole(mods.shape),
            whole(patch_rows.shape),
            pl.BlockSpec((1, D, columns), lambda step: (step, 0, 0)),
        ],
        out_specs=[whole((2, groups, D)), whole((PAIR, D))],
        out_shape=[
            jax.ShapeDtypeStruct((2, groups, D), jnp.float32),
            jax.ShapeDtypeStruct((PAIR, D), jnp.float32),
        ],
        scratch_shapes=[pltpu.VMEM((tokens, D), jnp.float32)],
        cost_estimate=pl.CostEstimate(
            flops=2 * tokens * D * blocks * columns,
            bytes_accessed=2 * blocks * D * columns + 16 * tokens * D,
            transcendentals=0,
        ),
        compiler_params=pltpu.CompilerParams(vmem_limit_bytes=60 << 20),
    )(grad_pairs, rows_in, grad_rows, mods, patch_rows, w_qkv)


def weight_kernel(clips, kinds, *refs):
    out = refs[-1]
    column = 0
    for kind in range(kinds):
        lefts = refs[2 * clips * kind : 2 * clips * kind + clips]
        rights = refs[2 * clips * kind + clips : 2 * clips * (kind + 1)]
        paired = len(rights[0].shape) == 3
        pieces = rights[0].shape[0] if paired else rights[0].shape[1] // 512
        width = rights[0].shape[2] if paired else 512
        for piece in range(pieces):
            total = None
            for left, right in zip(lefts, rights):
                block = right[piece] if paired else right[:, piece * width : (piece + 1) * width]
                part = contract(left[...], block, 0, 0)
                total = part if total is None else total + part
            out[0, :, column : column + width] = to_half(total)
            column += width


def weight_grads(blocks, terms):
    clips = len(terms[0][0])
    operands = []
    specs = []
    columns_all = 0
    flops = 0
    for lefts, rights in terms:
        for left in lefts:
            operands.append(left)
            specs.append(pl.BlockSpec(left.shape, lambda step: (0, 0)))
        for right in rights:
            operands.append(right)
            if right.ndim == 3:
                per_block = right.shape[0] // blocks
                specs.append(
                    pl.BlockSpec((per_block,) + right.shape[1:], lambda step: (step, 0, 0))
                )
                columns = per_block * right.shape[2]
            else:
                columns = right.shape[1] // blocks
                specs.append(pl.BlockSpec((right.shape[0], columns), lambda step: (0, step)))
            flops += 2 * right.size * D
        columns_all += columns
    return pl.pallas_call(
        partial(weight_kernel, clips, len(terms)),
        grid=(blocks,),
        in_specs=specs,
        out_specs=pl.BlockSpec((1, D, columns_all), lambda step: (step, 0, 0)),
        out_shape=jax.ShapeDtypeStruct((blocks, D, columns_all), jnp.bfloat16),
        cost_estimate=pl.CostEstimate(
            flops=flops,
            bytes_accessed=2 * blocks * D * columns_all + 2 * sum(op.size for op in operands),
            transcendentals=0,
        ),
        compiler_params=pltpu.CompilerParams(vmem_limit_bytes=62 << 20),
    )(*operands)


def pack_kernel(head_cols, in_ref, outs_ref, qkv_ref, rest_ref):
    pairs = head_cols // PAIR
    for pair in range(pairs):
        for kind in range(3):
            source = (kind * pairs + pair) * PAIR
            place = (pair * 3 + kind) * PAIR
            qkv_ref[:, place : place + PAIR] = to_half(in_ref[:, source : source + PAIR])
    hidden_cols = in_ref.shape[1] - 3 * head_cols
    rest_ref[:, :hidden_cols] = to_half(in_ref[:, 3 * head_cols :])
    columns = to_half(outs_ref[...].T)
    rest_ref[:, hidden_cols : 2 * hidden_cols] = columns[:, head_cols:]
    rest_ref[:, 2 * hidden_cols :] = columns[:, :head_cols]


def pack_weights(w_in, w_outs, head_cols):
    rows = w_in.shape[0]
    hidden_cols = w_in.shape[1] - 3 * head_cols
    return pl.pallas_call(
        partial(pack_kernel, head_cols),
        out_shape=[
            jax.ShapeDtypeStruct((rows, 3 * head_cols), jnp.bfloat16),
            jax.ShapeDtypeStruct((rows, 2 * hidden_cols + head_cols), jnp.bfloat16),
        ],
    )(w_in, w_outs)


def swap_groups(array_in):
    dp_size = lax.axis_size("dp")
    tensor_size = lax.axis_size("tensor")
    pairs = [
        (row * tensor_size + column, column * dp_size + row)
        for row in range(dp_size)
        for column in range(tensor_size)
    ]
    return lax.ppermute(array_in, ("dp", "tensor"), pairs)


MESH_ID = pl.DeviceIdType.MESH


def places():
    dp_size, frame_size, tensor_size = [
        lax.axis_size(axis) for axis in ("dp", "frame", "tensor")
    ]
    here = [lax.axis_index(axis) for axis in ("dp", "frame", "tensor")]
    return (dp_size, frame_size, tensor_size, *here)


def device(row, frame, column):
    return {"dp": row, "frame": frame, "tensor": column}


def greet_plane():
    dp_size, frame_size, tensor_size, row, frame, column = places()
    plane = dp_size * frame_size
    barrier = pltpu.get_barrier_semaphore()
    for shift in range(1, plane):
        other = lax.rem(row * frame_size + frame + shift, plane)
        pl.semaphore_signal(
            barrier,
            inc=1,
            device_id=device(lax.div(other, frame_size), lax.rem(other, frame_size), column),
            device_id_type=MESH_ID,
        )
    pl.semaphore_wait(barrier, plane - 1)


def greet_all():
    dp_size, frame_size, tensor_size, row, frame, column = places()
    plane = dp_size * frame_size
    everyone = plane * tensor_size
    here = (row * frame_size + frame) * tensor_size + column
    barrier = pltpu.get_barrier_semaphore()

    def signal(shift, unused):
        other = lax.rem(here + shift, everyone)
        place = lax.div(other, tensor_size)
        pl.semaphore_signal(
            barrier,
            inc=1,
            device_id=device(
                lax.div(place, frame_size), lax.rem(place, frame_size), lax.rem(other, tensor_size)
            ),
            device_id_type=MESH_ID,
        )
        return unused

    lax.fori_loop(1, everyone, signal, 0)
    pl.semaphore_wait(barrier, everyone - 1)


def send(source, target, send_sem, receive_sem, device_id):
    return pltpu.make_async_remote_copy(
        src_ref=source,
        dst_ref=target,
        send_sem=send_sem,
        recv_sem=receive_sem,
        device_id=device_id,
        device_id_type=MESH_ID,
    )


def plane_copies(source_of, target_of, send_sems, receive_sems):
    dp_size, frame_size, tensor_size, row, frame, column = places()
    plane = dp_size * frame_size
    here = row * frame_size + frame
    copies = []
    for shift in range(1, plane):
        other = lax.rem(here + shift, plane)
        copies.append(
            send(
                source_of(other),
                target_of(here),
                send_sems.at[shift - 1],
                receive_sems.at[shift - 1],
                device(lax.div(other, frame_size), lax.rem(other, frame_size), column),
            )
        )
    return copies


def axis_copies(axis, source_of, target_of, send_sems, receive_sems):
    size = lax.axis_size(axis)
    here = lax.axis_index(axis)
    row, frame, column = [lax.axis_index(name) for name in ("dp", "frame", "tensor")]
    copies = []
    for shift in range(1, size):
        other = lax.rem(here + shift, size)
        target = device(other, frame, column) if axis == "dp" else device(row, frame, other)
        copies.append(
            send(
                source_of(other),
                target_of(here),
                send_sems.at[shift - 1],
                receive_sems.at[shift - 1],
                target,
            )
        )
    return copies


def run_copies(copies):
    for copy in copies:
        copy.start()
    for copy in copies:
        copy.wait()


def plane_gather_kernel(count, *refs):
    ins = refs[:count]
    outs = refs[count : 2 * count]
    sems = refs[2 * count :]
    greet_plane()
    here = lax.axis_index("dp") * lax.axis_size("frame") + lax.axis_index("frame")
    copies = []
    for place in range(count):
        copies += plane_copies(
            lambda other, place=place: ins[place],
            lambda own, place=place: outs[place].at[own],
            sems[2 * place],
            sems[2 * place + 1],
        )
    for copy in copies:
        copy.start()
    for place in range(count):
        outs[place][here] = ins[place][...]
    for copy in copies:
        copy.wait()


def remote_call(kernel, collective_id, out_shape, scratch_shapes, operands):
    in_vmem = pl.BlockSpec(memory_space=pltpu.VMEM)
    return pl.pallas_call(
        kernel,
        out_shape=out_shape,
        in_specs=[in_vmem] * len(operands),
        out_specs=[in_vmem] * len(out_shape),
        scratch_shapes=scratch_shapes,
        compiler_params=pltpu.CompilerParams(
            collective_id=collective_id, has_side_effects=True, vmem_limit_bytes=48 << 20
        ),
    )(*operands)


def plane_gather(arrays):
    plane = lax.axis_size("dp") * lax.axis_size("frame")
    return remote_call(
        partial(plane_gather_kernel, len(arrays)),
        0,
        [jax.ShapeDtypeStruct((plane,) + array.shape, array.dtype) for array in arrays],
        [pltpu.SemaphoreType.DMA((plane - 1,))] * (2 * len(arrays)),
        arrays,
    )


def mods_kernel(
    parts, out, received, block, plane_send, plane_receive, block_send, block_receive
):
    dp_size, frame_size, tensor_size, row, frame, column = places()
    plane = dp_size * frame_size
    here = row * frame_size + frame
    greet_all()
    copies = plane_copies(
        lambda other: parts.at[other], lambda own: received.at[own], plane_send, plane_receive
    )
    for copy in copies:
        copy.start()
    received[here] = parts[here]
    for copy in copies:
        copy.wait()
    total = received[0]
    for place in range(1, plane):
        total = total + received[place]
    block[...] = total

    def block_copy(target):
        return send(
            block,
            out.at[column],
            block_send.at[target],
            block_receive.at[column],
            device(target, frame, row),
        )

    for target in range(dp_size):
        own = (row == column) & (row == target)

        @pl.when(jnp.logical_not(own))
        def start_copy():
            block_copy(target).start()

        @pl.when(own)
        def keep():
            out[column] = block[...]

    for target in range(dp_size):
        own = (row == column) & (row == target)

        @pl.when(jnp.logical_not(own))
        def sent():
            block_copy(target).wait_send()

    for source in range(tensor_size):
        own = (row == column) & (column == source)

        @pl.when(jnp.logical_not(own))
        def arrived():
            send(
                block,
                out.at[source],
                block_send.at[0],
                block_receive.at[source],
                device(column, frame, source),
            ).wait_recv()


def spread_mods(parts):
    plane, rows, columns = parts.shape
    dma = pltpu.SemaphoreType.DMA
    tensor_size = lax.axis_size("tensor")
    return remote_call(
        mods_kernel,
        1,
        [jax.ShapeDtypeStruct((tensor_size, rows, columns), jnp.float32)],
        [
            pltpu.VMEM(parts.shape, jnp.float32),
            pltpu.VMEM(parts.shape[1:], jnp.float32),
            dma((plane - 1,)),
            dma((plane - 1,)),
            dma((lax.axis_size("dp"),)),
            dma((tensor_size,)),
        ],
        [parts],
    )[0]


def cond_kernel(
    mod_parts,
    patch_parts,
    weight,
    mod_all,
    cond_all,
    patch_out,
    mod_received,
    patch_received,
    mod_block,
    patch_block,
    patch_tensor,
    cond_part,
    cond_tensor,
    dp_send,
    dp_receive,
    patch_send,
    patch_receive,
    spread_send,
    spread_receive,
    patch_tensor_send,
    patch_tensor_receive,
    cond_send,
    cond_receive,
    gather_send,
    gather_receive,
):
    dp_size, frame_size, tensor_size, row, frame, column = places()
    plane = dp_size * frame_size
    here = row * frame_size + frame
    greet_all()
    copies = axis_copies(
        "dp",
        lambda other: mod_parts.at[other],
        lambda own: mod_received.at[own],
        dp_send,
        dp_receive,
    ) + plane_copies(
        lambda other: patch_parts.at[other],
        lambda own: patch_received.at[own],
        patch_send,
        patch_receive,
    )
    for copy in copies:
        copy.start()
    mod_received[row] = mod_parts[row]
    patch_received[here] = patch_parts[here]
    for copy in copies:
        copy.wait()
    total = mod_received[0]
    for place in range(1, dp_size):
        total = total + mod_received[place]
    mod_block[...] = to_half(total)
    total = patch_received[0]
    for place in range(1, plane):
        total = total + patch_received[place]
    patch_block[...] = total
    slot = column * frame_size + frame

    def block_copy(target):
        return send(
            mod_block,
            mod_all.at[slot],
            spread_send.at[target],
            spread_receive.at[slot],
            device(target // frame_size, target % frame_size, row),
        )

    patch_copies = axis_copies(
        "tensor",
        lambda other: patch_block,
        lambda own: patch_tensor.at[own],
        patch_tensor_send,
        patch_tensor_receive,
    )
    for target in range(plane):
        own = (row == column) & (here == target)

        @pl.when(jnp.logical_not(own))
        def start_copy():
            block_copy(target).start()

        @pl.when(own)
        def keep():
            mod_all[slot] = mod_block[...]

    for copy in patch_copies:
        copy.start()
    patch_tensor[column] = patch_block[...]
    for target in range(plane):
        own = (row == column) & (here == target)

        @pl.when(jnp.logical_not(own))
        def sent():
            block_copy(target).wait_send()

    for source in range(plane):
        own = (row == column) & (here == source)

        @pl.when(jnp.logical_not(own))
        def arrived():
            send(
                mod_block,
                mod_all.at[source],
                spread_send.at[0],
                spread_receive.at[source],
                device(column, source % frame_size, source // frame_size),
            ).wait_recv()

    cond_part[...] = contract(mod_all[here], weight[...], 1, 1)
    cond_copies = axis_copies(
        "tensor",
        lambda other: cond_part,
        lambda own: cond_tensor.at[own],
        cond_send,
        cond_receive,
    )
    for copy in cond_copies:
        copy.start()
    cond_tensor[column] = cond_part[...]
    for copy in patch_copies + cond_copies:
        copy.wait()
    total = cond_tensor[0]
    total_patch = patch_tensor[0]
    for place in range(1, tensor_size):
        total = total + cond_tensor[place]
        total_patch = total_patch + patch_tensor[place]
    patch_out[...] = total_patch
    cond_all[here] = total
    run_copies(
        plane_copies(
            lambda other: cond_all.at[here],
            lambda own: cond_all.at[own],
            gather_send,
            gather_receive,
        )
    )


def cond_sums(mod_parts, patch_parts, weight):
    dp_size, rows, columns = mod_parts.shape
    plane = patch_parts.shape[0]
    tensor_size = lax.axis_size("tensor")
    features = weight.shape[0]

    def held(*shape):
        return pltpu.VMEM(shape, jnp.float32)

    def sems(*counts):
        return [pltpu.SemaphoreType.DMA((count,)) for count in counts]

    patch_shape = patch_parts.shape[1:]
    return remote_call(
        cond_kernel,
        2,
        [
            jax.ShapeDtypeStruct((plane, rows, columns), jnp.bfloat16),
            jax.ShapeDtypeStruct((plane, rows, features), jnp.float32),
            jax.ShapeDtypeStruct(patch_shape, jnp.float32),
        ],
        [
            held(*mod_parts.shape),
            held(*patch_parts.shape),
            pltpu.VMEM((rows, columns), jnp.bfloat16),
            held(*patch_shape),
            held(tensor_size, *patch_shape),
            held(rows, features),
            held(tensor_size, rows, features),
        ]
        + sems(dp_size - 1, dp_size - 1, plane - 1, plane - 1, plane, plane)
        + sems(*[tensor_size - 1] * 4, plane - 1, plane - 1),
        [mod_parts, patch_parts, weight],
    )


def total_kernel(tile, out, received, send_sems, receive_sems):
    dp_size, frame_size, tensor_size, row, frame, column = places()
    everyone = dp_size * frame_size * tensor_size
    here = (row * frame_size + frame) * tensor_size + column
    greet_all()

    def copy_to(shift):
        other = lax.rem(here + shift, everyone)
        place = lax.div(other, tensor_size)
        return send(
            tile,
            received.at[here],
            send_sems.at[shift - 1],
            receive_sems.at[shift - 1],
            device(
                lax.div(place, frame_size), lax.rem(place, frame_size), lax.rem(other, tensor_size)
            ),
        )

    def start(shift, unused):
        copy_to(shift).start()
        return unused

    def finish(shift, unused):
        copy_to(shift).wait()
        return unused

    lax.fori_loop(1, everyone, start, 0)
    received[here] = tile[...]
    lax.fori_loop(1, everyone, finish, 0)
    out[...] = jnp.sum(received[...], axis=0)


def total_over_all(first, second):
    lane = jnp.arange(PAIR)[None, :]
    tile = jnp.where(lane == 0, first, jnp.where(lane == 1, second, 0.0))
    tile = jnp.broadcast_to(tile, (8, PAIR)).astype(jnp.float32)
    everyone = lax.axis_size(EVERY)
    sums = remote_call(
        total_kernel,
        3,
        [jax.ShapeDtypeStruct((8, PAIR), jnp.float32)],
        [
            pltpu.VMEM((everyone, 8, PAIR), jnp.float32),
            pltpu.SemaphoreType.DMA((everyone - 1,)),
            pltpu.SemaphoreType.DMA((everyone - 1,)),
        ],
        [tile],
    )[0]
    return (sums[0, 0], sums[0, 1])


def spread_heads():
    return (D // PAIR) % (lax.axis_size("dp") * lax.axis_size("frame")) == 0


def exchange_axes():
    axes = PLANE if spread_heads() else ("dp",)
    return (axes, math.prod(lax.axis_size(axis) for axis in axes))


def to_heads(pairs_in):
    axes, parts = exchange_axes()
    pairs, tokens, columns = pairs_in.shape
    moved = lax.all_to_all(
        pairs_in.reshape(parts, pairs // parts, tokens, columns), axes, 0, 0, tiled=True
    )
    return jnp.swapaxes(moved, 0, 1).reshape(pairs // parts, parts * tokens, columns)


def to_tokens(units_in):
    axes, parts = exchange_axes()
    units, tokens_all, columns = units_in.shape
    by_place = jnp.swapaxes(units_in.reshape(units, parts, tokens_all // parts, columns), 0, 1)
    moved = lax.all_to_all(by_place, axes, 0, 0, tiled=True)
    return moved.reshape(parts * units, tokens_all // parts, columns)


def gather_blocks(shard):
    whole = lax.all_gather(shard, EVERY, axis=0, tiled=True)
    return whole.reshape(lax.axis_size("tensor"), D, -1)


def scatter_blocks(blocks_in):
    flat = blocks_in.reshape(-1, blocks_in.shape[-1])
    return lax.psum_scatter(flat, EVERY, scatter_dimension=0, tiled=True).astype(jnp.float32)


def swap_qkv(columns_in, outer, inner):
    rows = columns_in.shape[0]
    return jnp.transpose(
        columns_in.reshape(rows, outer, inner, PAIR), (0, 2, 1, 3)
    ).reshape(rows, outer * inner * PAIR)


def pad_lanes(rows_in, axis):
    widths = [(0, 0)] * rows_in.ndim
    widths[axis] = (0, PAIR - rows_in.shape[axis])
    return jnp.pad(rows_in, widths)


def after(value, *others):
    return lax.optimization_barrier((value,) + others)[0]


def adam_update(master, first_old, second_old, grad_in, factor, fix_first, fix_second):
    clipped = grad_in * factor
    first_new = BETA_FIRST * first_old + (1.0 - BETA_FIRST) * clipped
    second_new = BETA_SECOND * second_old + (1.0 - BETA_SECOND) * clipped * clipped
    step_dir = first_new / fix_first / (jnp.sqrt(second_new / fix_second) + ADAM_EPS)
    master_new = master - LEARN_RATE * (step_dir + WEIGHT_DECAY * master)
    return (master_new, first_new, second_new)


def shards(
    latent,
    noise_draw,
    levels,
    context,
    step_count,
    w_in,
    w_outs,
    w_cond,
    w_time,
    w_patch,
    m_in,
    m_outs,
    m_cond,
    m_time,
    m_patch,
    v_in,
    v_outs,
    v_cond,
    v_time,
    v_patch,
):
    head_cols = D // lax.axis_size("tensor")
    pairs_block = head_cols // PAIR
    pairs_all = D // PAIR
    masters = (w_in, w_outs, w_cond, w_time, w_patch)
    clips, frames_here, patch_rows, width = latent.shape
    groups = clips * frames_here
    plane_index = lax.axis_index(PLANE)
    half_cond, half_time, half_patch = [to_half(m) for m in masters[2:]]
    hidden_cols = w_in.shape[1] - 3 * head_cols
    shard_qkv, shard_rest = pack_weights(w_in, w_outs, head_cols)

    fields = swap_groups(jnp.stack([latent, noise_draw]))
    w_qkv = gather_blocks(shard_qkv)
    level_rows = jnp.pad(
        levels.astype(jnp.float32), ((0, 8 - clips), (0, PAIR - frames_here))
    )
    time_places, patch_places, level_places = plane_gather([half_time, half_patch, level_rows])
    time_whole = time_places.reshape(-1, D)
    patch_whole = jnp.moveaxis(patch_places, 0, 2).reshape(2, PD, D)
    levels_all = level_places[:, :clips, :frames_here]
    blocks = lax.axis_size("tensor")
    w_first = time_whole[:TEMB]
    w_second = time_whole[TEMB:]
    w_embed = pad_lanes(patch_whole[0], 0)
    w_head = pad_lanes(patch_whole[1], 0)

    token_total = (TOKF * jnp.sum(FRAMES - context)).astype(jnp.float32)
    dp_size = lax.axis_size("dp")
    frame_size = lax.axis_size("frame")
    clip_ids = jnp.arange(dp_size * clips, dtype=jnp.int32).reshape(dp_size, 1, clips, 1)
    frame_ids = jnp.arange(FRAMES, dtype=jnp.int32).reshape(1, frame_size, 1, frames_here)
    clean_all = frame_ids < context[clip_ids]
    level_all = jnp.where(
        clean_all, 0.0, levels_all.reshape(dp_size, frame_size, clips, frames_here)
    )
    embed_low = to_half(frequency_table(level_all.reshape(-1)))
    hidden_time = product(embed_low, w_first)
    first_low = to_half(jax.nn.silu(hidden_time))
    cond_vec = product(first_low, w_second)
    cond_low = to_half(jax.nn.silu(cond_vec))
    frame_index = lax.axis_index("frame")
    tensor_index = lax.axis_index("tensor")
    cond_rows = half_cond.shape[0]
    cond_own = lax.dynamic_slice_in_dim(cond_low, plane_index * cond_rows, cond_rows, 1)
    mod_parts = product(cond_own, half_cond).reshape(dp_size * frame_size, groups, -1)
    modulation = jnp.swapaxes(spread_mods(mod_parts), 0, 1)
    mods = modulation.reshape(clips, frames_here, -1)

    def own_part(whole):
        part = lax.dynamic_index_in_dim(whole, tensor_index, 0, keepdims=False)
        return lax.dynamic_index_in_dim(part, frame_index, 0, keepdims=False)

    clean_frames = own_part(clean_all)
    alpha_coef, sigma_coef = noise_terms(own_part(level_all))
    alpha_field = alpha_coef[:, :, None, None]
    sigma_field = sigma_coef[:, :, None, None]
    clean_field = fields[0].astype(jnp.float32)
    noise_field = fields[1].astype(jnp.float32)
    noisy_field = alpha_field * clean_field + sigma_field * noise_field
    target = alpha_field * noise_field - sigma_field * clean_field
    patch_low = pad_lanes(to_half(patchify(noisy_field).reshape(clips, -1, PD)), 2)
    goal_rows = pad_lanes(patchify(target).reshape(clips, -1, PD), 2)
    coef = (1.0 - clean_frames.astype(jnp.float32)) / token_total
    coef_rows = jnp.broadcast_to(coef[:, :, None], (clips, frames_here, PAIR))


    spread = spread_heads()
    each_clip = range(clips)
    opened = [
        open_layer(patch_low[clip], w_embed, mods[clip], w_qkv) for clip in each_clip
    ]
    rows_in = [parts[0] for parts in opened]
    flat_one = [parts[1] for parts in opened]
    kept = []
    mixed_pairs = []
    for clip in each_clip:
        qkv_send = opened[clip][2]
        if clip > 1:
            qkv_send = after(qkv_send, kept[clip - 2][5])
        qkv_heads = to_heads(qkv_send)
        if clip == 0:
            w_rest = gather_blocks(after(shard_rest, qkv_heads, *rows_in[1:]))
            cond_whole = lax.all_gather(after(half_cond, w_rest), PLANE, axis=0, tiled=True)
        else:
            qkv_heads = after(qkv_heads, kept[clip - 1][5])
        if spread:
            key_value, key_place = qkv_heads, 1
        else:
            key_value = lax.all_gather(qkv_heads[..., PAIR:], "frame", axis=1, tiled=True)
            key_place = 0
        exps, mixed_low, mixed, inverse = attend(qkv_heads, key_value, key_place)
        kept.append((exps, qkv_heads, key_value, key_place, mixed, inverse))
        mixed_pairs.append(to_tokens(mixed_low))
    middles = []
    grad_heads = []
    for clip in each_clip:
        mixed_now = mixed_pairs[clip]
        if clip > 1:
            mixed_now = after(mixed_now, grad_heads[clip - 2])
        middles.append(
            middle_layer(
                mixed_now,
                rows_in[clip],
                mods[clip],
                goal_rows[clip],
                coef_rows[clip],
                w_head,
                w_rest,
                head_cols,
                hidden_cols,
            )
        )
        grad_heads.append(to_heads(middles[clip][6]))
    flat_two, act_low, grad_mlp, grad_hidden, grad_attn, grad_rows = [
        [parts[place] for parts in middles] for place in range(6)
    ]
    flat_two[-1] = after(flat_two[-1], *grad_heads[:-1])
    loss_part = sum(jnp.sum(parts[9]) for parts in middles)
    grad_head = sum(parts[8][:PD] for parts in middles)
    grad_rest = weight_grads(
        blocks,
        [(flat_two, grad_hidden), (grad_mlp, act_low), (grad_attn, mixed_pairs)],
    )
    scattered_rest = scatter_blocks(grad_rest)
    final_up = scattered_rest[:, :hidden_cols]
    final_down = jnp.transpose(scattered_rest[:, hidden_cols : 2 * hidden_cols])
    final_out = jnp.transpose(scattered_rest[:, 2 * hidden_cols :])
    grad_pairs = []
    for clip in each_clip:
        exps, qkv_heads, key_value, key_place, mixed, inverse = kept[clip]
        grad_now = after(grad_heads[clip], grad_rest)
        if clip > 1:
            grad_now = after(grad_now, grad_pairs[clip - 2])
        grads = attend_back(exps, qkv_heads, key_value, key_place, grad_now, mixed, inverse)
        if not spread:
            grads = [grads[0]] + [
                lax.psum_scatter(grad, "frame", scatter_dimension=1, tiled=True)
                for grad in grads[1:]
            ]
        grad_units = grads[0] if len(grads) == 1 else jnp.concatenate(grads, axis=-1)
        grad_pairs.append(to_tokens(grad_units))
    closed = []
    for clip in each_clip:
        if clip == clips - 1:
            grad_pairs[clip] = after(
                grad_pairs[clip], scattered_rest, *[parts[0] for parts in closed]
            )
            grad_wqkv = weight_grads(blocks, [(flat_one, grad_pairs)])
            final_qkv = swap_qkv(scatter_blocks(grad_wqkv), pairs_block, 3)
            grad_pairs[clip] = after(grad_pairs[clip], grad_wqkv)
        closed.append(
            close_layer(
                grad_pairs[clip], rows_in[clip], grad_rows[clip], mods[clip], patch_low[clip], w_qkv
            )
        )
    grad_embed = sum(parts[1][:PD] for parts in closed)
    patch_cols = half_patch.shape[2]
    patch_parts = jnp.swapaxes(
        jnp.concatenate([grad_embed, grad_head], axis=0).reshape(2 * PD, -1, patch_cols), 0, 1
    )
    grad_mod = jnp.stack(
        [jnp.concatenate([closed[clip][0], middles[clip][7]], axis=0) for clip in each_clip]
    )
    mod_parts = jnp.transpose(
        grad_mod.reshape(clips, dp_size, -1, frames_here, D), (1, 0, 3, 2, 4)
    ).reshape(dp_size, groups, -1)
    mod_all, cond_places, patch_block = cond_sums(mod_parts, patch_parts, cond_whole)
    mod_all = mod_all.reshape(-1, mod_all.shape[-1])
    grad_cond_all = cond_places.reshape(-1, D)
    final_patch = patch_block.reshape(2, PD, patch_cols)
    final_cond = rows_product(cond_own, mod_all)
    unused, silu_cond = jax.vjp(jax.nn.silu, cond_vec)
    grad_cond_low = to_half(silu_cond(grad_cond_all)[0])
    grad_second = rows_product(first_low, grad_cond_low)
    grad_first_act = cols_product(grad_cond_low, w_second)
    unused, silu_first = jax.vjp(jax.nn.silu, hidden_time)
    grad_hidden_time = to_half(silu_first(grad_first_act)[0])
    grad_first = rows_product(embed_low, grad_hidden_time)
    time_rows = half_time.shape[0]
    final_time = lax.dynamic_slice_in_dim(
        jnp.concatenate([grad_first, grad_second], axis=0), plane_index * time_rows, time_rows, 0
    )
    final_grads = (
        jnp.concatenate([final_qkv, final_up], axis=1),
        jnp.concatenate([final_out, final_down], axis=0),
        final_cond,
        final_time,
        final_patch,
    )
    split_square = sum((jnp.sum(grad_in * grad_in) for grad_in in final_grads[:3]))
    shared_square = sum(
        (jnp.sum(grad_in * grad_in) for grad_in in final_grads[3:])
    ) / lax.axis_size("tensor")
    totals = total_over_all(loss_part, split_square + shared_square)
    loss_value = totals[0]
    grad_norm = jnp.sqrt(totals[1])
    factor = jnp.minimum(1.0, MAX_NORM / (grad_norm + 1e-06))
    steps_done = step_count[0].astype(jnp.float32)
    fix_first = 1.0 - BETA_FIRST**steps_done
    fix_second = 1.0 - BETA_SECOND**steps_done
    firsts = (m_in, m_outs, m_cond, m_time, m_patch)
    seconds = (v_in, v_outs, v_cond, v_time, v_patch)
    results = [
        adam_update(
            masters[which],
            firsts[which],
            seconds[which],
            final_grads[which],
            factor,
            fix_first,
            fix_second,
        )
        for which in range(5)
    ]
    return (
        loss_value,
        grad_norm,
        results[0][0],
        results[1][0],
        results[2][0],
        results[3][0],
        results[4][0],
        results[0][1],
        results[1][1],
        results[2][1],
        results[3][1],
        results[4][1],
        results[0][2],
        results[1][2],
        results[2][2],
        results[3][2],
        results[4][2],
        to_half(results[0][0]),
        to_half(results[1][0]),
        to_half(results[2][0]),
        to_half(results[3][0]),
        to_half(results[4][0]),
    )


def solution(mesh):
    placed = (
        P("dp", "frame", "tensor", None),
        P("dp", "frame", "tensor", None),
        P("dp", "frame"),
        P(),
        P(),
        P(("dp", "frame"), "tensor"),
        P("tensor", ("dp", "frame")),
        P(("dp", "frame"), "tensor"),
        P(("dp", "frame"), None),
        P(None, None, ("dp", "frame")),
        P(("dp", "frame"), "tensor"),
        P("tensor", ("dp", "frame")),
        P(("dp", "frame"), "tensor"),
        P(("dp", "frame"), None),
        P(None, None, ("dp", "frame")),
        P(("dp", "frame"), "tensor"),
        P("tensor", ("dp", "frame")),
        P(("dp", "frame"), "tensor"),
        P(("dp", "frame"), None),
        P(None, None, ("dp", "frame")),
    )
    return jax.shard_map(
        shards,
        mesh=mesh,
        in_specs=placed,
        out_specs=(
            P(),
            P(),
            P(("dp", "frame"), "tensor"),
            P("tensor", ("dp", "frame")),
            P(("dp", "frame"), "tensor"),
            P(("dp", "frame"), None),
            P(None, None, ("dp", "frame")),
            P(("dp", "frame"), "tensor"),
            P("tensor", ("dp", "frame")),
            P(("dp", "frame"), "tensor"),
            P(("dp", "frame"), None),
            P(None, None, ("dp", "frame")),
            P(("dp", "frame"), "tensor"),
            P("tensor", ("dp", "frame")),
            P(("dp", "frame"), "tensor"),
            P(("dp", "frame"), None),
            P(None, None, ("dp", "frame")),
            P(("dp", "frame"), "tensor"),
            P("tensor", ("dp", "frame")),
            P(("dp", "frame"), "tensor"),
            P(("dp", "frame"), None),
            P(None, None, ("dp", "frame")),
        ),
        check_vma=False,
    )
```

```python
from functools import partial
import math

import jax
import jax.numpy as jnp
from jax import lax
from jax.experimental import pallas as pl
from jax.experimental.pallas import tpu as pltpu
from jax.sharding import PartitionSpec as P

D = 1024
HD = 64
TEMB = 256
CHANNELS = 4
PATCH = 2
PD = 16
TOKF = 256
FRAMES = 16
NLEV = 1000
PAIR = 2 * HD
PLANE = ("dp", "frame")
EVERY = ("tensor", "dp", "frame")
SCORE_SCALE = HD ** (-0.5) * math.log2(math.e)
TOTAL_LOW = 2.0**-40
TOTAL_HIGH = 2.0**70


EPS_NORM = 1e-06
MAX_NORM = 0.1
LEARN_RATE = 0.08
WEIGHT_DECAY = 0.1
BETA_FIRST = 0.5
BETA_SECOND = 0.5
ADAM_EPS = 1e-08


def to_half(array_in):
    return array_in.astype(jnp.bfloat16)


def product(left_mat, right_mat):
    return jnp.dot(left_mat, right_mat, preferred_element_type=jnp.float32)


def rows_product(left_mat, right_mat):
    return lax.dot_general(
        left_mat, right_mat, (((0,), (0,)), ((), ())), preferred_element_type=jnp.float32
    )


def cols_product(left_mat, right_mat):
    return lax.dot_general(
        left_mat, right_mat, (((1,), (1,)), ((), ())), preferred_element_type=jnp.float32
    )


def frequency_table(level_values):
    half_width = TEMB // 2
    rate_table = jnp.exp(
        -math.log(10000.0) * jnp.arange(half_width, dtype=jnp.float32) / half_width
    )
    angles = level_values[..., None] * rate_table
    return jnp.concatenate([jnp.cos(angles), jnp.sin(angles)], axis=-1)


def noise_terms(level_values):
    angles = level_values * (0.5 * math.pi / NLEV)
    return (jnp.cos(angles), jnp.sin(angles))


def patchify(field_in):
    lead_shape = field_in.shape[:-2]
    rows_here = field_in.shape[-2]
    width_cells = field_in.shape[-1] // CHANNELS
    lead_rank = len(lead_shape)
    blocks_view = field_in.reshape(
        lead_shape + (rows_here // PATCH, PATCH, width_cells // PATCH, PATCH, CHANNELS)
    )
    order_axes = tuple(range(lead_rank)) + (
        lead_rank,
        lead_rank + 2,
        lead_rank + 1,
        lead_rank + 3,
        lead_rank + 4,
    )
    return jnp.transpose(blocks_view, order_axes).reshape(
        lead_shape + (rows_here // PATCH * (width_cells // PATCH), PATCH * PATCH * CHANNELS)
    )


def contract(left_mat, right_mat, left_dim, right_dim):
    return lax.dot_general(
        left_mat,
        right_mat,
        (((left_dim,), (right_dim,)), ((), ())),
        preferred_element_type=jnp.float32,
    )


def head_lanes(head):
    return lax.broadcasted_iota(jnp.int32, (1, PAIR), 1) // HD == head


def attend_kernel(chunk, query_ref, key_ref, value_ref, exps_ref, low_ref, mixed_ref, inverse_ref):
    key_total = key_ref.shape[1]
    block_rows = query_ref.shape[1]
    query_pair = query_ref[0]
    mixed_parts = []
    inverse_parts = []
    for head in range(2):
        lanes = head_lanes(head)
        query_head = jnp.where(lanes, query_pair, jnp.zeros_like(query_pair))

        def scores_of(rows):
            return contract(key_ref[0, rows, :], query_head, 1, 1) * SCORE_SCALE

        def add_chunk(rows, scores, total):
            exps = jnp.exp2(scores).astype(jnp.bfloat16)
            exps_ref[0, head, :, rows] = exps.T
            values = value_ref[0, rows, :]
            values = jnp.where(lanes, values, jnp.ones_like(values))
            return total + contract(values, exps, 0, 0)

        zeros = jnp.zeros((PAIR, block_rows), jnp.float32)
        total = zeros
        for start in range(0, key_total, chunk):
            rows = slice(start, start + chunk)
            total = add_chunk(rows, scores_of(rows), total)
        sum_rows = total[(1 - head) * HD : (1 - head) * HD + 8]
        outside = jnp.max(
            jnp.where((sum_rows > TOTAL_LOW) & (sum_rows < TOTAL_HIGH), 0.0, 1.0)
        )

        def shifted(unused):
            def chunk_rows(step):
                return pl.ds(pl.multiple_of(step * chunk, chunk), chunk)

            def highest(step, top):
                return jnp.maximum(
                    top, jnp.max(scores_of(chunk_rows(step)), axis=0, keepdims=True)
                )

            top = lax.fori_loop(
                0, key_total // chunk, highest, jnp.full((1, block_rows), -jnp.inf, jnp.float32)
            )

            def one_chunk(step, total):
                rows = chunk_rows(step)
                return add_chunk(rows, scores_of(rows) - top, total)

            return lax.fori_loop(0, key_total // chunk, one_chunk, zeros)

        total = lax.cond(outside > 0.0, shifted, lambda kept: kept, total)
        inverse = 1.0 / total[(1 - head) * HD : (2 - head) * HD]
        mixed_parts.append(total[head * HD : (head + 1) * HD] * inverse)
        inverse_parts.append(inverse)
    mixed = jnp.concatenate(mixed_parts, axis=0).T
    mixed_ref[0] = mixed
    low_ref[0] = mixed.astype(jnp.bfloat16)
    inverse_ref[0] = jnp.concatenate(inverse_parts, axis=0).T


def attend(query_in, key_value, key_place):
    units, query_total = query_in.shape[:2]
    key_total = key_value.shape[1]
    block_rows = min(1024, query_total)
    chunk = min(1024, key_total)

    def query_map(unit, step):
        return (unit, step, 0)

    query_spec = pl.BlockSpec((1, block_rows, PAIR), query_map)
    shape_rows = (units, query_total, PAIR)
    products = 4 * units * query_total * key_total * PAIR
    return pl.pallas_call(
        partial(attend_kernel, chunk),
        grid=(units, query_total // block_rows),
        in_specs=[
            query_spec,
            pl.BlockSpec((1, key_total, PAIR), lambda unit, step: (unit, 0, key_place)),
            pl.BlockSpec((1, key_total, PAIR), lambda unit, step: (unit, 0, key_place + 1)),
        ],
        out_specs=[
            pl.BlockSpec((1, 2, block_rows, key_total), lambda unit, step: (unit, 0, step, 0)),
            query_spec,
            query_spec,
            query_spec,
        ],
        out_shape=[
            jax.ShapeDtypeStruct((units, 2, query_total, key_total), jnp.bfloat16),
            jax.ShapeDtypeStruct(shape_rows, jnp.bfloat16),
            jax.ShapeDtypeStruct(shape_rows, jnp.float32),
            jax.ShapeDtypeStruct(shape_rows, jnp.float32),
        ],
        cost_estimate=pl.CostEstimate(
            flops=4 * products,
            bytes_accessed=4 * units * query_total * key_total,
            transcendentals=2 * units * query_total * key_total,
        ),
        compiler_params=pltpu.CompilerParams(vmem_limit_bytes=62 << 20),
    )(query_in, key_value, key_value)


def attend_back_kernel(
    chunk,
    exps_ref,
    query_ref,
    key_ref,
    value_ref,
    grad_ref,
    mixed_ref,
    inverse_ref,
    *grads_and_sums,
):
    *grad_refs, key_sums, value_sums = grads_and_sums
    step = pl.program_id(1)
    head = pl.program_id(2)
    key_total = key_ref.shape[1]
    block_rows = query_ref.shape[1]
    lane = lax.broadcasted_iota(jnp.int32, (1, PAIR), 1)
    lanes = head_lanes(head)
    grad_low = jnp.where(lanes, grad_ref[0].astype(jnp.float32) * inverse_ref[0], 0.0).astype(
        jnp.bfloat16
    )
    row_terms = jnp.sum(grad_low.astype(jnp.float32) * mixed_ref[0], axis=1, keepdims=True)
    term_high = row_terms.astype(jnp.bfloat16).astype(jnp.float32)
    term_rest = row_terms - term_high
    term_lanes = jnp.where(lane == 0, -term_high, jnp.where(lane == 1, -term_rest, 0.0))
    grad_wide = jnp.concatenate([grad_low, term_lanes.astype(jnp.bfloat16)], axis=1)
    query_pair = query_ref[0]
    query_columns = jnp.where(lanes, query_pair, jnp.zeros_like(query_pair)).T
    grad_columns = grad_low.T
    term_ones = jnp.broadcast_to(jnp.where(lane < 2, 1.0, 0.0).astype(jnp.bfloat16), (chunk, PAIR))

    @pl.when((step == 0) & (head == 0))
    def start_sums():
        key_sums[...] = jnp.zeros_like(key_sums)
        value_sums[...] = jnp.zeros_like(value_sums)

    grad_query = jnp.zeros((block_rows, PAIR), jnp.float32)
    for start in range(0, key_total, chunk):
        rows = slice(start, start + chunk)
        values_wide = jnp.concatenate([value_ref[0, rows, :], term_ones], axis=1)
        grad_probs = contract(grad_wide, values_wide, 1, 1).astype(jnp.bfloat16)
        exps = exps_ref[0, 0, :, rows]
        grad_scores = exps * grad_probs
        value_sums[:, rows] += contract(grad_columns, exps, 1, 0)
        key_sums[:, rows] += contract(query_columns, grad_scores, 1, 0)
        keys = key_ref[0, rows, :]
        keys = jnp.where(lanes, keys, jnp.zeros_like(keys))
        grad_query = grad_query + contract(grad_scores, keys, 1, 0)
    grad_query_low = (grad_query * HD ** (-0.5)).astype(jnp.bfloat16)

    fused = len(grad_refs) == 1
    first_row = pl.multiple_of(step * block_rows, block_rows) if fused else 0
    query_place = (0, pl.ds(first_row, block_rows), slice(0, PAIR))

    @pl.when(head == 0)
    def first_head():
        grad_refs[0][query_place] = grad_query_low

    @pl.when(head == 1)
    def second_head():
        grad_refs[0][query_place] = jnp.where(lanes, grad_query_low, grad_refs[0][query_place])

    @pl.when((step == pl.num_programs(1) - 1) & (head == 1))
    def write_sums():
        grad_key = (key_sums[...].T * HD ** (-0.5)).astype(jnp.bfloat16)
        grad_value = value_sums[...].T.astype(jnp.bfloat16)
        if fused:
            grad_refs[0][0, :, PAIR : 2 * PAIR] = grad_key
            grad_refs[0][0, :, 2 * PAIR :] = grad_value
        else:
            grad_refs[1][0] = grad_key
            grad_refs[2][0] = grad_value


def attend_back(exps, query_in, key_value, key_place, grad_mixed, mixed, inverse):
    units, query_total = mixed.shape[:2]
    key_total = key_value.shape[1]
    block_rows = min(1024, query_total)
    chunk = min(1024, key_total)
    query_spec = pl.BlockSpec((1, block_rows, PAIR), lambda unit, step, head: (unit, step, 0))
    whole_spec = pl.BlockSpec((1, key_total, PAIR), lambda unit, step, head: (unit, 0, 0))
    if query_total == key_total:
        out_sizes = [(key_total, 3 * PAIR)]
        out_specs = [
            pl.BlockSpec((1, key_total, 3 * PAIR), lambda unit, step, head: (unit, 0, 0))
        ]
    else:
        out_sizes = [(query_total, PAIR), (key_total, PAIR), (key_total, PAIR)]
        out_specs = [query_spec, whole_spec, whole_spec]
    products = 8 * units * query_total * key_total * PAIR
    return pl.pallas_call(
        partial(attend_back_kernel, chunk),
        grid=(units, query_total // block_rows, 2),
        in_specs=[
            pl.BlockSpec(
                (1, 1, block_rows, key_total), lambda unit, step, head: (unit, head, step, 0)
            ),
            query_spec,
            pl.BlockSpec((1, key_total, PAIR), lambda unit, step, head: (unit, 0, key_place)),
            pl.BlockSpec((1, key_total, PAIR), lambda unit, step, head: (unit, 0, key_place + 1)),
            query_spec,
            query_spec,
            query_spec,
        ],
        out_specs=out_specs,
        out_shape=[
            jax.ShapeDtypeStruct((units, rows, columns), jnp.bfloat16)
            for rows, columns in out_sizes
        ],
        scratch_shapes=[pltpu.VMEM((PAIR, key_total), jnp.float32)] * 2,
        cost_estimate=pl.CostEstimate(
            flops=4 * products,
            bytes_accessed=4 * units * query_total * key_total,
            transcendentals=0,
        ),
        compiler_params=pltpu.CompilerParams(vmem_limit_bytes=62 << 20),
    )(exps, query_in, key_value, key_value, grad_mixed, mixed, inverse)


def normalize(rows_in):
    centre = rows_in - jnp.mean(rows_in, axis=-1, keepdims=True)
    spread = jnp.mean(centre * centre, axis=-1, keepdims=True)
    inverse = lax.rsqrt(spread + EPS_NORM)
    return (centre * inverse, inverse)


def normalize_back(normed, inverse, scale_row, grad_out):
    grad_shift = jnp.sum(grad_out, axis=0, keepdims=True)
    grad_scale = jnp.sum(grad_out * normed, axis=0, keepdims=True)
    grad_normed = grad_out * (1.0 + scale_row)
    grad_rows = inverse * (
        grad_normed
        - jnp.mean(grad_normed, axis=-1, keepdims=True)
        - normed * jnp.mean(grad_normed * normed, axis=-1, keepdims=True)
    )
    return (grad_rows, grad_shift, grad_scale)


def mod_row(mods_ref, place, group):
    return mods_ref[pl.ds(group, 1), place * D : (place + 1) * D]


def group_rows(group, rows_group):
    return pl.ds(pl.multiple_of(group * rows_group, rows_group), rows_group)


def open_kernel(patch_ref, embed_ref, mods_ref, weight_ref, rows_ref, normed_ref, send_ref):
    groups = mods_ref.shape[0]
    rows_group = rows_ref.shape[0] // groups

    @pl.when(pl.program_id(0) == 0)
    def embed_rows():
        def one_group(group, unused):
            rows = group_rows(group, rows_group)
            residual = product(patch_ref[rows, :], embed_ref[...])
            rows_ref[rows, :] = residual
            normed, unused_inverse = normalize(residual)
            normed_ref[rows, :] = to_half(
                normed * (1.0 + mod_row(mods_ref, 1, group)) + mod_row(mods_ref, 0, group)
            )
            return unused

        lax.fori_loop(0, groups, one_group, 0)

    columns = send_ref.shape[2]
    for place in range(send_ref.shape[0]):
        send_ref[place] = to_half(
            product(
                normed_ref[...], weight_ref[0, :, place * columns : (place + 1) * columns]
            )
        )


def open_layer(patch_rows, w_embed, mods, w_qkv):
    tokens = patch_rows.shape[0]
    blocks, unused, columns = w_qkv.shape
    per_block = columns // (3 * PAIR)
    whole = pl.BlockSpec((tokens, D), lambda step: (0, 0))
    return pl.pallas_call(
        open_kernel,
        grid=(blocks,),
        in_specs=[
            pl.BlockSpec(patch_rows.shape, lambda step: (0, 0)),
            pl.BlockSpec(w_embed.shape, lambda step: (0, 0)),
            pl.BlockSpec(mods.shape, lambda step: (0, 0)),
            pl.BlockSpec((1, D, columns), lambda step: (step, 0, 0)),
        ],
        out_specs=[
            whole,
            whole,
            pl.BlockSpec((per_block, tokens, 3 * PAIR), lambda step: (step, 0, 0)),
        ],
        out_shape=[
            jax.ShapeDtypeStruct((tokens, D), jnp.float32),
            jax.ShapeDtypeStruct((tokens, D), jnp.bfloat16),
            jax.ShapeDtypeStruct((blocks * per_block, tokens, 3 * PAIR), jnp.bfloat16),
        ],
        cost_estimate=pl.CostEstimate(
            flops=2 * tokens * D * blocks * columns,
            bytes_accessed=2 * blocks * D * columns + 12 * tokens * D,
            transcendentals=0,
        ),
        compiler_params=pltpu.CompilerParams(vmem_limit_bytes=60 << 20),
    )(patch_rows, w_embed, mods, w_qkv)


GELU_RATE = math.sqrt(2.0 / math.pi)
GELU_CUBE = 0.044715


def middle_kernel(
    head_cols,
    hidden_cols,
    mixed_ref,
    rows_ref,
    mods_ref,
    goal_ref,
    coef_ref,
    head_ref,
    weights_hbm,
    normed_hbm,
    act_hbm,
    grad_mlp_hbm,
    grad_hidden_hbm,
    grad_attn_hbm,
    grad_rows_hbm,
    send_ref,
    grad_mods_ref,
    grad_head_ref,
    loss_ref,
    weights,
    normed_low,
    act_low,
    grad_mlp_low,
    grad_hidden_low,
    grad_attn_low,
    grad_rows,
    attn_sum,
    middle,
    mlp_sum,
    slopes,
    out_sems,
    wide_sems,
    act_sems,
    hidden_sems,
    row_sems,
):
    blocks = weights.shape[0]
    groups = mods_ref.shape[0]
    rows_group = rows_ref.shape[0] // groups
    per_block = head_cols // PAIR
    wide = 2 * hidden_cols
    up_columns = slice(0, hidden_cols)
    down_columns = slice(hidden_cols, wide)
    out_columns = slice(wide, wide + head_cols)

    def fetch_out(block):
        return pltpu.make_async_copy(
            weights_hbm.at[block, :, out_columns],
            weights.at[block, :, out_columns],
            out_sems.at[block],
        )

    def fetch_wide(block):
        return pltpu.make_async_copy(
            weights_hbm.at[block, :, 0:wide], weights.at[block, :, 0:wide], wide_sems.at[block]
        )

    def put_act(block):
        columns = pl.ds(pl.multiple_of(block * hidden_cols, hidden_cols), hidden_cols)
        return pltpu.make_async_copy(
            act_low.at[block], act_hbm.at[:, columns], act_sems.at[block]
        )

    def put_hidden(block):
        columns = pl.ds(pl.multiple_of(block * hidden_cols, hidden_cols), hidden_cols)
        return pltpu.make_async_copy(
            grad_hidden_low.at[block], grad_hidden_hbm.at[:, columns], hidden_sems.at[block]
        )

    put_normed = pltpu.make_async_copy(normed_low, normed_hbm, row_sems.at[0])
    put_grad_mlp = pltpu.make_async_copy(grad_mlp_low, grad_mlp_hbm, row_sems.at[1])
    put_grad_attn = pltpu.make_async_copy(grad_attn_low, grad_attn_hbm, row_sems.at[2])
    put_grad_rows = pltpu.make_async_copy(grad_rows, grad_rows_hbm, row_sems.at[3])

    def each_block(one_block):
        def step(block, unused):
            one_block(block)
            return unused

        lax.fori_loop(0, blocks, step, 0)

    def each_group(one_group):
        def step(group, unused):
            one_group(group, group_rows(group, rows_group))
            return unused

        lax.fori_loop(0, groups, step, 0)

    each_block(lambda block: fetch_out(block).start())
    each_block(lambda block: fetch_wide(block).start())
    attn_sum[...] = jnp.zeros_like(attn_sum)
    mlp_sum[...] = jnp.zeros_like(mlp_sum)

    def attn_out(block):
        fetch_out(block).wait()
        mixed = jnp.concatenate(
            [mixed_ref[block * per_block + place] for place in range(per_block)], axis=1
        )
        attn_sum[...] += contract(mixed, weights[block, :, out_columns], 1, 1)

    each_block(attn_out)

    def to_middle(group, rows):
        residual = rows_ref[rows, :] + mod_row(mods_ref, 2, group) * attn_sum[rows, :]
        middle[rows, :] = residual
        normed, unused_inverse = normalize(residual)
        normed_low[rows, :] = to_half(
            normed * (1.0 + mod_row(mods_ref, 4, group)) + mod_row(mods_ref, 3, group)
        )

    each_group(to_middle)
    put_normed.start()

    def forward_mlp(block):
        fetch_wide(block).wait()
        hidden = product(normed_low[...], weights[block, :, up_columns])
        square = hidden * hidden
        bend = jnp.tanh(GELU_RATE * hidden * (1.0 + GELU_CUBE * square))
        half_open = 0.5 * (1.0 + bend)
        act = to_half(hidden * half_open)
        act_low[block] = act
        slope = half_open + 0.5 * hidden * (1.0 - bend * bend) * (
            GELU_RATE * (1.0 + 3.0 * GELU_CUBE * square)
        )
        slopes[block] = to_half(slope)
        put_act(block).start()
        mlp_sum[...] += contract(act, weights[block, :, down_columns], 1, 1)

    each_block(forward_mlp)
    grad_head_ref[...] = jnp.zeros_like(grad_head_ref)
    loss_ref[...] = jnp.zeros_like(loss_ref)

    def turn(group, rows):
        mlp_out = mlp_sum[rows, :]
        gate = mod_row(mods_ref, 5, group)
        normed, inverse = normalize(middle[rows, :] + gate * mlp_out)
        scale_row = mod_row(mods_ref, 7, group)
        final_low = to_half(normed * (1.0 + scale_row) + mod_row(mods_ref, 6, group))
        error_rows = contract(final_low, head_ref[...], 1, 1) - goal_ref[rows, :]
        weighted = coef_ref[pl.ds(group, 1), :] * error_rows
        loss_ref[pl.ds(0, 1), :] += jnp.sum(weighted * error_rows, axis=0, keepdims=True)
        grad_pred = to_half(2.0 * weighted)
        grad_head_ref[...] += contract(grad_pred, final_low, 0, 0)
        grad_final = product(grad_pred, head_ref[...])
        grad_residual, grad_six, grad_seven = normalize_back(
            normed, inverse, scale_row, grad_final
        )
        grad_mods_ref[4, pl.ds(group, 1), :] = grad_six
        grad_mods_ref[5, pl.ds(group, 1), :] = grad_seven
        grad_mods_ref[3, pl.ds(group, 1), :] = jnp.sum(
            mlp_out * grad_residual, axis=0, keepdims=True
        )
        grad_rows[rows, :] = grad_residual
        grad_mlp_low[rows, :] = to_half(gate * grad_residual)

    each_group(turn)
    put_grad_mlp.start()
    mlp_sum[...] = jnp.zeros_like(mlp_sum)

    def backward_mlp(block):
        grad_act = product(grad_mlp_low[...], weights[block, :, down_columns])
        grad_hidden = to_half(grad_act * slopes[block].astype(jnp.float32))
        grad_hidden_low[block] = grad_hidden
        put_hidden(block).start()
        mlp_sum[...] += contract(grad_hidden, weights[block, :, up_columns], 1, 1)

    each_block(backward_mlp)

    def from_middle(group, rows):
        normed, inverse = normalize(middle[rows, :])
        grad_branch, grad_three, grad_four = normalize_back(
            normed, inverse, mod_row(mods_ref, 4, group), mlp_sum[rows, :]
        )
        grad_residual = grad_rows[rows, :] + grad_branch
        grad_mods_ref[1, pl.ds(group, 1), :] = grad_three
        grad_mods_ref[2, pl.ds(group, 1), :] = grad_four
        grad_mods_ref[0, pl.ds(group, 1), :] = jnp.sum(
            attn_sum[rows, :] * grad_residual, axis=0, keepdims=True
        )
        grad_rows[rows, :] = grad_residual
        grad_attn_low[rows, :] = to_half(mod_row(mods_ref, 2, group) * grad_residual)

    each_group(from_middle)
    put_grad_rows.start()
    put_grad_attn.start()

    def to_send(block):
        grad_mixed = to_half(product(grad_attn_low[...], weights[block, :, out_columns]))
        for place in range(per_block):
            send_ref[block * per_block + place] = grad_mixed[
                :, place * PAIR : (place + 1) * PAIR
            ]

    each_block(to_send)
    put_normed.wait()
    put_grad_mlp.wait()
    put_grad_rows.wait()
    put_grad_attn.wait()
    each_block(lambda block: put_act(block).wait())
    each_block(lambda block: put_hidden(block).wait())


def middle_layer(mixed_pairs, rows_in, mods, goal, coef, w_head, weights, head_cols, hidden_cols):
    blocks = weights.shape[0]
    tokens = rows_in.shape[0]
    groups = mods.shape[0]
    in_vmem = pl.BlockSpec(memory_space=pltpu.VMEM)
    in_hbm = pl.BlockSpec(memory_space=pl.ANY)
    rows_low = pltpu.VMEM((tokens, D), jnp.bfloat16)
    rows_full = pltpu.VMEM((tokens, D), jnp.float32)
    wide_low = pltpu.VMEM((blocks, tokens, hidden_cols), jnp.bfloat16)
    block_sems = pltpu.SemaphoreType.DMA((blocks,))
    return pl.pallas_call(
        partial(middle_kernel, head_cols, hidden_cols),
        in_specs=[in_vmem] * 6 + [in_hbm],
        out_specs=[in_hbm] * 6 + [in_vmem] * 4,
        out_shape=[
            jax.ShapeDtypeStruct((tokens, D), jnp.bfloat16),
            jax.ShapeDtypeStruct((tokens, blocks * hidden_cols), jnp.bfloat16),
            jax.ShapeDtypeStruct((tokens, D), jnp.bfloat16),
            jax.ShapeDtypeStruct((tokens, blocks * hidden_cols), jnp.bfloat16),
            jax.ShapeDtypeStruct((tokens, D), jnp.bfloat16),
            jax.ShapeDtypeStruct((tokens, D), jnp.float32),
            jax.ShapeDtypeStruct(mixed_pairs.shape, jnp.bfloat16),
            jax.ShapeDtypeStruct((6, groups, D), jnp.float32),
            jax.ShapeDtypeStruct(w_head.shape, jnp.float32),
            jax.ShapeDtypeStruct((8, PAIR), jnp.float32),
        ],
        scratch_shapes=[
            pltpu.VMEM(weights.shape, jnp.bfloat16),
            rows_low,
            wide_low,
            rows_low,
            wide_low,
            rows_low,
            rows_full,
            rows_full,
            rows_full,
            rows_full,
            wide_low,
            block_sems,
            block_sems,
            block_sems,
            block_sems,
            pltpu.SemaphoreType.DMA((4,)),
        ],
        cost_estimate=pl.CostEstimate(
            flops=4 * tokens * D * blocks * (2 * hidden_cols + head_cols),
            bytes_accessed=2 * weights.size + 30 * tokens * D,
            transcendentals=tokens * blocks * hidden_cols,
        ),
        compiler_params=pltpu.CompilerParams(vmem_limit_bytes=62 << 20),
    )(mixed_pairs, rows_in, mods, goal, coef, w_head, weights)


def close_kernel(
    blocks,
    grad_ref,
    rows_ref,
    grad_rows_ref,
    mods_ref,
    patch_ref,
    weight_ref,
    grad_mods_ref,
    grad_embed_ref,
    total,
):
    step = pl.program_id(0)
    groups = mods_ref.shape[0]
    rows_group = rows_ref.shape[0] // groups
    columns = grad_ref.shape[2]
    part = jnp.zeros(total.shape, jnp.float32)
    for place in range(grad_ref.shape[0]):
        part = part + contract(
            grad_ref[place], weight_ref[0, :, place * columns : (place + 1) * columns], 1, 1
        )

    @pl.when(step == 0)
    def first():
        total[...] = part

    @pl.when(step > 0)
    def later():
        total[...] += part

    @pl.when(step == blocks - 1)
    def finish():
        grad_embed_ref[...] = jnp.zeros_like(grad_embed_ref)

        def one_group(group, unused):
            rows = group_rows(group, rows_group)
            normed, inverse = normalize(rows_ref[rows, :])
            grad_branch, grad_zero, grad_one = normalize_back(
                normed, inverse, mod_row(mods_ref, 1, group), total[rows, :]
            )
            grad_mods_ref[0, pl.ds(group, 1), :] = grad_zero
            grad_mods_ref[1, pl.ds(group, 1), :] = grad_one
            grad_low = to_half(grad_rows_ref[rows, :] + grad_branch)
            grad_embed_ref[...] += contract(patch_ref[rows, :], grad_low, 0, 0)
            return unused

        lax.fori_loop(0, groups, one_group, 0)


def close_layer(grad_pairs, rows_in, grad_rows, mods, patch_rows, w_qkv):
    tokens = rows_in.shape[0]
    groups = mods.shape[0]
    blocks, unused, columns = w_qkv.shape
    per_block = columns // (3 * PAIR)

    def whole(shape):
        return pl.BlockSpec(shape, lambda step: (0,) * len(shape))

    return pl.pallas_call(
        partial(close_kernel, blocks),
        grid=(blocks,),
        in_specs=[
            pl.BlockSpec((per_block, tokens, 3 * PAIR), lambda step: (step, 0, 0)),
            whole(rows_in.shape),
            whole(grad_rows.shape),
            whole(mods.shape),
            whole(patch_rows.shape),
            pl.BlockSpec((1, D, columns), lambda step: (step, 0, 0)),
        ],
        out_specs=[whole((2, groups, D)), whole((PAIR, D))],
        out_shape=[
            jax.ShapeDtypeStruct((2, groups, D), jnp.float32),
            jax.ShapeDtypeStruct((PAIR, D), jnp.float32),
        ],
        scratch_shapes=[pltpu.VMEM((tokens, D), jnp.float32)],
        cost_estimate=pl.CostEstimate(
            flops=2 * tokens * D * blocks * columns,
            bytes_accessed=2 * blocks * D * columns + 16 * tokens * D,
            transcendentals=0,
        ),
        compiler_params=pltpu.CompilerParams(vmem_limit_bytes=60 << 20),
    )(grad_pairs, rows_in, grad_rows, mods, patch_rows, w_qkv)


def weight_kernel(clips, kinds, *refs):
    out = refs[-1]
    column = 0
    for kind in range(kinds):
        lefts = refs[2 * clips * kind : 2 * clips * kind + clips]
        rights = refs[2 * clips * kind + clips : 2 * clips * (kind + 1)]
        paired = len(rights[0].shape) == 3
        pieces = rights[0].shape[0] if paired else rights[0].shape[1] // 512
        width = rights[0].shape[2] if paired else 512
        for piece in range(pieces):
            total = None
            for left, right in zip(lefts, rights):
                block = right[piece] if paired else right[:, piece * width : (piece + 1) * width]
                part = contract(left[...], block, 0, 0)
                total = part if total is None else total + part
            out[0, :, column : column + width] = to_half(total)
            column += width


def weight_grads(blocks, terms):
    clips = len(terms[0][0])
    operands = []
    specs = []
    columns_all = 0
    flops = 0
    for lefts, rights in terms:
        for left in lefts:
            operands.append(left)
            specs.append(pl.BlockSpec(left.shape, lambda step: (0, 0)))
        for right in rights:
            operands.append(right)
            if right.ndim == 3:
                per_block = right.shape[0] // blocks
                specs.append(
                    pl.BlockSpec((per_block,) + right.shape[1:], lambda step: (step, 0, 0))
                )
                columns = per_block * right.shape[2]
            else:
                columns = right.shape[1] // blocks
                specs.append(pl.BlockSpec((right.shape[0], columns), lambda step: (0, step)))
            flops += 2 * right.size * D
        columns_all += columns
    return pl.pallas_call(
        partial(weight_kernel, clips, len(terms)),
        grid=(blocks,),
        in_specs=specs,
        out_specs=pl.BlockSpec((1, D, columns_all), lambda step: (step, 0, 0)),
        out_shape=jax.ShapeDtypeStruct((blocks, D, columns_all), jnp.bfloat16),
        cost_estimate=pl.CostEstimate(
            flops=flops,
            bytes_accessed=2 * blocks * D * columns_all + 2 * sum(op.size for op in operands),
            transcendentals=0,
        ),
        compiler_params=pltpu.CompilerParams(vmem_limit_bytes=62 << 20),
    )(*operands)


def pack_kernel(head_cols, in_ref, outs_ref, qkv_ref, rest_ref):
    pairs = head_cols // PAIR
    for pair in range(pairs):
        for kind in range(3):
            source = (kind * pairs + pair) * PAIR
            place = (pair * 3 + kind) * PAIR
            qkv_ref[:, place : place + PAIR] = to_half(in_ref[:, source : source + PAIR])
    hidden_cols = in_ref.shape[1] - 3 * head_cols
    rest_ref[:, :hidden_cols] = to_half(in_ref[:, 3 * head_cols :])
    columns = to_half(outs_ref[...].T)
    rest_ref[:, hidden_cols : 2 * hidden_cols] = columns[:, head_cols:]
    rest_ref[:, 2 * hidden_cols :] = columns[:, :head_cols]


def pack_weights(w_in, w_outs, head_cols):
    rows = w_in.shape[0]
    hidden_cols = w_in.shape[1] - 3 * head_cols
    return pl.pallas_call(
        partial(pack_kernel, head_cols),
        out_shape=[
            jax.ShapeDtypeStruct((rows, 3 * head_cols), jnp.bfloat16),
            jax.ShapeDtypeStruct((rows, 2 * hidden_cols + head_cols), jnp.bfloat16),
        ],
    )(w_in, w_outs)


def swap_groups(array_in):
    dp_size = lax.axis_size("dp")
    tensor_size = lax.axis_size("tensor")
    pairs = [
        (row * tensor_size + column, column * dp_size + row)
        for row in range(dp_size)
        for column in range(tensor_size)
    ]
    return lax.ppermute(array_in, ("dp", "tensor"), pairs)


MESH_ID = pl.DeviceIdType.MESH


def places():
    dp_size, frame_size, tensor_size = [
        lax.axis_size(axis) for axis in ("dp", "frame", "tensor")
    ]
    here = [lax.axis_index(axis) for axis in ("dp", "frame", "tensor")]
    return (dp_size, frame_size, tensor_size, *here)


def device(row, frame, column):
    return {"dp": row, "frame": frame, "tensor": column}


def greet_plane():
    dp_size, frame_size, tensor_size, row, frame, column = places()
    plane = dp_size * frame_size
    barrier = pltpu.get_barrier_semaphore()
    for shift in range(1, plane):
        other = lax.rem(row * frame_size + frame + shift, plane)
        pl.semaphore_signal(
            barrier,
            inc=1,
            device_id=device(lax.div(other, frame_size), lax.rem(other, frame_size), column),
            device_id_type=MESH_ID,
        )
    pl.semaphore_wait(barrier, plane - 1)


def greet_all():
    dp_size, frame_size, tensor_size, row, frame, column = places()
    plane = dp_size * frame_size
    everyone = plane * tensor_size
    here = (row * frame_size + frame) * tensor_size + column
    barrier = pltpu.get_barrier_semaphore()

    def signal(shift, unused):
        other = lax.rem(here + shift, everyone)
        place = lax.div(other, tensor_size)
        pl.semaphore_signal(
            barrier,
            inc=1,
            device_id=device(
                lax.div(place, frame_size), lax.rem(place, frame_size), lax.rem(other, tensor_size)
            ),
            device_id_type=MESH_ID,
        )
        return unused

    lax.fori_loop(1, everyone, signal, 0)
    pl.semaphore_wait(barrier, everyone - 1)


def send(source, target, send_sem, receive_sem, device_id):
    return pltpu.make_async_remote_copy(
        src_ref=source,
        dst_ref=target,
        send_sem=send_sem,
        recv_sem=receive_sem,
        device_id=device_id,
        device_id_type=MESH_ID,
    )


def plane_copies(source_of, target_of, send_sems, receive_sems):
    dp_size, frame_size, tensor_size, row, frame, column = places()
    plane = dp_size * frame_size
    here = row * frame_size + frame
    copies = []
    for shift in range(1, plane):
        other = lax.rem(here + shift, plane)
        copies.append(
            send(
                source_of(other),
                target_of(here),
                send_sems.at[shift - 1],
                receive_sems.at[shift - 1],
                device(lax.div(other, frame_size), lax.rem(other, frame_size), column),
            )
        )
    return copies


def axis_copies(axis, source_of, target_of, send_sems, receive_sems):
    size = lax.axis_size(axis)
    here = lax.axis_index(axis)
    row, frame, column = [lax.axis_index(name) for name in ("dp", "frame", "tensor")]
    copies = []
    for shift in range(1, size):
        other = lax.rem(here + shift, size)
        target = device(other, frame, column) if axis == "dp" else device(row, frame, other)
        copies.append(
            send(
                source_of(other),
                target_of(here),
                send_sems.at[shift - 1],
                receive_sems.at[shift - 1],
                target,
            )
        )
    return copies


def plane_gather_kernel(count, *refs):
    ins = refs[:count]
    outs = refs[count : 2 * count]
    sems = refs[2 * count :]
    greet_plane()
    here = lax.axis_index("dp") * lax.axis_size("frame") + lax.axis_index("frame")
    copies = []
    for place in range(count):
        copies += plane_copies(
            lambda other, place=place: ins[place],
            lambda own, place=place: outs[place].at[own],
            sems[2 * place],
            sems[2 * place + 1],
        )
    for copy in copies:
        copy.start()
    for place in range(count):
        outs[place][here] = ins[place][...]
    for copy in copies:
        copy.wait()


def remote_call(kernel, collective_id, out_shape, scratch_shapes, operands):
    in_vmem = pl.BlockSpec(memory_space=pltpu.VMEM)
    return pl.pallas_call(
        kernel,
        out_shape=out_shape,
        in_specs=[in_vmem] * len(operands),
        out_specs=[in_vmem] * len(out_shape),
        scratch_shapes=scratch_shapes,
        compiler_params=pltpu.CompilerParams(
            collective_id=collective_id, has_side_effects=True, vmem_limit_bytes=48 << 20
        ),
    )(*operands)


def plane_gather(arrays):
    plane = lax.axis_size("dp") * lax.axis_size("frame")
    return remote_call(
        partial(plane_gather_kernel, len(arrays)),
        0,
        [jax.ShapeDtypeStruct((plane,) + array.shape, array.dtype) for array in arrays],
        [pltpu.SemaphoreType.DMA((plane - 1,))] * (2 * len(arrays)),
        arrays,
    )


def swap_block(block, swapped, send_sem, receive_sem, start):
    row, frame, column = [lax.axis_index(name) for name in ("dp", "frame", "tensor")]
    own = row == column
    copy = send(block, swapped, send_sem, receive_sem, device(column, frame, row))

    @pl.when(jnp.logical_not(own))
    def remote():
        copy.start() if start else copy.wait()

    if start:

        @pl.when(own)
        def keep():
            swapped[...] = block[...]


def mods_kernel(
    parts,
    out,
    received,
    block,
    swapped,
    plane_send,
    plane_receive,
    swap_send,
    swap_receive,
    spread_send,
    spread_receive,
):
    dp_size, frame_size, tensor_size, row, frame, column = places()
    plane = dp_size * frame_size
    here = row * frame_size + frame
    greet_all()
    copies = plane_copies(
        lambda other: parts.at[other], lambda own: received.at[own], plane_send, plane_receive
    )
    for copy in copies:
        copy.start()
    received[here] = parts[here]
    for copy in copies:
        copy.wait()
    total = received[0]
    for place in range(1, plane):
        total = total + received[place]
    block[...] = total
    swap_block(block, swapped, swap_send.at[0], swap_receive.at[0], True)
    swap_block(block, swapped, swap_send.at[0], swap_receive.at[0], False)
    copies = axis_copies(
        "dp", lambda other: swapped, lambda own: out.at[own], spread_send, spread_receive
    )
    for copy in copies:
        copy.start()
    out[row] = swapped[...]
    for copy in copies:
        copy.wait()


def spread_mods(parts):
    plane, rows, columns = parts.shape
    dma = pltpu.SemaphoreType.DMA
    dp_size = lax.axis_size("dp")
    return remote_call(
        mods_kernel,
        1,
        [jax.ShapeDtypeStruct((dp_size, rows, columns), jnp.float32)],
        [
            pltpu.VMEM(parts.shape, jnp.float32),
            pltpu.VMEM(parts.shape[1:], jnp.float32),
            pltpu.VMEM(parts.shape[1:], jnp.float32),
            dma((plane - 1,)),
            dma((plane - 1,)),
            dma((1,)),
            dma((1,)),
            dma((dp_size - 1,)),
            dma((dp_size - 1,)),
        ],
        [parts],
    )[0]


def cond_kernel(
    mod_parts,
    patch_parts,
    weight,
    mod_all,
    cond_all,
    patch_out,
    mod_received,
    patch_received,
    mod_block,
    patch_block,
    patch_tensor,
    cond_part,
    cond_tensor,
    mod_swapped,
    cond_block,
    swap_send,
    swap_receive,
    dp_send,
    dp_receive,
    patch_send,
    patch_receive,
    spread_send,
    spread_receive,
    patch_tensor_send,
    patch_tensor_receive,
    cond_send,
    cond_receive,
    gather_send,
    gather_receive,
):
    dp_size, frame_size, tensor_size, row, frame, column = places()
    plane = dp_size * frame_size
    here = row * frame_size + frame
    greet_all()
    copies = axis_copies(
        "dp",
        lambda other: mod_parts.at[other],
        lambda own: mod_received.at[own],
        dp_send,
        dp_receive,
    ) + plane_copies(
        lambda other: patch_parts.at[other],
        lambda own: patch_received.at[own],
        patch_send,
        patch_receive,
    )
    for copy in copies:
        copy.start()
    mod_received[row] = mod_parts[row]
    patch_received[here] = patch_parts[here]
    for copy in copies:
        copy.wait()
    total = mod_received[0]
    for place in range(1, dp_size):
        total = total + mod_received[place]
    mod_block[...] = to_half(total)
    total = patch_received[0]
    for place in range(1, plane):
        total = total + patch_received[place]
    patch_block[...] = total
    swap_block(mod_block, mod_swapped, swap_send.at[0], swap_receive.at[0], True)
    patch_copies = axis_copies(
        "tensor",
        lambda other: patch_block,
        lambda own: patch_tensor.at[own],
        patch_tensor_send,
        patch_tensor_receive,
    )
    for copy in patch_copies:
        copy.start()
    patch_tensor[column] = patch_block[...]
    swap_block(mod_block, mod_swapped, swap_send.at[0], swap_receive.at[0], False)
    mod_copies = plane_copies(
        lambda other: mod_swapped, lambda own: mod_all.at[own], spread_send, spread_receive
    )
    cond_part[...] = contract(mod_swapped[...], weight[...], 1, 1)
    cond_copies = axis_copies(
        "tensor",
        lambda other: cond_part,
        lambda own: cond_tensor.at[own],
        cond_send,
        cond_receive,
    )
    for copy in cond_copies + mod_copies:
        copy.start()
    mod_all[here] = mod_swapped[...]
    cond_tensor[column] = cond_part[...]
    for copy in patch_copies + cond_copies:
        copy.wait()
    total = cond_tensor[0]
    total_patch = patch_tensor[0]
    for place in range(1, tensor_size):
        total = total + cond_tensor[place]
        total_patch = total_patch + patch_tensor[place]
    patch_out[...] = total_patch
    cond_block[...] = total
    gather_copies = plane_copies(
        lambda other: cond_block, lambda own: cond_all.at[own], gather_send, gather_receive
    )
    for copy in gather_copies:
        copy.start()
    cond_all[here] = total
    for copy in gather_copies + mod_copies:
        copy.wait()


def cond_sums(mod_parts, patch_parts, weight):
    dp_size, rows, columns = mod_parts.shape
    plane = patch_parts.shape[0]
    tensor_size = lax.axis_size("tensor")
    features = weight.shape[0]

    def held(*shape):
        return pltpu.VMEM(shape, jnp.float32)

    def sems(*counts):
        return [pltpu.SemaphoreType.DMA((count,)) for count in counts]

    patch_shape = patch_parts.shape[1:]
    return remote_call(
        cond_kernel,
        2,
        [
            jax.ShapeDtypeStruct((plane, rows, columns), jnp.bfloat16),
            jax.ShapeDtypeStruct((plane, rows, features), jnp.float32),
            jax.ShapeDtypeStruct(patch_shape, jnp.float32),
        ],
        [
            held(*mod_parts.shape),
            held(*patch_parts.shape),
            pltpu.VMEM((rows, columns), jnp.bfloat16),
            held(*patch_shape),
            held(tensor_size, *patch_shape),
            held(rows, features),
            held(tensor_size, rows, features),
            pltpu.VMEM((rows, columns), jnp.bfloat16),
            held(rows, features),
        ]
        + sems(1, 1, dp_size - 1, dp_size - 1, *[plane - 1] * 4)
        + sems(*[tensor_size - 1] * 4, plane - 1, plane - 1),
        [mod_parts, patch_parts, weight],
    )


def total_kernel(tile, out, received, send_sems, receive_sems):
    dp_size, frame_size, tensor_size, row, frame, column = places()
    everyone = dp_size * frame_size * tensor_size
    here = (row * frame_size + frame) * tensor_size + column
    greet_all()

    def copy_to(shift):
        other = lax.rem(here + shift, everyone)
        place = lax.div(other, tensor_size)
        return send(
            tile,
            received.at[here],
            send_sems.at[shift - 1],
            receive_sems.at[shift - 1],
            device(
                lax.div(place, frame_size), lax.rem(place, frame_size), lax.rem(other, tensor_size)
            ),
        )

    def start(shift, unused):
        copy_to(shift).start()
        return unused

    def finish(shift, unused):
        copy_to(shift).wait()
        return unused

    lax.fori_loop(1, everyone, start, 0)
    received[here] = tile[...]
    lax.fori_loop(1, everyone, finish, 0)
    out[...] = jnp.sum(received[...], axis=0)


def total_over_all(first, second):
    lane = jnp.arange(PAIR)[None, :]
    tile = jnp.where(lane == 0, first, jnp.where(lane == 1, second, 0.0))
    tile = jnp.broadcast_to(tile, (8, PAIR)).astype(jnp.float32)
    everyone = lax.axis_size(EVERY)
    sums = remote_call(
        total_kernel,
        3,
        [jax.ShapeDtypeStruct((8, PAIR), jnp.float32)],
        [
            pltpu.VMEM((everyone, 8, PAIR), jnp.float32),
            pltpu.SemaphoreType.DMA((everyone - 1,)),
            pltpu.SemaphoreType.DMA((everyone - 1,)),
        ],
        [tile],
    )[0]
    return (sums[0, 0], sums[0, 1])


def spread_heads():
    return (D // PAIR) % (lax.axis_size("dp") * lax.axis_size("frame")) == 0


def exchange_axes():
    axes = PLANE if spread_heads() else ("dp",)
    return (axes, math.prod(lax.axis_size(axis) for axis in axes))


def to_heads(pairs_in):
    axes, parts = exchange_axes()
    pairs, tokens, columns = pairs_in.shape
    moved = lax.all_to_all(
        pairs_in.reshape(parts, pairs // parts, tokens, columns), axes, 0, 0, tiled=True
    )
    return jnp.swapaxes(moved, 0, 1).reshape(pairs // parts, parts * tokens, columns)


def to_tokens(units_in):
    axes, parts = exchange_axes()
    units, tokens_all, columns = units_in.shape
    by_place = jnp.swapaxes(units_in.reshape(units, parts, tokens_all // parts, columns), 0, 1)
    moved = lax.all_to_all(by_place, axes, 0, 0, tiled=True)
    return moved.reshape(parts * units, tokens_all // parts, columns)


def gather_blocks(shard):
    whole = lax.all_gather(shard, EVERY, axis=0, tiled=True)
    return whole.reshape(lax.axis_size("tensor"), D, -1)


def scatter_blocks(blocks_in):
    flat = blocks_in.reshape(-1, blocks_in.shape[-1])
    return lax.psum_scatter(flat, EVERY, scatter_dimension=0, tiled=True)


def pad_lanes(rows_in, axis):
    widths = [(0, 0)] * rows_in.ndim
    widths[axis] = (0, PAIR - rows_in.shape[axis])
    return jnp.pad(rows_in, widths)


def after(value, *others):
    return lax.optimization_barrier((value,) + others)[0]


def update_part(refs, rows, columns, gradient, rates):
    master_ref, first_ref, second_ref, master_out, first_out, second_out, half_out = refs
    factor, fix_first, fix_second = rates
    place = (Ellipsis, rows, columns)
    master = master_ref[place]
    clipped = gradient * factor
    first_new = BETA_FIRST * first_ref[place] + (1.0 - BETA_FIRST) * clipped
    second_new = BETA_SECOND * second_ref[place] + (1.0 - BETA_SECOND) * clipped * clipped
    step_dir = first_new / fix_first / (jnp.sqrt(second_new / fix_second) + ADAM_EPS)
    master_new = master - LEARN_RATE * (step_dir + WEIGHT_DECAY * master)
    master_out[place] = master_new
    first_out[place] = first_new
    second_out[place] = second_new
    half_out[place] = to_half(master_new)


def update_kernel(head_cols, rates_ref, qkv_ref, rest_ref, cond_ref, time_ref, patch_ref, *refs):
    rates = (rates_ref[0], rates_ref[1], rates_ref[2])
    sets = [refs[which::5] for which in range(5)]
    everything = slice(None)
    pairs = head_cols // PAIR
    for pair in range(pairs):
        for kind in range(3):
            source = (pair * 3 + kind) * PAIR
            place = (kind * pairs + pair) * PAIR
            update_part(
                sets[0],
                everything,
                slice(place, place + PAIR),
                qkv_ref[:, source : source + PAIR].astype(jnp.float32),
                rates,
            )
    qkv_cols = 3 * head_cols
    hidden_cols = sets[0][0].shape[1] - qkv_cols
    for start in range(0, hidden_cols, 256):
        update_part(
            sets[0],
            everything,
            slice(qkv_cols + start, qkv_cols + start + 256),
            rest_ref[:, start : start + 256].astype(jnp.float32),
            rates,
        )
    for start in range(0, hidden_cols + head_cols, 256):
        source = 2 * hidden_cols if start == 0 else hidden_cols + start - head_cols
        gradient = rest_ref[:, source : source + 256].astype(jnp.float32).T
        update_part(sets[1], slice(start, start + 256), everything, gradient, rates)
    for start in range(0, cond_ref.shape[1], 256):
        columns = slice(start, start + 256)
        update_part(sets[2], everything, columns, cond_ref[:, columns], rates)
    for start in range(0, D, 256):
        columns = slice(start, start + 256)
        update_part(sets[3], everything, columns, time_ref[:, columns], rates)
    update_part(sets[4], everything, everything, patch_ref[...], rates)


def update_all(rates, gradients, masters, firsts, seconds, head_cols):
    operands = list(gradients) + list(masters) + list(firsts) + list(seconds)
    shapes = [master.shape for master in masters]
    in_vmem = pl.BlockSpec(memory_space=pltpu.VMEM)
    return pl.pallas_call(
        partial(update_kernel, head_cols),
        in_specs=[pl.BlockSpec(memory_space=pltpu.SMEM)] + [in_vmem] * len(operands),
        out_specs=[in_vmem] * 20,
        out_shape=[jax.ShapeDtypeStruct(shape, jnp.float32) for shape in shapes] * 3
        + [jax.ShapeDtypeStruct(shape, jnp.bfloat16) for shape in shapes],
        compiler_params=pltpu.CompilerParams(vmem_limit_bytes=60 << 20),
    )(rates, *operands)


def shards(
    latent,
    noise_draw,
    levels,
    context,
    step_count,
    w_in,
    w_outs,
    w_cond,
    w_time,
    w_patch,
    m_in,
    m_outs,
    m_cond,
    m_time,
    m_patch,
    v_in,
    v_outs,
    v_cond,
    v_time,
    v_patch,
):
    head_cols = D // lax.axis_size("tensor")
    pairs_block = head_cols // PAIR
    pairs_all = D // PAIR
    masters = (w_in, w_outs, w_cond, w_time, w_patch)
    clips, frames_here, patch_rows, width = latent.shape
    groups = clips * frames_here
    plane_index = lax.axis_index(PLANE)
    half_cond, half_time, half_patch = [to_half(m) for m in masters[2:]]
    hidden_cols = w_in.shape[1] - 3 * head_cols
    shard_qkv, shard_rest = pack_weights(w_in, w_outs, head_cols)

    w_qkv = gather_blocks(shard_qkv)
    level_rows = jnp.pad(
        levels.astype(jnp.float32), ((0, 8 - clips), (0, PAIR - frames_here))
    )
    time_places, patch_places, level_places = plane_gather([half_time, half_patch, level_rows])
    time_whole = time_places.reshape(-1, D)
    patch_whole = jnp.moveaxis(patch_places, 0, 2).reshape(2, PD, D)
    fields = swap_groups(jnp.stack([latent, noise_draw]))
    levels_all = level_places[:, :clips, :frames_here]
    blocks = lax.axis_size("tensor")
    w_first = time_whole[:TEMB]
    w_second = time_whole[TEMB:]
    w_embed = pad_lanes(patch_whole[0], 0)
    w_head = pad_lanes(patch_whole[1], 0)

    token_total = (TOKF * jnp.sum(FRAMES - context)).astype(jnp.float32)
    dp_size = lax.axis_size("dp")
    frame_size = lax.axis_size("frame")
    clip_ids = jnp.arange(dp_size * clips, dtype=jnp.int32).reshape(dp_size, 1, clips, 1)
    frame_ids = jnp.arange(FRAMES, dtype=jnp.int32).reshape(1, frame_size, 1, frames_here)
    clean_all = frame_ids < context[clip_ids]
    level_all = jnp.where(
        clean_all, 0.0, levels_all.reshape(dp_size, frame_size, clips, frames_here)
    )
    embed_low = to_half(frequency_table(level_all.reshape(-1)))
    hidden_time = product(embed_low, w_first)
    first_low = to_half(jax.nn.silu(hidden_time))
    cond_vec = product(first_low, w_second)
    cond_low = to_half(jax.nn.silu(cond_vec))
    frame_index = lax.axis_index("frame")
    tensor_index = lax.axis_index("tensor")
    cond_rows = half_cond.shape[0]
    cond_own = lax.dynamic_slice_in_dim(cond_low, plane_index * cond_rows, cond_rows, 1)
    mod_parts = product(cond_own, half_cond).reshape(dp_size * frame_size, groups, -1)
    def own_part(whole):
        part = lax.dynamic_index_in_dim(whole, tensor_index, 0, keepdims=False)
        return lax.dynamic_index_in_dim(part, frame_index, 0, keepdims=False)

    clean_frames = own_part(clean_all)
    alpha_coef, sigma_coef = noise_terms(own_part(level_all))
    alpha_field = alpha_coef[:, :, None, None]
    sigma_field = sigma_coef[:, :, None, None]
    clean_field = fields[0].astype(jnp.float32)
    noise_field = fields[1].astype(jnp.float32)
    noisy_field = alpha_field * clean_field + sigma_field * noise_field
    target = alpha_field * noise_field - sigma_field * clean_field
    patch_low = pad_lanes(to_half(patchify(noisy_field).reshape(clips, -1, PD)), 2)
    goal_rows = pad_lanes(patchify(target).reshape(clips, -1, PD), 2)
    coef = (1.0 - clean_frames.astype(jnp.float32)) / token_total
    coef_rows = jnp.broadcast_to(coef[:, :, None], (clips, frames_here, PAIR))


    mod_parts, patch_low, goal_rows, coef_rows = lax.optimization_barrier(
        (mod_parts, patch_low, goal_rows, coef_rows)
    )
    modulation = jnp.swapaxes(spread_mods(mod_parts), 0, 1)
    mods = modulation.reshape(clips, frames_here, -1)

    spread = spread_heads()
    each_clip = range(clips)
    opened = [
        open_layer(patch_low[clip], w_embed, mods[clip], w_qkv) for clip in each_clip
    ]
    rows_in = [parts[0] for parts in opened]
    flat_one = [parts[1] for parts in opened]
    kept = []
    mixed_pairs = []
    mixed_lows = []
    for clip in each_clip:
        qkv_send = opened[clip][2]
        if clip > 1:
            qkv_send = after(qkv_send, mixed_lows[clip - 2])
        qkv_heads = to_heads(qkv_send)
        if clip == 0:
            w_rest = gather_blocks(after(shard_rest, qkv_heads, *rows_in[1:]))
            cond_whole = lax.all_gather(after(half_cond, w_rest), PLANE, axis=0, tiled=True)
        else:
            qkv_heads = after(qkv_heads, mixed_lows[clip - 1])
        if spread:
            key_value, key_place = qkv_heads, 1
        else:
            key_value = lax.all_gather(qkv_heads[..., PAIR:], "frame", axis=1, tiled=True)
            key_place = 0
        exps, mixed_low, mixed, inverse = attend(qkv_heads, key_value, key_place)
        kept.append((exps, qkv_heads, key_value, key_place, mixed, inverse))
        mixed_lows.append(mixed_low)
    middles = []
    grad_heads = []
    for clip in each_clip:
        gates = mixed_lows[clip + 1 : clip + 2]
        if not gates and clip > 1:
            gates = [middles[clip - 2][5]]
        mixed_pairs.append(to_tokens(after(mixed_lows[clip], *gates)))
        middles.append(
            middle_layer(
                mixed_pairs[clip],
                rows_in[clip],
                mods[clip],
                goal_rows[clip],
                coef_rows[clip],
                w_head,
                w_rest,
                head_cols,
                hidden_cols,
            )
        )
    flat_two, act_low, grad_mlp, grad_hidden, grad_attn, grad_rows = [
        [parts[place] for parts in middles] for place in range(6)
    ]
    loss_part = sum(jnp.sum(parts[9]) for parts in middles)
    grad_head = sum(parts[8][:PD] for parts in middles)
    grad_heads = [to_heads(after(middles[0][6], middles[1 % clips][5]))]
    flat_two[-1] = after(flat_two[-1], *grad_heads)
    grad_rest = weight_grads(
        blocks,
        [(flat_two, grad_hidden), (grad_mlp, act_low), (grad_attn, mixed_pairs)],
    )
    scattered_rest = scatter_blocks(after(grad_rest, cond_whole))
    if clips > 1:
        sends = after(jnp.concatenate([parts[6] for parts in middles[1:]], axis=1), grad_rest)
        together = to_heads(sends).reshape(
            kept[0][5].shape[0], -1, clips - 1, sends.shape[1] // (clips - 1), PAIR
        )
        grad_heads += [
            together[:, :, clip].reshape(together.shape[0], -1, PAIR) for clip in range(clips - 1)
        ]
    grad_pairs = []
    for clip in each_clip:
        exps, qkv_heads, key_value, key_place, mixed, inverse = kept[clip]
        grad_now = after(grad_heads[clip], grad_rest)
        if clip > 1:
            grad_now = after(grad_now, grad_pairs[clip - 2])
        grads = attend_back(exps, qkv_heads, key_value, key_place, grad_now, mixed, inverse)
        if not spread:
            grads = [grads[0]] + [
                lax.psum_scatter(grad, "frame", scatter_dimension=1, tiled=True)
                for grad in grads[1:]
            ]
        grad_units = grads[0] if len(grads) == 1 else jnp.concatenate(grads, axis=-1)
        grad_pairs.append(to_tokens(grad_units))
    closed = []
    for clip in each_clip:
        if clip == clips - 1:
            grad_pairs[clip] = after(
                grad_pairs[clip], scattered_rest, *[parts[0] for parts in closed]
            )
            grad_wqkv = weight_grads(blocks, [(flat_one, grad_pairs)])
            scattered_qkv = scatter_blocks(grad_wqkv)
            grad_pairs[clip] = after(grad_pairs[clip], grad_wqkv)
        closed.append(
            close_layer(
                grad_pairs[clip], rows_in[clip], grad_rows[clip], mods[clip], patch_low[clip], w_qkv
            )
        )
    grad_embed = sum(parts[1][:PD] for parts in closed)
    patch_cols = half_patch.shape[2]
    patch_parts = jnp.swapaxes(
        jnp.concatenate([grad_embed, grad_head], axis=0).reshape(2 * PD, -1, patch_cols), 0, 1
    )
    grad_mod = jnp.stack(
        [jnp.concatenate([closed[clip][0], middles[clip][7]], axis=0) for clip in each_clip]
    )
    mod_parts = jnp.transpose(
        grad_mod.reshape(clips, dp_size, -1, frames_here, D), (1, 0, 3, 2, 4)
    ).reshape(dp_size, groups, -1)
    mod_all, cond_places, patch_block = cond_sums(mod_parts, patch_parts, cond_whole)
    mod_all = mod_all.reshape(-1, mod_all.shape[-1])
    grad_cond_all = cond_places.reshape(-1, D)
    final_patch = patch_block.reshape(2, PD, patch_cols)
    final_cond = rows_product(cond_own, mod_all)
    unused, silu_cond = jax.vjp(jax.nn.silu, cond_vec)
    grad_cond_low = to_half(silu_cond(grad_cond_all)[0])
    grad_second = rows_product(first_low, grad_cond_low)
    grad_first_act = cols_product(grad_cond_low, w_second)
    unused, silu_first = jax.vjp(jax.nn.silu, hidden_time)
    grad_hidden_time = to_half(silu_first(grad_first_act)[0])
    grad_first = rows_product(embed_low, grad_hidden_time)
    time_rows = half_time.shape[0]
    final_time = lax.dynamic_slice_in_dim(
        jnp.concatenate([grad_first, grad_second], axis=0), plane_index * time_rows, time_rows, 0
    )
    def square_sum(gradient):
        wide = gradient.astype(jnp.float32)
        return jnp.sum(wide * wide)

    split_square = sum(square_sum(part) for part in (scattered_qkv, scattered_rest, final_cond))
    shared_square = (square_sum(final_time) + square_sum(final_patch)) / blocks
    totals = total_over_all(loss_part, split_square + shared_square)
    loss_value = totals[0]
    grad_norm = jnp.sqrt(totals[1])
    factor = jnp.minimum(1.0, MAX_NORM / (grad_norm + 1e-06))
    steps_done = step_count[0].astype(jnp.float32)
    fix_first = 1.0 - BETA_FIRST**steps_done
    fix_second = 1.0 - BETA_SECOND**steps_done
    results = update_all(
        jnp.stack([factor, fix_first, fix_second]),
        (scattered_qkv, scattered_rest, final_cond, final_time, final_patch),
        masters,
        (m_in, m_outs, m_cond, m_time, m_patch),
        (v_in, v_outs, v_cond, v_time, v_patch),
        head_cols,
    )
    return (loss_value, grad_norm, *results)


def solution(mesh):
    placed = (
        P("dp", "frame", "tensor", None),
        P("dp", "frame", "tensor", None),
        P("dp", "frame"),
        P(),
        P(),
        P(("dp", "frame"), "tensor"),
        P("tensor", ("dp", "frame")),
        P(("dp", "frame"), "tensor"),
        P(("dp", "frame"), None),
        P(None, None, ("dp", "frame")),
        P(("dp", "frame"), "tensor"),
        P("tensor", ("dp", "frame")),
        P(("dp", "frame"), "tensor"),
        P(("dp", "frame"), None),
        P(None, None, ("dp", "frame")),
        P(("dp", "frame"), "tensor"),
        P("tensor", ("dp", "frame")),
        P(("dp", "frame"), "tensor"),
        P(("dp", "frame"), None),
        P(None, None, ("dp", "frame")),
    )
    return jax.shard_map(
        shards,
        mesh=mesh,
        in_specs=placed,
        out_specs=(
            P(),
            P(),
            P(("dp", "frame"), "tensor"),
            P("tensor", ("dp", "frame")),
            P(("dp", "frame"), "tensor"),
            P(("dp", "frame"), None),
            P(None, None, ("dp", "frame")),
            P(("dp", "frame"), "tensor"),
            P("tensor", ("dp", "frame")),
            P(("dp", "frame"), "tensor"),
            P(("dp", "frame"), None),
            P(None, None, ("dp", "frame")),
            P(("dp", "frame"), "tensor"),
            P("tensor", ("dp", "frame")),
            P(("dp", "frame"), "tensor"),
            P(("dp", "frame"), None),
            P(None, None, ("dp", "frame")),
            P(("dp", "frame"), "tensor"),
            P("tensor", ("dp", "frame")),
            P(("dp", "frame"), "tensor"),
            P(("dp", "frame"), None),
            P(None, None, ("dp", "frame")),
        ),
        check_vma=False,
    )
```

```python
from functools import partial
import math

import jax
import jax.numpy as jnp
from jax import lax
from jax.experimental import pallas as pl
from jax.experimental.pallas import tpu as pltpu
from jax.sharding import PartitionSpec as P

D = 1024
HD = 64
TEMB = 256
CHANNELS = 4
PATCH = 2
PD = 16
TOKF = 256
FRAMES = 16
NLEV = 1000
PAIR = 2 * HD
PLANE = ("dp", "frame")
EVERY = ("tensor", "dp", "frame")
SCORE_SCALE = HD ** (-0.5) * math.log2(math.e)
TOTAL_LOW = 2.0**-40
TOTAL_HIGH = 2.0**70


EPS_NORM = 1e-06
MAX_NORM = 0.1
LEARN_RATE = 0.08
WEIGHT_DECAY = 0.1
BETA_FIRST = 0.5
BETA_SECOND = 0.5
ADAM_EPS = 1e-08


def to_half(array_in):
    return array_in.astype(jnp.bfloat16)


def product(left_mat, right_mat):
    return jnp.dot(left_mat, right_mat, preferred_element_type=jnp.float32)


def rows_product(left_mat, right_mat):
    return lax.dot_general(
        left_mat, right_mat, (((0,), (0,)), ((), ())), preferred_element_type=jnp.float32
    )


def cols_product(left_mat, right_mat):
    return lax.dot_general(
        left_mat, right_mat, (((1,), (1,)), ((), ())), preferred_element_type=jnp.float32
    )


def frequency_table(level_values):
    half_width = TEMB // 2
    rate_table = jnp.exp(
        -math.log(10000.0) * jnp.arange(half_width, dtype=jnp.float32) / half_width
    )
    angles = level_values[..., None] * rate_table
    return jnp.concatenate([jnp.cos(angles), jnp.sin(angles)], axis=-1)


def noise_terms(level_values):
    angles = level_values * (0.5 * math.pi / NLEV)
    return (jnp.cos(angles), jnp.sin(angles))


def patchify(field_in):
    lead_shape = field_in.shape[:-2]
    rows_here = field_in.shape[-2]
    width_cells = field_in.shape[-1] // CHANNELS
    lead_rank = len(lead_shape)
    blocks_view = field_in.reshape(
        lead_shape + (rows_here // PATCH, PATCH, width_cells // PATCH, PATCH, CHANNELS)
    )
    order_axes = tuple(range(lead_rank)) + (
        lead_rank,
        lead_rank + 2,
        lead_rank + 1,
        lead_rank + 3,
        lead_rank + 4,
    )
    return jnp.transpose(blocks_view, order_axes).reshape(
        lead_shape + (rows_here // PATCH * (width_cells // PATCH), PATCH * PATCH * CHANNELS)
    )


def contract(left_mat, right_mat, left_dim, right_dim):
    return lax.dot_general(
        left_mat,
        right_mat,
        (((left_dim,), (right_dim,)), ((), ())),
        preferred_element_type=jnp.float32,
    )


def head_lanes(head):
    return lax.broadcasted_iota(jnp.int32, (1, PAIR), 1) // HD == head


def attend_kernel(chunk, query_ref, key_ref, value_ref, exps_ref, low_ref, mixed_ref, inverse_ref):
    key_total = key_ref.shape[1]
    block_rows = query_ref.shape[1]
    query_pair = query_ref[0]
    mixed_parts = []
    inverse_parts = []
    for head in range(2):
        lanes = head_lanes(head)
        query_head = jnp.where(lanes, query_pair, jnp.zeros_like(query_pair))

        def scores_of(rows):
            return contract(key_ref[0, rows, :], query_head, 1, 1) * SCORE_SCALE

        def add_chunk(rows, scores, total):
            exps = jnp.exp2(scores).astype(jnp.bfloat16)
            exps_ref[0, head, :, rows] = exps.T
            values = value_ref[0, rows, :]
            values = jnp.where(lanes, values, jnp.ones_like(values))
            return total + contract(values, exps, 0, 0)

        zeros = jnp.zeros((PAIR, block_rows), jnp.float32)
        total = zeros
        for start in range(0, key_total, chunk):
            rows = slice(start, start + chunk)
            total = add_chunk(rows, scores_of(rows), total)
        sum_rows = total[(1 - head) * HD : (1 - head) * HD + 8]
        outside = jnp.max(
            jnp.where((sum_rows > TOTAL_LOW) & (sum_rows < TOTAL_HIGH), 0.0, 1.0)
        )

        def shifted(unused):
            def chunk_rows(step):
                return pl.ds(pl.multiple_of(step * chunk, chunk), chunk)

            def highest(step, top):
                return jnp.maximum(
                    top, jnp.max(scores_of(chunk_rows(step)), axis=0, keepdims=True)
                )

            top = lax.fori_loop(
                0, key_total // chunk, highest, jnp.full((1, block_rows), -jnp.inf, jnp.float32)
            )

            def one_chunk(step, total):
                rows = chunk_rows(step)
                return add_chunk(rows, scores_of(rows) - top, total)

            return lax.fori_loop(0, key_total // chunk, one_chunk, zeros)

        total = lax.cond(outside > 0.0, shifted, lambda kept: kept, total)
        inverse = 1.0 / total[(1 - head) * HD : (2 - head) * HD]
        mixed_parts.append(total[head * HD : (head + 1) * HD] * inverse)
        inverse_parts.append(inverse)
    mixed = jnp.concatenate(mixed_parts, axis=0).T
    mixed_ref[0] = mixed
    low_ref[0] = mixed.astype(jnp.bfloat16)
    inverse_ref[0] = jnp.concatenate(inverse_parts, axis=0).T


def attend(query_in, key_value, key_place):
    units, query_total = query_in.shape[:2]
    key_total = key_value.shape[1]
    block_rows = min(1024, query_total)
    chunk = min(1024, key_total)

    def query_map(unit, step):
        return (unit, step, 0)

    query_spec = pl.BlockSpec((1, block_rows, PAIR), query_map)
    shape_rows = (units, query_total, PAIR)
    products = 4 * units * query_total * key_total * PAIR
    return pl.pallas_call(
        partial(attend_kernel, chunk),
        grid=(units, query_total // block_rows),
        in_specs=[
            query_spec,
            pl.BlockSpec((1, key_total, PAIR), lambda unit, step: (unit, 0, key_place)),
            pl.BlockSpec((1, key_total, PAIR), lambda unit, step: (unit, 0, key_place + 1)),
        ],
        out_specs=[
            pl.BlockSpec((1, 2, block_rows, key_total), lambda unit, step: (unit, 0, step, 0)),
            query_spec,
            query_spec,
            query_spec,
        ],
        out_shape=[
            jax.ShapeDtypeStruct((units, 2, query_total, key_total), jnp.bfloat16),
            jax.ShapeDtypeStruct(shape_rows, jnp.bfloat16),
            jax.ShapeDtypeStruct(shape_rows, jnp.float32),
            jax.ShapeDtypeStruct(shape_rows, jnp.float32),
        ],
        cost_estimate=pl.CostEstimate(
            flops=4 * products,
            bytes_accessed=4 * units * query_total * key_total,
            transcendentals=2 * units * query_total * key_total,
        ),
        compiler_params=pltpu.CompilerParams(vmem_limit_bytes=62 << 20),
    )(query_in, key_value, key_value)


def attend_back_kernel(
    chunk,
    exps_ref,
    query_ref,
    key_ref,
    value_ref,
    grad_ref,
    mixed_ref,
    inverse_ref,
    *grads_and_sums,
):
    *grad_refs, key_sums, value_sums = grads_and_sums
    step = pl.program_id(1)
    head = pl.program_id(2)
    key_total = key_ref.shape[1]
    block_rows = query_ref.shape[1]
    lane = lax.broadcasted_iota(jnp.int32, (1, PAIR), 1)
    lanes = head_lanes(head)
    grad_low = jnp.where(lanes, grad_ref[0].astype(jnp.float32) * inverse_ref[0], 0.0).astype(
        jnp.bfloat16
    )
    row_terms = jnp.sum(grad_low.astype(jnp.float32) * mixed_ref[0], axis=1, keepdims=True)
    term_high = row_terms.astype(jnp.bfloat16).astype(jnp.float32)
    term_rest = row_terms - term_high
    term_lanes = jnp.where(lane == 0, -term_high, jnp.where(lane == 1, -term_rest, 0.0))
    grad_wide = jnp.concatenate([grad_low, term_lanes.astype(jnp.bfloat16)], axis=1)
    query_pair = query_ref[0]
    query_columns = jnp.where(lanes, query_pair, jnp.zeros_like(query_pair)).T
    grad_columns = grad_low.T
    term_ones = jnp.broadcast_to(jnp.where(lane < 2, 1.0, 0.0).astype(jnp.bfloat16), (chunk, PAIR))

    @pl.when((step == 0) & (head == 0))
    def start_sums():
        key_sums[...] = jnp.zeros_like(key_sums)
        value_sums[...] = jnp.zeros_like(value_sums)

    grad_query = jnp.zeros((block_rows, PAIR), jnp.float32)
    for start in range(0, key_total, chunk):
        rows = slice(start, start + chunk)
        values_wide = jnp.concatenate([value_ref[0, rows, :], term_ones], axis=1)
        grad_probs = contract(grad_wide, values_wide, 1, 1).astype(jnp.bfloat16)
        exps = exps_ref[0, 0, :, rows]
        grad_scores = exps * grad_probs
        value_sums[:, rows] += contract(grad_columns, exps, 1, 0)
        key_sums[:, rows] += contract(query_columns, grad_scores, 1, 0)
        keys = key_ref[0, rows, :]
        keys = jnp.where(lanes, keys, jnp.zeros_like(keys))
        grad_query = grad_query + contract(grad_scores, keys, 1, 0)
    grad_query_low = (grad_query * HD ** (-0.5)).astype(jnp.bfloat16)

    fused = len(grad_refs) == 1
    first_row = pl.multiple_of(step * block_rows, block_rows) if fused else 0
    query_place = (0, pl.ds(first_row, block_rows), slice(0, PAIR))

    @pl.when(head == 0)
    def first_head():
        grad_refs[0][query_place] = grad_query_low

    @pl.when(head == 1)
    def second_head():
        grad_refs[0][query_place] = jnp.where(lanes, grad_query_low, grad_refs[0][query_place])

    @pl.when((step == pl.num_programs(1) - 1) & (head == 1))
    def write_sums():
        grad_key = (key_sums[...].T * HD ** (-0.5)).astype(jnp.bfloat16)
        grad_value = value_sums[...].T.astype(jnp.bfloat16)
        if fused:
            grad_refs[0][0, :, PAIR : 2 * PAIR] = grad_key
            grad_refs[0][0, :, 2 * PAIR :] = grad_value
        else:
            grad_refs[1][0] = grad_key
            grad_refs[2][0] = grad_value


def attend_back(exps, query_in, key_value, key_place, grad_mixed, mixed, inverse):
    units, query_total = mixed.shape[:2]
    key_total = key_value.shape[1]
    block_rows = min(1024, query_total)
    chunk = min(1024, key_total)
    query_spec = pl.BlockSpec((1, block_rows, PAIR), lambda unit, step, head: (unit, step, 0))
    whole_spec = pl.BlockSpec((1, key_total, PAIR), lambda unit, step, head: (unit, 0, 0))
    if query_total == key_total:
        out_sizes = [(key_total, 3 * PAIR)]
        out_specs = [
            pl.BlockSpec((1, key_total, 3 * PAIR), lambda unit, step, head: (unit, 0, 0))
        ]
    else:
        out_sizes = [(query_total, PAIR), (key_total, PAIR), (key_total, PAIR)]
        out_specs = [query_spec, whole_spec, whole_spec]
    products = 8 * units * query_total * key_total * PAIR
    return pl.pallas_call(
        partial(attend_back_kernel, chunk),
        grid=(units, query_total // block_rows, 2),
        in_specs=[
            pl.BlockSpec(
                (1, 1, block_rows, key_total), lambda unit, step, head: (unit, head, step, 0)
            ),
            query_spec,
            pl.BlockSpec((1, key_total, PAIR), lambda unit, step, head: (unit, 0, key_place)),
            pl.BlockSpec((1, key_total, PAIR), lambda unit, step, head: (unit, 0, key_place + 1)),
            query_spec,
            query_spec,
            query_spec,
        ],
        out_specs=out_specs,
        out_shape=[
            jax.ShapeDtypeStruct((units, rows, columns), jnp.bfloat16)
            for rows, columns in out_sizes
        ],
        scratch_shapes=[pltpu.VMEM((PAIR, key_total), jnp.float32)] * 2,
        cost_estimate=pl.CostEstimate(
            flops=4 * products,
            bytes_accessed=4 * units * query_total * key_total,
            transcendentals=0,
        ),
        compiler_params=pltpu.CompilerParams(vmem_limit_bytes=62 << 20),
    )(exps, query_in, key_value, key_value, grad_mixed, mixed, inverse)


def normalize(rows_in):
    centre = rows_in - jnp.mean(rows_in, axis=-1, keepdims=True)
    spread = jnp.mean(centre * centre, axis=-1, keepdims=True)
    inverse = lax.rsqrt(spread + EPS_NORM)
    return (centre * inverse, inverse)


def normalize_back(normed, inverse, scale_row, grad_out):
    grad_shift = jnp.sum(grad_out, axis=0, keepdims=True)
    grad_scale = jnp.sum(grad_out * normed, axis=0, keepdims=True)
    grad_normed = grad_out * (1.0 + scale_row)
    grad_rows = inverse * (
        grad_normed
        - jnp.mean(grad_normed, axis=-1, keepdims=True)
        - normed * jnp.mean(grad_normed * normed, axis=-1, keepdims=True)
    )
    return (grad_rows, grad_shift, grad_scale)


def mod_row(mods_ref, place, group):
    return mods_ref[pl.ds(group, 1), place * D : (place + 1) * D]


def group_rows(group, rows_group):
    return pl.ds(pl.multiple_of(group * rows_group, rows_group), rows_group)


def open_kernel(patch_ref, embed_ref, mods_ref, weight_ref, rows_ref, normed_ref, send_ref):
    groups = mods_ref.shape[0]
    rows_group = rows_ref.shape[0] // groups

    @pl.when(pl.program_id(0) == 0)
    def embed_rows():
        def one_group(group, unused):
            rows = group_rows(group, rows_group)
            residual = product(patch_ref[rows, :], embed_ref[...])
            rows_ref[rows, :] = residual
            normed, unused_inverse = normalize(residual)
            normed_ref[rows, :] = to_half(
                normed * (1.0 + mod_row(mods_ref, 1, group)) + mod_row(mods_ref, 0, group)
            )
            return unused

        lax.fori_loop(0, groups, one_group, 0, unroll=True)

    columns = send_ref.shape[2]
    for place in range(send_ref.shape[0]):
        send_ref[place] = to_half(
            product(
                normed_ref[...], weight_ref[0, :, place * columns : (place + 1) * columns]
            )
        )


def open_layer(patch_rows, w_embed, mods, w_qkv):
    tokens = patch_rows.shape[0]
    blocks, unused, columns = w_qkv.shape
    per_block = columns // (3 * PAIR)
    whole = pl.BlockSpec((tokens, D), lambda step: (0, 0))
    return pl.pallas_call(
        open_kernel,
        grid=(blocks,),
        in_specs=[
            pl.BlockSpec(patch_rows.shape, lambda step: (0, 0)),
            pl.BlockSpec(w_embed.shape, lambda step: (0, 0)),
            pl.BlockSpec(mods.shape, lambda step: (0, 0)),
            pl.BlockSpec((1, D, columns), lambda step: (step, 0, 0)),
        ],
        out_specs=[
            whole,
            whole,
            pl.BlockSpec((per_block, tokens, 3 * PAIR), lambda step: (step, 0, 0)),
        ],
        out_shape=[
            jax.ShapeDtypeStruct((tokens, D), jnp.float32),
            jax.ShapeDtypeStruct((tokens, D), jnp.bfloat16),
            jax.ShapeDtypeStruct((blocks * per_block, tokens, 3 * PAIR), jnp.bfloat16),
        ],
        cost_estimate=pl.CostEstimate(
            flops=2 * tokens * D * blocks * columns,
            bytes_accessed=2 * blocks * D * columns + 12 * tokens * D,
            transcendentals=0,
        ),
        compiler_params=pltpu.CompilerParams(vmem_limit_bytes=60 << 20),
    )(patch_rows, w_embed, mods, w_qkv)


GELU_RATE = math.sqrt(2.0 / math.pi)
GELU_CUBE = 0.044715


def middle_kernel(
    head_cols,
    hidden_cols,
    mixed_ref,
    rows_ref,
    mods_ref,
    goal_ref,
    coef_ref,
    head_ref,
    weights_hbm,
    normed_hbm,
    act_hbm,
    grad_mlp_hbm,
    grad_hidden_hbm,
    grad_attn_hbm,
    grad_rows_hbm,
    send_ref,
    grad_mods_ref,
    grad_head_ref,
    loss_ref,
    weights,
    normed_low,
    act_low,
    grad_mlp_low,
    grad_hidden_low,
    grad_attn_low,
    grad_rows,
    attn_sum,
    middle,
    mlp_sum,
    slopes,
    out_sems,
    wide_sems,
    act_sems,
    hidden_sems,
    row_sems,
):
    blocks = weights.shape[0]
    groups = mods_ref.shape[0]
    rows_group = rows_ref.shape[0] // groups
    per_block = head_cols // PAIR
    wide = 2 * hidden_cols
    up_columns = slice(0, hidden_cols)
    down_columns = slice(hidden_cols, wide)
    out_columns = slice(wide, wide + head_cols)

    def fetch_out(block):
        return pltpu.make_async_copy(
            weights_hbm.at[block, :, out_columns],
            weights.at[block, :, out_columns],
            out_sems.at[block],
        )

    def fetch_wide(block):
        return pltpu.make_async_copy(
            weights_hbm.at[block, :, 0:wide], weights.at[block, :, 0:wide], wide_sems.at[block]
        )

    def put_act(block):
        columns = pl.ds(pl.multiple_of(block * hidden_cols, hidden_cols), hidden_cols)
        return pltpu.make_async_copy(
            act_low.at[block], act_hbm.at[:, columns], act_sems.at[block]
        )

    def put_hidden(block):
        columns = pl.ds(pl.multiple_of(block * hidden_cols, hidden_cols), hidden_cols)
        return pltpu.make_async_copy(
            grad_hidden_low.at[block], grad_hidden_hbm.at[:, columns], hidden_sems.at[block]
        )

    put_normed = pltpu.make_async_copy(normed_low, normed_hbm, row_sems.at[0])
    put_grad_mlp = pltpu.make_async_copy(grad_mlp_low, grad_mlp_hbm, row_sems.at[1])
    put_grad_attn = pltpu.make_async_copy(grad_attn_low, grad_attn_hbm, row_sems.at[2])
    put_grad_rows = pltpu.make_async_copy(grad_rows, grad_rows_hbm, row_sems.at[3])

    def each_block(one_block):
        def step(block, unused):
            one_block(block)
            return unused

        lax.fori_loop(0, blocks, step, 0)

    def each_group(one_group):
        def step(group, unused):
            one_group(group, group_rows(group, rows_group))
            return unused

        lax.fori_loop(0, groups, step, 0, unroll=True)

    each_block(lambda block: fetch_out(block).start())
    each_block(lambda block: fetch_wide(block).start())
    attn_sum[...] = jnp.zeros_like(attn_sum)
    mlp_sum[...] = jnp.zeros_like(mlp_sum)

    def attn_out(block):
        fetch_out(block).wait()
        mixed = jnp.concatenate(
            [mixed_ref[block * per_block + place] for place in range(per_block)], axis=1
        )
        attn_sum[...] += contract(mixed, weights[block, :, out_columns], 1, 1)

    each_block(attn_out)

    def to_middle(group, rows):
        residual = rows_ref[rows, :] + mod_row(mods_ref, 2, group) * attn_sum[rows, :]
        middle[rows, :] = residual
        normed, unused_inverse = normalize(residual)
        normed_low[rows, :] = to_half(
            normed * (1.0 + mod_row(mods_ref, 4, group)) + mod_row(mods_ref, 3, group)
        )

    each_group(to_middle)
    put_normed.start()

    def forward_mlp(block):
        fetch_wide(block).wait()
        hidden = product(normed_low[...], weights[block, :, up_columns])
        square = hidden * hidden
        bend = jnp.tanh(GELU_RATE * hidden * (1.0 + GELU_CUBE * square))
        half_open = 0.5 * (1.0 + bend)
        act = to_half(hidden * half_open)
        act_low[block] = act
        slope = half_open + 0.5 * hidden * (1.0 - bend * bend) * (
            GELU_RATE * (1.0 + 3.0 * GELU_CUBE * square)
        )
        slopes[block] = to_half(slope)
        put_act(block).start()
        mlp_sum[...] += contract(act, weights[block, :, down_columns], 1, 1)

    each_block(forward_mlp)
    grad_head_ref[...] = jnp.zeros_like(grad_head_ref)
    loss_ref[...] = jnp.zeros_like(loss_ref)

    def turn(group, rows):
        mlp_out = mlp_sum[rows, :]
        gate = mod_row(mods_ref, 5, group)
        normed, inverse = normalize(middle[rows, :] + gate * mlp_out)
        scale_row = mod_row(mods_ref, 7, group)
        final_low = to_half(normed * (1.0 + scale_row) + mod_row(mods_ref, 6, group))
        error_rows = contract(final_low, head_ref[...], 1, 1) - goal_ref[rows, :]
        weighted = coef_ref[pl.ds(group, 1), :] * error_rows
        loss_ref[pl.ds(0, 1), :] += jnp.sum(weighted * error_rows, axis=0, keepdims=True)
        grad_pred = to_half(2.0 * weighted)
        grad_head_ref[...] += contract(grad_pred, final_low, 0, 0)
        grad_final = product(grad_pred, head_ref[...])
        grad_residual, grad_six, grad_seven = normalize_back(
            normed, inverse, scale_row, grad_final
        )
        grad_mods_ref[4, pl.ds(group, 1), :] = grad_six
        grad_mods_ref[5, pl.ds(group, 1), :] = grad_seven
        grad_mods_ref[3, pl.ds(group, 1), :] = jnp.sum(
            mlp_out * grad_residual, axis=0, keepdims=True
        )
        grad_rows[rows, :] = grad_residual
        grad_mlp_low[rows, :] = to_half(gate * grad_residual)

    each_group(turn)
    put_grad_mlp.start()
    mlp_sum[...] = jnp.zeros_like(mlp_sum)

    def backward_mlp(block):
        grad_act = product(grad_mlp_low[...], weights[block, :, down_columns])
        grad_hidden = to_half(grad_act * slopes[block].astype(jnp.float32))
        grad_hidden_low[block] = grad_hidden
        put_hidden(block).start()
        mlp_sum[...] += contract(grad_hidden, weights[block, :, up_columns], 1, 1)

    each_block(backward_mlp)

    def from_middle(group, rows):
        normed, inverse = normalize(middle[rows, :])
        grad_branch, grad_three, grad_four = normalize_back(
            normed, inverse, mod_row(mods_ref, 4, group), mlp_sum[rows, :]
        )
        grad_residual = grad_rows[rows, :] + grad_branch
        grad_mods_ref[1, pl.ds(group, 1), :] = grad_three
        grad_mods_ref[2, pl.ds(group, 1), :] = grad_four
        grad_mods_ref[0, pl.ds(group, 1), :] = jnp.sum(
            attn_sum[rows, :] * grad_residual, axis=0, keepdims=True
        )
        grad_rows[rows, :] = grad_residual
        grad_attn_low[rows, :] = to_half(mod_row(mods_ref, 2, group) * grad_residual)

    each_group(from_middle)
    put_grad_rows.start()
    put_grad_attn.start()

    def to_send(block):
        grad_mixed = to_half(product(grad_attn_low[...], weights[block, :, out_columns]))
        for place in range(per_block):
            send_ref[block * per_block + place] = grad_mixed[
                :, place * PAIR : (place + 1) * PAIR
            ]

    each_block(to_send)
    put_normed.wait()
    put_grad_mlp.wait()
    put_grad_rows.wait()
    put_grad_attn.wait()
    each_block(lambda block: put_act(block).wait())
    each_block(lambda block: put_hidden(block).wait())


def middle_layer(mixed_pairs, rows_in, mods, goal, coef, w_head, weights, head_cols, hidden_cols):
    blocks = weights.shape[0]
    tokens = rows_in.shape[0]
    groups = mods.shape[0]
    in_vmem = pl.BlockSpec(memory_space=pltpu.VMEM)
    in_hbm = pl.BlockSpec(memory_space=pl.ANY)
    rows_low = pltpu.VMEM((tokens, D), jnp.bfloat16)
    rows_full = pltpu.VMEM((tokens, D), jnp.float32)
    wide_low = pltpu.VMEM((blocks, tokens, hidden_cols), jnp.bfloat16)
    block_sems = pltpu.SemaphoreType.DMA((blocks,))
    return pl.pallas_call(
        partial(middle_kernel, head_cols, hidden_cols),
        in_specs=[in_vmem] * 6 + [in_hbm],
        out_specs=[in_hbm] * 6 + [in_vmem] * 4,
        out_shape=[
            jax.ShapeDtypeStruct((tokens, D), jnp.bfloat16),
            jax.ShapeDtypeStruct((tokens, blocks * hidden_cols), jnp.bfloat16),
            jax.ShapeDtypeStruct((tokens, D), jnp.bfloat16),
            jax.ShapeDtypeStruct((tokens, blocks * hidden_cols), jnp.bfloat16),
            jax.ShapeDtypeStruct((tokens, D), jnp.bfloat16),
            jax.ShapeDtypeStruct((tokens, D), jnp.float32),
            jax.ShapeDtypeStruct(mixed_pairs.shape, jnp.bfloat16),
            jax.ShapeDtypeStruct((6, groups, D), jnp.float32),
            jax.ShapeDtypeStruct(w_head.shape, jnp.float32),
            jax.ShapeDtypeStruct((8, PAIR), jnp.float32),
        ],
        scratch_shapes=[
            pltpu.VMEM(weights.shape, jnp.bfloat16),
            rows_low,
            wide_low,
            rows_low,
            wide_low,
            rows_low,
            rows_full,
            rows_full,
            rows_full,
            rows_full,
            wide_low,
            block_sems,
            block_sems,
            block_sems,
            block_sems,
            pltpu.SemaphoreType.DMA((4,)),
        ],
        cost_estimate=pl.CostEstimate(
            flops=4 * tokens * D * blocks * (2 * hidden_cols + head_cols),
            bytes_accessed=2 * weights.size + 30 * tokens * D,
            transcendentals=tokens * blocks * hidden_cols,
        ),
        compiler_params=pltpu.CompilerParams(vmem_limit_bytes=62 << 20),
    )(mixed_pairs, rows_in, mods, goal, coef, w_head, weights)


def close_kernel(
    blocks,
    grad_ref,
    rows_ref,
    grad_rows_ref,
    mods_ref,
    patch_ref,
    weight_ref,
    grad_mods_ref,
    grad_embed_ref,
    total,
):
    step = pl.program_id(0)
    groups = mods_ref.shape[0]
    rows_group = rows_ref.shape[0] // groups
    columns = grad_ref.shape[2]
    part = jnp.zeros(total.shape, jnp.float32)
    for place in range(grad_ref.shape[0]):
        part = part + contract(
            grad_ref[place], weight_ref[0, :, place * columns : (place + 1) * columns], 1, 1
        )

    @pl.when(step == 0)
    def first():
        total[...] = part

    @pl.when(step > 0)
    def later():
        total[...] += part

    @pl.when(step == blocks - 1)
    def finish():
        grad_embed_ref[...] = jnp.zeros_like(grad_embed_ref)

        def one_group(group, unused):
            rows = group_rows(group, rows_group)
            normed, inverse = normalize(rows_ref[rows, :])
            grad_branch, grad_zero, grad_one = normalize_back(
                normed, inverse, mod_row(mods_ref, 1, group), total[rows, :]
            )
            grad_mods_ref[0, pl.ds(group, 1), :] = grad_zero
            grad_mods_ref[1, pl.ds(group, 1), :] = grad_one
            grad_low = to_half(grad_rows_ref[rows, :] + grad_branch)
            grad_embed_ref[...] += contract(patch_ref[rows, :], grad_low, 0, 0)
            return unused

        lax.fori_loop(0, groups, one_group, 0, unroll=True)


def close_layer(grad_pairs, rows_in, grad_rows, mods, patch_rows, w_qkv):
    tokens = rows_in.shape[0]
    groups = mods.shape[0]
    blocks, unused, columns = w_qkv.shape
    per_block = columns // (3 * PAIR)

    def whole(shape):
        return pl.BlockSpec(shape, lambda step: (0,) * len(shape))

    return pl.pallas_call(
        partial(close_kernel, blocks),
        grid=(blocks,),
        in_specs=[
            pl.BlockSpec((per_block, tokens, 3 * PAIR), lambda step: (step, 0, 0)),
            whole(rows_in.shape),
            whole(grad_rows.shape),
            whole(mods.shape),
            whole(patch_rows.shape),
            pl.BlockSpec((1, D, columns), lambda step: (step, 0, 0)),
        ],
        out_specs=[whole((2, groups, D)), whole((PAIR, D))],
        out_shape=[
            jax.ShapeDtypeStruct((2, groups, D), jnp.float32),
            jax.ShapeDtypeStruct((PAIR, D), jnp.float32),
        ],
        scratch_shapes=[pltpu.VMEM((tokens, D), jnp.float32)],
        cost_estimate=pl.CostEstimate(
            flops=2 * tokens * D * blocks * columns,
            bytes_accessed=2 * blocks * D * columns + 16 * tokens * D,
            transcendentals=0,
        ),
        compiler_params=pltpu.CompilerParams(vmem_limit_bytes=60 << 20),
    )(grad_pairs, rows_in, grad_rows, mods, patch_rows, w_qkv)


def weight_kernel(clips, kinds, *refs):
    out = refs[-1]
    column = 0
    for kind in range(kinds):
        lefts = refs[2 * clips * kind : 2 * clips * kind + clips]
        rights = refs[2 * clips * kind + clips : 2 * clips * (kind + 1)]
        paired = len(rights[0].shape) == 3
        pieces = rights[0].shape[0] if paired else rights[0].shape[1] // 512
        width = rights[0].shape[2] if paired else 512
        for piece in range(pieces):
            total = None
            for left, right in zip(lefts, rights):
                block = right[piece] if paired else right[:, piece * width : (piece + 1) * width]
                part = contract(left[...], block, 0, 0)
                total = part if total is None else total + part
            out[0, :, column : column + width] = to_half(total)
            column += width


def weight_grads(blocks, terms):
    clips = len(terms[0][0])
    operands = []
    specs = []
    columns_all = 0
    flops = 0
    for lefts, rights in terms:
        for left in lefts:
            operands.append(left)
            specs.append(pl.BlockSpec(left.shape, lambda step: (0, 0)))
        for right in rights:
            operands.append(right)
            if right.ndim == 3:
                per_block = right.shape[0] // blocks
                specs.append(
                    pl.BlockSpec((per_block,) + right.shape[1:], lambda step: (step, 0, 0))
                )
                columns = per_block * right.shape[2]
            else:
                columns = right.shape[1] // blocks
                specs.append(pl.BlockSpec((right.shape[0], columns), lambda step: (0, step)))
            flops += 2 * right.size * D
        columns_all += columns
    return pl.pallas_call(
        partial(weight_kernel, clips, len(terms)),
        grid=(blocks,),
        in_specs=specs,
        out_specs=pl.BlockSpec((1, D, columns_all), lambda step: (step, 0, 0)),
        out_shape=jax.ShapeDtypeStruct((blocks, D, columns_all), jnp.bfloat16),
        cost_estimate=pl.CostEstimate(
            flops=flops,
            bytes_accessed=2 * blocks * D * columns_all + 2 * sum(op.size for op in operands),
            transcendentals=0,
        ),
        compiler_params=pltpu.CompilerParams(vmem_limit_bytes=62 << 20),
    )(*operands)


def pack_kernel(head_cols, in_ref, outs_ref, qkv_ref, rest_ref):
    pairs = head_cols // PAIR
    for pair in range(pairs):
        for kind in range(3):
            source = (kind * pairs + pair) * PAIR
            place = (pair * 3 + kind) * PAIR
            qkv_ref[:, place : place + PAIR] = to_half(in_ref[:, source : source + PAIR])
    hidden_cols = in_ref.shape[1] - 3 * head_cols
    rest_ref[:, :hidden_cols] = to_half(in_ref[:, 3 * head_cols :])
    columns = to_half(outs_ref[...].T)
    rest_ref[:, hidden_cols : 2 * hidden_cols] = columns[:, head_cols:]
    rest_ref[:, 2 * hidden_cols :] = columns[:, :head_cols]


def pack_weights(w_in, w_outs, head_cols):
    rows = w_in.shape[0]
    hidden_cols = w_in.shape[1] - 3 * head_cols
    return pl.pallas_call(
        partial(pack_kernel, head_cols),
        out_shape=[
            jax.ShapeDtypeStruct((rows, 3 * head_cols), jnp.bfloat16),
            jax.ShapeDtypeStruct((rows, 2 * hidden_cols + head_cols), jnp.bfloat16),
        ],
    )(w_in, w_outs)


def swap_groups(array_in):
    dp_size = lax.axis_size("dp")
    tensor_size = lax.axis_size("tensor")
    pairs = [
        (row * tensor_size + column, column * dp_size + row)
        for row in range(dp_size)
        for column in range(tensor_size)
    ]
    return lax.ppermute(array_in, ("dp", "tensor"), pairs)


MESH_ID = pl.DeviceIdType.MESH


def places():
    dp_size, frame_size, tensor_size = [
        lax.axis_size(axis) for axis in ("dp", "frame", "tensor")
    ]
    here = [lax.axis_index(axis) for axis in ("dp", "frame", "tensor")]
    return (dp_size, frame_size, tensor_size, *here)


def device(row, frame, column):
    return {"dp": row, "frame": frame, "tensor": column}


def greet_plane():
    dp_size, frame_size, tensor_size, row, frame, column = places()
    plane = dp_size * frame_size
    barrier = pltpu.get_barrier_semaphore()
    for shift in range(1, plane):
        other = lax.rem(row * frame_size + frame + shift, plane)
        pl.semaphore_signal(
            barrier,
            inc=1,
            device_id=device(lax.div(other, frame_size), lax.rem(other, frame_size), column),
            device_id_type=MESH_ID,
        )
    pl.semaphore_wait(barrier, plane - 1)


def greet_all():
    dp_size, frame_size, tensor_size, row, frame, column = places()
    plane = dp_size * frame_size
    everyone = plane * tensor_size
    here = (row * frame_size + frame) * tensor_size + column
    barrier = pltpu.get_barrier_semaphore()

    def signal(shift, unused):
        other = lax.rem(here + shift, everyone)
        place = lax.div(other, tensor_size)
        pl.semaphore_signal(
            barrier,
            inc=1,
            device_id=device(
                lax.div(place, frame_size), lax.rem(place, frame_size), lax.rem(other, tensor_size)
            ),
            device_id_type=MESH_ID,
        )
        return unused

    lax.fori_loop(1, everyone, signal, 0)
    pl.semaphore_wait(barrier, everyone - 1)


def send(source, target, send_sem, receive_sem, device_id):
    return pltpu.make_async_remote_copy(
        src_ref=source,
        dst_ref=target,
        send_sem=send_sem,
        recv_sem=receive_sem,
        device_id=device_id,
        device_id_type=MESH_ID,
    )


def plane_copies(source_of, target_of, send_sems, receive_sems):
    dp_size, frame_size, tensor_size, row, frame, column = places()
    plane = dp_size * frame_size
    here = row * frame_size + frame
    copies = []
    for shift in range(1, plane):
        other = lax.rem(here + shift, plane)
        copies.append(
            send(
                source_of(other),
                target_of(here),
                send_sems.at[shift - 1],
                receive_sems.at[shift - 1],
                device(lax.div(other, frame_size), lax.rem(other, frame_size), column),
            )
        )
    return copies


def axis_copies(axis, source_of, target_of, send_sems, receive_sems):
    size = lax.axis_size(axis)
    here = lax.axis_index(axis)
    row, frame, column = [lax.axis_index(name) for name in ("dp", "frame", "tensor")]
    copies = []
    for shift in range(1, size):
        other = lax.rem(here + shift, size)
        target = device(other, frame, column) if axis == "dp" else device(row, frame, other)
        copies.append(
            send(
                source_of(other),
                target_of(here),
                send_sems.at[shift - 1],
                receive_sems.at[shift - 1],
                target,
            )
        )
    return copies


def plane_gather_kernel(count, *refs):
    ins = refs[:count]
    outs = refs[count : 2 * count]
    sems = refs[2 * count :]
    greet_plane()
    here = lax.axis_index("dp") * lax.axis_size("frame") + lax.axis_index("frame")
    copies = []
    for place in range(count):
        copies += plane_copies(
            lambda other, place=place: ins[place],
            lambda own, place=place: outs[place].at[own],
            sems[2 * place],
            sems[2 * place + 1],
        )
    for copy in copies:
        copy.start()
    for place in range(count):
        outs[place][here] = ins[place][...]
    for copy in copies:
        copy.wait()


def remote_call(kernel, collective_id, out_shape, scratch_shapes, operands):
    in_vmem = pl.BlockSpec(memory_space=pltpu.VMEM)
    return pl.pallas_call(
        kernel,
        out_shape=out_shape,
        in_specs=[in_vmem] * len(operands),
        out_specs=[in_vmem] * len(out_shape),
        scratch_shapes=scratch_shapes,
        compiler_params=pltpu.CompilerParams(
            collective_id=collective_id, has_side_effects=True, vmem_limit_bytes=48 << 20
        ),
    )(*operands)


def plane_gather(arrays):
    plane = lax.axis_size("dp") * lax.axis_size("frame")
    return remote_call(
        partial(plane_gather_kernel, len(arrays)),
        0,
        [jax.ShapeDtypeStruct((plane,) + array.shape, array.dtype) for array in arrays],
        [pltpu.SemaphoreType.DMA((plane - 1,))] * (2 * len(arrays)),
        arrays,
    )


def swap_block(block, swapped, send_sem, receive_sem, start):
    row, frame, column = [lax.axis_index(name) for name in ("dp", "frame", "tensor")]
    own = row == column
    copy = send(block, swapped, send_sem, receive_sem, device(column, frame, row))

    @pl.when(jnp.logical_not(own))
    def remote():
        copy.start() if start else copy.wait()

    if start:

        @pl.when(own)
        def keep():
            swapped[...] = block[...]


def mods_kernel(
    parts,
    out,
    received,
    block,
    swapped,
    plane_send,
    plane_receive,
    swap_send,
    swap_receive,
    spread_send,
    spread_receive,
):
    dp_size, frame_size, tensor_size, row, frame, column = places()
    plane = dp_size * frame_size
    here = row * frame_size + frame
    greet_all()
    copies = plane_copies(
        lambda other: parts.at[other], lambda own: received.at[own], plane_send, plane_receive
    )
    for copy in copies:
        copy.start()
    received[here] = parts[here]
    for copy in copies:
        copy.wait()
    total = received[0]
    for place in range(1, plane):
        total = total + received[place]
    block[...] = total
    swap_block(block, swapped, swap_send.at[0], swap_receive.at[0], True)
    swap_block(block, swapped, swap_send.at[0], swap_receive.at[0], False)
    copies = axis_copies(
        "dp", lambda other: swapped, lambda own: out.at[own], spread_send, spread_receive
    )
    for copy in copies:
        copy.start()
    out[row] = swapped[...]
    for copy in copies:
        copy.wait()


def spread_mods(parts):
    plane, rows, columns = parts.shape
    dma = pltpu.SemaphoreType.DMA
    dp_size = lax.axis_size("dp")
    return remote_call(
        mods_kernel,
        1,
        [jax.ShapeDtypeStruct((dp_size, rows, columns), jnp.float32)],
        [
            pltpu.VMEM(parts.shape, jnp.float32),
            pltpu.VMEM(parts.shape[1:], jnp.float32),
            pltpu.VMEM(parts.shape[1:], jnp.float32),
            dma((plane - 1,)),
            dma((plane - 1,)),
            dma((1,)),
            dma((1,)),
            dma((dp_size - 1,)),
            dma((dp_size - 1,)),
        ],
        [parts],
    )[0]


def cond_kernel(
    mod_parts,
    patch_parts,
    weight,
    mod_all,
    cond_all,
    patch_out,
    mod_received,
    patch_received,
    mod_block,
    patch_block,
    patch_tensor,
    cond_part,
    cond_tensor,
    mod_swapped,
    cond_block,
    swap_send,
    swap_receive,
    dp_send,
    dp_receive,
    patch_send,
    patch_receive,
    spread_send,
    spread_receive,
    patch_tensor_send,
    patch_tensor_receive,
    cond_send,
    cond_receive,
    gather_send,
    gather_receive,
):
    dp_size, frame_size, tensor_size, row, frame, column = places()
    plane = dp_size * frame_size
    here = row * frame_size + frame
    greet_all()
    copies = axis_copies(
        "dp",
        lambda other: mod_parts.at[other],
        lambda own: mod_received.at[own],
        dp_send,
        dp_receive,
    ) + plane_copies(
        lambda other: patch_parts.at[other],
        lambda own: patch_received.at[own],
        patch_send,
        patch_receive,
    )
    for copy in copies:
        copy.start()
    mod_received[row] = mod_parts[row]
    patch_received[here] = patch_parts[here]
    for copy in copies:
        copy.wait()
    total = mod_received[0].astype(jnp.float32)
    for place in range(1, dp_size):
        total = total + mod_received[place].astype(jnp.float32)
    mod_block[...] = to_half(total)
    total = patch_received[0]
    for place in range(1, plane):
        total = total + patch_received[place]
    patch_block[...] = total
    swap_block(mod_block, mod_swapped, swap_send.at[0], swap_receive.at[0], True)
    patch_copies = axis_copies(
        "tensor",
        lambda other: patch_block,
        lambda own: patch_tensor.at[own],
        patch_tensor_send,
        patch_tensor_receive,
    )
    for copy in patch_copies:
        copy.start()
    patch_tensor[column] = patch_block[...]
    swap_block(mod_block, mod_swapped, swap_send.at[0], swap_receive.at[0], False)
    mod_copies = plane_copies(
        lambda other: mod_swapped, lambda own: mod_all.at[own], spread_send, spread_receive
    )
    cond_part[...] = to_half(contract(mod_swapped[...], weight[...], 1, 1))
    cond_copies = axis_copies(
        "tensor",
        lambda other: cond_part,
        lambda own: cond_tensor.at[own],
        cond_send,
        cond_receive,
    )
    for copy in cond_copies + mod_copies:
        copy.start()
    mod_all[here] = mod_swapped[...]
    cond_tensor[column] = cond_part[...]
    for copy in patch_copies + cond_copies:
        copy.wait()
    total = cond_tensor[0].astype(jnp.float32)
    total_patch = patch_tensor[0]
    for place in range(1, tensor_size):
        total = total + cond_tensor[place].astype(jnp.float32)
        total_patch = total_patch + patch_tensor[place]
    patch_out[...] = total_patch
    cond_block[...] = to_half(total)
    gather_copies = plane_copies(
        lambda other: cond_block, lambda own: cond_all.at[own], gather_send, gather_receive
    )
    for copy in gather_copies:
        copy.start()
    cond_all[here] = cond_block[...]
    for copy in gather_copies + mod_copies:
        copy.wait()


def cond_sums(mod_parts, patch_parts, weight):
    dp_size, rows, columns = mod_parts.shape
    plane = patch_parts.shape[0]
    tensor_size = lax.axis_size("tensor")
    features = weight.shape[0]

    def held(*shape):
        return pltpu.VMEM(shape, jnp.float32)

    def low(*shape):
        return pltpu.VMEM(shape, jnp.bfloat16)

    def sems(*counts):
        return [pltpu.SemaphoreType.DMA((count,)) for count in counts]

    patch_shape = patch_parts.shape[1:]
    return remote_call(
        cond_kernel,
        2,
        [
            jax.ShapeDtypeStruct((plane, rows, columns), jnp.bfloat16),
            jax.ShapeDtypeStruct((plane, rows, features), jnp.bfloat16),
            jax.ShapeDtypeStruct(patch_shape, jnp.float32),
        ],
        [
            low(*mod_parts.shape),
            held(*patch_parts.shape),
            low(rows, columns),
            held(*patch_shape),
            held(tensor_size, *patch_shape),
            low(rows, features),
            low(tensor_size, rows, features),
            low(rows, columns),
            low(rows, features),
        ]
        + sems(1, 1, dp_size - 1, dp_size - 1, *[plane - 1] * 4)
        + sems(*[tensor_size - 1] * 4, plane - 1, plane - 1),
        [mod_parts, patch_parts, weight],
    )


def total_kernel(tile, out, received, send_sems, receive_sems):
    dp_size, frame_size, tensor_size, row, frame, column = places()
    everyone = dp_size * frame_size * tensor_size
    here = (row * frame_size + frame) * tensor_size + column
    greet_all()

    def copy_to(shift):
        other = lax.rem(here + shift, everyone)
        place = lax.div(other, tensor_size)
        return send(
            tile,
            received.at[here],
            send_sems.at[shift - 1],
            receive_sems.at[shift - 1],
            device(
                lax.div(place, frame_size), lax.rem(place, frame_size), lax.rem(other, tensor_size)
            ),
        )

    def start(shift, unused):
        copy_to(shift).start()
        return unused

    def finish(shift, unused):
        copy_to(shift).wait()
        return unused

    lax.fori_loop(1, everyone, start, 0)
    received[here] = tile[...]
    lax.fori_loop(1, everyone, finish, 0)
    out[...] = jnp.sum(received[...], axis=0)


def total_over_all(first, second):
    lane = jnp.arange(PAIR)[None, :]
    tile = jnp.where(lane == 0, first, jnp.where(lane == 1, second, 0.0))
    tile = jnp.broadcast_to(tile, (8, PAIR)).astype(jnp.float32)
    everyone = lax.axis_size(EVERY)
    sums = remote_call(
        total_kernel,
        3,
        [jax.ShapeDtypeStruct((8, PAIR), jnp.float32)],
        [
            pltpu.VMEM((everyone, 8, PAIR), jnp.float32),
            pltpu.SemaphoreType.DMA((everyone - 1,)),
            pltpu.SemaphoreType.DMA((everyone - 1,)),
        ],
        [tile],
    )[0]
    return (sums[0, 0], sums[0, 1])


def spread_heads():
    return (D // PAIR) % (lax.axis_size("dp") * lax.axis_size("frame")) == 0


def exchange_axes():
    axes = PLANE if spread_heads() else ("dp",)
    return (axes, math.prod(lax.axis_size(axis) for axis in axes))


def to_heads(pairs_in):
    axes, parts = exchange_axes()
    pairs, tokens, columns = pairs_in.shape
    moved = lax.all_to_all(
        pairs_in.reshape(parts, pairs // parts, tokens, columns), axes, 0, 0, tiled=True
    )
    return jnp.swapaxes(moved, 0, 1).reshape(pairs // parts, parts * tokens, columns)


def to_tokens(units_in):
    axes, parts = exchange_axes()
    units, tokens_all, columns = units_in.shape
    by_place = jnp.swapaxes(units_in.reshape(units, parts, tokens_all // parts, columns), 0, 1)
    moved = lax.all_to_all(by_place, axes, 0, 0, tiled=True)
    return moved.reshape(parts * units, tokens_all // parts, columns)


def gather_blocks(shard):
    whole = lax.all_gather(shard, EVERY, axis=0, tiled=True)
    return whole.reshape(lax.axis_size("tensor"), D, -1)


def scatter_blocks(blocks_in):
    flat = blocks_in.reshape(-1, blocks_in.shape[-1])
    return lax.psum_scatter(flat, EVERY, scatter_dimension=0, tiled=True)


def scatter_stages(blocks_in):
    dp_size, frame_size, tensor_size, row, frame, column = places()
    pairs_dp = dp_size // 2
    side = lax.rem(row, 2)
    columns = blocks_in.shape[-1]
    parted = blocks_in.reshape(tensor_size, pairs_dp, 2, frame_size, -1, columns)

    def of_side(which):
        return lax.dynamic_index_in_dim(parted, which, 2, keepdims=False)

    swaps = [(place, place + 1 - 2 * (place % 2)) for place in range(dp_size)]
    received = lax.ppermute(of_side(1 - side), "dp", swaps)
    halves = to_half(of_side(side).astype(jnp.float32) + received.astype(jnp.float32))
    members = pairs_dp * frame_size
    halves = jnp.moveaxis(halves, 0, 2).reshape(members, tensor_size, -1, columns)
    here = lax.div(row, 2) * frame_size + frame
    total = lax.dynamic_index_in_dim(halves, here, 0, keepdims=False).astype(jnp.float32)
    moved = []
    for shift in range(1, members):
        routes = []
        for source in range(members):
            target = (source + shift) % members
            for core in range(2):
                source_row = source // frame_size * 2 + core
                target_row = target // frame_size * 2 + core
                routes.append(
                    (
                        source_row * frame_size + source % frame_size,
                        target_row * frame_size + target % frame_size,
                    )
                )
        block = lax.dynamic_index_in_dim(
            halves, lax.rem(here + shift, members), 0, keepdims=False
        )
        moved.append(lax.ppermute(block, PLANE, routes))
    for block in moved:
        total = total + block.astype(jnp.float32)
    over_tensor = lax.all_to_all(to_half(total), "tensor", 0, 0, tiled=True)
    return jnp.sum(over_tensor.astype(jnp.float32), axis=0)


def pad_lanes(rows_in, axis):
    widths = [(0, 0)] * rows_in.ndim
    widths[axis] = (0, PAIR - rows_in.shape[axis])
    return jnp.pad(rows_in, widths)


def after(value, *others):
    return lax.optimization_barrier((value,) + others)[0]


def update_part(refs, rows, columns, gradient, rates):
    master_ref, first_ref, second_ref, master_out, first_out, second_out, half_out = refs
    factor, fix_first, fix_second = rates
    place = (Ellipsis, rows, columns)
    master = master_ref[place]
    clipped = gradient * factor
    first_new = BETA_FIRST * first_ref[place] + (1.0 - BETA_FIRST) * clipped
    second_new = BETA_SECOND * second_ref[place] + (1.0 - BETA_SECOND) * clipped * clipped
    step_dir = first_new / fix_first / (jnp.sqrt(second_new / fix_second) + ADAM_EPS)
    master_new = master - LEARN_RATE * (step_dir + WEIGHT_DECAY * master)
    master_out[place] = master_new
    first_out[place] = first_new
    second_out[place] = second_new
    half_out[place] = to_half(master_new)


def update_kernel(head_cols, rates_ref, qkv_ref, rest_ref, cond_ref, time_ref, patch_ref, *refs):
    rates = (rates_ref[0], rates_ref[1], rates_ref[2])
    sets = [refs[which::5] for which in range(5)]
    everything = slice(None)
    pairs = head_cols // PAIR
    for pair in range(pairs):
        for kind in range(3):
            source = (pair * 3 + kind) * PAIR
            place = (kind * pairs + pair) * PAIR
            update_part(
                sets[0],
                everything,
                slice(place, place + PAIR),
                qkv_ref[:, source : source + PAIR].astype(jnp.float32),
                rates,
            )
    qkv_cols = 3 * head_cols
    hidden_cols = sets[0][0].shape[1] - qkv_cols
    for start in range(0, hidden_cols, 256):
        update_part(
            sets[0],
            everything,
            slice(qkv_cols + start, qkv_cols + start + 256),
            rest_ref[:, start : start + 256].astype(jnp.float32),
            rates,
        )
    for start in range(0, hidden_cols + head_cols, 256):
        source = 2 * hidden_cols if start == 0 else hidden_cols + start - head_cols
        gradient = rest_ref[:, source : source + 256].astype(jnp.float32).T
        update_part(sets[1], slice(start, start + 256), everything, gradient, rates)
    for start in range(0, cond_ref.shape[1], 256):
        columns = slice(start, start + 256)
        update_part(sets[2], everything, columns, cond_ref[:, columns], rates)
    for start in range(0, D, 256):
        columns = slice(start, start + 256)
        update_part(sets[3], everything, columns, time_ref[:, columns], rates)
    update_part(sets[4], everything, everything, patch_ref[...], rates)


def update_all(rates, gradients, masters, firsts, seconds, head_cols):
    operands = list(gradients) + list(masters) + list(firsts) + list(seconds)
    shapes = [master.shape for master in masters]
    in_vmem = pl.BlockSpec(memory_space=pltpu.VMEM)
    return pl.pallas_call(
        partial(update_kernel, head_cols),
        in_specs=[pl.BlockSpec(memory_space=pltpu.SMEM)] + [in_vmem] * len(operands),
        out_specs=[in_vmem] * 20,
        out_shape=[jax.ShapeDtypeStruct(shape, jnp.float32) for shape in shapes] * 3
        + [jax.ShapeDtypeStruct(shape, jnp.bfloat16) for shape in shapes],
        compiler_params=pltpu.CompilerParams(vmem_limit_bytes=60 << 20),
    )(rates, *operands)


def shards(
    latent,
    noise_draw,
    levels,
    context,
    step_count,
    w_in,
    w_outs,
    w_cond,
    w_time,
    w_patch,
    m_in,
    m_outs,
    m_cond,
    m_time,
    m_patch,
    v_in,
    v_outs,
    v_cond,
    v_time,
    v_patch,
):
    head_cols = D // lax.axis_size("tensor")
    pairs_block = head_cols // PAIR
    pairs_all = D // PAIR
    masters = (w_in, w_outs, w_cond, w_time, w_patch)
    clips, frames_here, patch_rows, width = latent.shape
    groups = clips * frames_here
    plane_index = lax.axis_index(PLANE)
    half_cond, half_time, half_patch = [to_half(m) for m in masters[2:]]
    hidden_cols = w_in.shape[1] - 3 * head_cols
    shard_qkv, shard_rest = pack_weights(w_in, w_outs, head_cols)

    w_qkv = gather_blocks(shard_qkv)
    level_rows = jnp.pad(
        levels.astype(jnp.float32), ((0, 8 - clips), (0, PAIR - frames_here))
    )
    time_places, patch_places, level_places = plane_gather([half_time, half_patch, level_rows])
    time_whole = time_places.reshape(-1, D)
    patch_whole = jnp.moveaxis(patch_places, 0, 2).reshape(2, PD, D)
    fields = swap_groups(jnp.stack([latent, noise_draw]))
    levels_all = level_places[:, :clips, :frames_here]
    blocks = lax.axis_size("tensor")
    w_first = time_whole[:TEMB]
    w_second = time_whole[TEMB:]
    w_embed = pad_lanes(patch_whole[0], 0)
    w_head = pad_lanes(patch_whole[1], 0)

    token_total = (TOKF * jnp.sum(FRAMES - context)).astype(jnp.float32)
    dp_size = lax.axis_size("dp")
    frame_size = lax.axis_size("frame")
    clip_ids = jnp.arange(dp_size * clips, dtype=jnp.int32).reshape(dp_size, 1, clips, 1)
    frame_ids = jnp.arange(FRAMES, dtype=jnp.int32).reshape(1, frame_size, 1, frames_here)
    clean_all = frame_ids < context[clip_ids]
    level_all = jnp.where(
        clean_all, 0.0, levels_all.reshape(dp_size, frame_size, clips, frames_here)
    )
    embed_low = to_half(frequency_table(level_all.reshape(-1)))
    hidden_time = product(embed_low, w_first)
    first_low = to_half(jax.nn.silu(hidden_time))
    cond_vec = product(first_low, w_second)
    cond_low = to_half(jax.nn.silu(cond_vec))
    frame_index = lax.axis_index("frame")
    tensor_index = lax.axis_index("tensor")
    cond_rows = half_cond.shape[0]
    cond_own = lax.dynamic_slice_in_dim(cond_low, plane_index * cond_rows, cond_rows, 1)
    mod_parts = product(cond_own, half_cond).reshape(dp_size * frame_size, groups, -1)
    def own_part(whole):
        part = lax.dynamic_index_in_dim(whole, tensor_index, 0, keepdims=False)
        return lax.dynamic_index_in_dim(part, frame_index, 0, keepdims=False)

    clean_frames = own_part(clean_all)
    alpha_coef, sigma_coef = noise_terms(own_part(level_all))
    alpha_field = alpha_coef[:, :, None, None]
    sigma_field = sigma_coef[:, :, None, None]
    clean_field = fields[0].astype(jnp.float32)
    noise_field = fields[1].astype(jnp.float32)
    noisy_field = alpha_field * clean_field + sigma_field * noise_field
    target = alpha_field * noise_field - sigma_field * clean_field
    patch_low = pad_lanes(to_half(patchify(noisy_field).reshape(clips, -1, PD)), 2)
    goal_rows = pad_lanes(patchify(target).reshape(clips, -1, PD), 2)
    coef = (1.0 - clean_frames.astype(jnp.float32)) / token_total
    coef_rows = jnp.broadcast_to(coef[:, :, None], (clips, frames_here, PAIR))


    mod_parts, patch_low, goal_rows, coef_rows = lax.optimization_barrier(
        (mod_parts, patch_low, goal_rows, coef_rows)
    )
    modulation = jnp.swapaxes(spread_mods(mod_parts), 0, 1)
    mods = modulation.reshape(clips, frames_here, -1)

    spread = spread_heads()
    each_clip = range(clips)
    opened = [
        open_layer(patch_low[clip], w_embed, mods[clip], w_qkv) for clip in each_clip
    ]
    rows_in = [parts[0] for parts in opened]
    flat_one = [parts[1] for parts in opened]
    kept = []
    mixed_pairs = []
    mixed_lows = []
    for clip in each_clip:
        qkv_send = opened[clip][2]
        if clip > 1:
            qkv_send = after(qkv_send, mixed_lows[clip - 2])
        qkv_heads = to_heads(qkv_send)
        if clip == 0:
            w_rest = gather_blocks(after(shard_rest, qkv_heads, *rows_in[1:]))
            cond_whole = lax.all_gather(after(half_cond, w_rest), PLANE, axis=0, tiled=True)
        else:
            qkv_heads = after(qkv_heads, mixed_lows[clip - 1])
        if spread:
            key_value, key_place = qkv_heads, 1
        else:
            key_value = lax.all_gather(qkv_heads[..., PAIR:], "frame", axis=1, tiled=True)
            key_place = 0
        exps, mixed_low, mixed, inverse = attend(qkv_heads, key_value, key_place)
        kept.append((exps, qkv_heads, key_value, key_place, mixed, inverse))
        mixed_lows.append(mixed_low)
    middles = []
    grad_heads = []
    for clip in each_clip:
        gates = mixed_lows[clip + 1 : clip + 2]
        if not gates and clip > 1:
            gates = [middles[clip - 2][5]]
        mixed_pairs.append(to_tokens(after(mixed_lows[clip], *gates)))
        middles.append(
            middle_layer(
                mixed_pairs[clip],
                rows_in[clip],
                mods[clip],
                goal_rows[clip],
                coef_rows[clip],
                w_head,
                w_rest,
                head_cols,
                hidden_cols,
            )
        )
    flat_two, act_low, grad_mlp, grad_hidden, grad_attn, grad_rows = [
        [parts[place] for parts in middles] for place in range(6)
    ]
    loss_part = sum(jnp.sum(parts[9]) for parts in middles)
    grad_head = sum(parts[8][:PD] for parts in middles)
    grad_heads = [to_heads(after(middles[0][6], middles[1 % clips][5]))]
    flat_two[-1] = after(flat_two[-1], *grad_heads)
    grad_rest = weight_grads(
        blocks,
        [(flat_two, grad_hidden), (grad_mlp, act_low), (grad_attn, mixed_pairs)],
    )
    scattered_rest = scatter_blocks(after(grad_rest, cond_whole))
    if clips > 1:
        sends = after(jnp.concatenate([parts[6] for parts in middles[1:]], axis=1), grad_rest)
        together = to_heads(sends).reshape(
            kept[0][5].shape[0], -1, clips - 1, sends.shape[1] // (clips - 1), PAIR
        )
        grad_heads += [
            together[:, :, clip].reshape(together.shape[0], -1, PAIR) for clip in range(clips - 1)
        ]
    grad_pairs = []
    for clip in each_clip:
        exps, qkv_heads, key_value, key_place, mixed, inverse = kept[clip]
        grad_now = after(grad_heads[clip], grad_rest)
        if clip > 1:
            grad_now = after(grad_now, grad_pairs[clip - 2])
        grads = attend_back(exps, qkv_heads, key_value, key_place, grad_now, mixed, inverse)
        if not spread:
            grads = [grads[0]] + [
                lax.psum_scatter(grad, "frame", scatter_dimension=1, tiled=True)
                for grad in grads[1:]
            ]
        grad_units = grads[0] if len(grads) == 1 else jnp.concatenate(grads, axis=-1)
        grad_pairs.append(to_tokens(grad_units))
    closed = []
    for clip in each_clip:
        if clip == clips - 1:
            grad_pairs[clip] = after(
                grad_pairs[clip], scattered_rest, *[parts[0] for parts in closed]
            )
            grad_wqkv = weight_grads(blocks, [(flat_one, grad_pairs)])
            scattered_qkv = scatter_stages(grad_wqkv)
            grad_pairs[clip] = after(grad_pairs[clip], grad_wqkv)
        closed.append(
            close_layer(
                grad_pairs[clip], rows_in[clip], grad_rows[clip], mods[clip], patch_low[clip], w_qkv
            )
        )
    grad_embed = sum(parts[1][:PD] for parts in closed)
    patch_cols = half_patch.shape[2]
    patch_parts = jnp.swapaxes(
        jnp.concatenate([grad_embed, grad_head], axis=0).reshape(2 * PD, -1, patch_cols), 0, 1
    )
    grad_mod = jnp.stack(
        [jnp.concatenate([closed[clip][0], middles[clip][7]], axis=0) for clip in each_clip]
    )
    mod_parts = jnp.transpose(
        grad_mod.reshape(clips, dp_size, -1, frames_here, D), (1, 0, 3, 2, 4)
    ).reshape(dp_size, groups, -1)
    mod_all, cond_places, patch_block = cond_sums(to_half(mod_parts), patch_parts, cond_whole)
    mod_all = mod_all.reshape(-1, mod_all.shape[-1])
    grad_cond_all = cond_places.reshape(-1, D).astype(jnp.float32)
    final_patch = patch_block.reshape(2, PD, patch_cols)
    final_cond = rows_product(cond_own, mod_all)
    unused, silu_cond = jax.vjp(jax.nn.silu, cond_vec)
    grad_cond_low = to_half(silu_cond(grad_cond_all)[0])
    grad_second = rows_product(first_low, grad_cond_low)
    grad_first_act = cols_product(grad_cond_low, w_second)
    unused, silu_first = jax.vjp(jax.nn.silu, hidden_time)
    grad_hidden_time = to_half(silu_first(grad_first_act)[0])
    grad_first = rows_product(embed_low, grad_hidden_time)
    time_rows = half_time.shape[0]
    final_time = lax.dynamic_slice_in_dim(
        jnp.concatenate([grad_first, grad_second], axis=0), plane_index * time_rows, time_rows, 0
    )
    def square_sum(gradient):
        wide = gradient.astype(jnp.float32)
        return jnp.sum(wide * wide)

    split_square = sum(square_sum(part) for part in (scattered_qkv, scattered_rest, final_cond))
    shared_square = (square_sum(final_time) + square_sum(final_patch)) / blocks
    totals = total_over_all(loss_part, split_square + shared_square)
    loss_value = totals[0]
    grad_norm = jnp.sqrt(totals[1])
    factor = jnp.minimum(1.0, MAX_NORM / (grad_norm + 1e-06))
    steps_done = step_count[0].astype(jnp.float32)
    fix_first = 1.0 - BETA_FIRST**steps_done
    fix_second = 1.0 - BETA_SECOND**steps_done
    results = update_all(
        jnp.stack([factor, fix_first, fix_second]),
        (scattered_qkv, scattered_rest, final_cond, final_time, final_patch),
        masters,
        (m_in, m_outs, m_cond, m_time, m_patch),
        (v_in, v_outs, v_cond, v_time, v_patch),
        head_cols,
    )
    return (loss_value, grad_norm, *results)


def solution(mesh):
    placed = (
        P("dp", "frame", "tensor", None),
        P("dp", "frame", "tensor", None),
        P("dp", "frame"),
        P(),
        P(),
        P(("dp", "frame"), "tensor"),
        P("tensor", ("dp", "frame")),
        P(("dp", "frame"), "tensor"),
        P(("dp", "frame"), None),
        P(None, None, ("dp", "frame")),
        P(("dp", "frame"), "tensor"),
        P("tensor", ("dp", "frame")),
        P(("dp", "frame"), "tensor"),
        P(("dp", "frame"), None),
        P(None, None, ("dp", "frame")),
        P(("dp", "frame"), "tensor"),
        P("tensor", ("dp", "frame")),
        P(("dp", "frame"), "tensor"),
        P(("dp", "frame"), None),
        P(None, None, ("dp", "frame")),
    )
    return jax.shard_map(
        shards,
        mesh=mesh,
        in_specs=placed,
        out_specs=(
            P(),
            P(),
            P(("dp", "frame"), "tensor"),
            P("tensor", ("dp", "frame")),
            P(("dp", "frame"), "tensor"),
            P(("dp", "frame"), None),
            P(None, None, ("dp", "frame")),
            P(("dp", "frame"), "tensor"),
            P("tensor", ("dp", "frame")),
            P(("dp", "frame"), "tensor"),
            P(("dp", "frame"), None),
            P(None, None, ("dp", "frame")),
            P(("dp", "frame"), "tensor"),
            P("tensor", ("dp", "frame")),
            P(("dp", "frame"), "tensor"),
            P(("dp", "frame"), None),
            P(None, None, ("dp", "frame")),
            P(("dp", "frame"), "tensor"),
            P("tensor", ("dp", "frame")),
            P(("dp", "frame"), "tensor"),
            P(("dp", "frame"), None),
            P(None, None, ("dp", "frame")),
        ),
        check_vma=False,
    )
```

```python
from functools import partial
import math

import jax
import jax.numpy as jnp
from jax import lax
from jax.experimental import pallas as pl
from jax.experimental.pallas import tpu as pltpu
from jax.sharding import PartitionSpec as P

D = 1024
HD = 64
TEMB = 256
CHANNELS = 4
PATCH = 2
PD = 16
TOKF = 256
FRAMES = 16
NLEV = 1000
PAIR = 2 * HD
PLANE = ("dp", "frame")
EVERY = ("tensor", "dp", "frame")
SCORE_SCALE = HD ** (-0.5) * math.log2(math.e)
TOTAL_LOW = 2.0**-40
TOTAL_HIGH = 2.0**70


EPS_NORM = 1e-06
MAX_NORM = 0.1
LEARN_RATE = 0.08
WEIGHT_DECAY = 0.1
BETA_FIRST = 0.5
BETA_SECOND = 0.5
ADAM_EPS = 1e-08


def to_half(array_in):
    return array_in.astype(jnp.bfloat16)


def product(left_mat, right_mat):
    return jnp.dot(left_mat, right_mat, preferred_element_type=jnp.float32)


def rows_product(left_mat, right_mat):
    return lax.dot_general(
        left_mat, right_mat, (((0,), (0,)), ((), ())), preferred_element_type=jnp.float32
    )


def cols_product(left_mat, right_mat):
    return lax.dot_general(
        left_mat, right_mat, (((1,), (1,)), ((), ())), preferred_element_type=jnp.float32
    )


def frequency_table(level_values):
    half_width = TEMB // 2
    rate_table = jnp.exp(
        -math.log(10000.0) * jnp.arange(half_width, dtype=jnp.float32) / half_width
    )
    angles = level_values[..., None] * rate_table
    return jnp.concatenate([jnp.cos(angles), jnp.sin(angles)], axis=-1)


def noise_terms(level_values):
    angles = level_values * (0.5 * math.pi / NLEV)
    return (jnp.cos(angles), jnp.sin(angles))


def patchify(field_in):
    lead_shape = field_in.shape[:-2]
    rows_here = field_in.shape[-2]
    width_cells = field_in.shape[-1] // CHANNELS
    lead_rank = len(lead_shape)
    blocks_view = field_in.reshape(
        lead_shape + (rows_here // PATCH, PATCH, width_cells // PATCH, PATCH, CHANNELS)
    )
    order_axes = tuple(range(lead_rank)) + (
        lead_rank,
        lead_rank + 2,
        lead_rank + 1,
        lead_rank + 3,
        lead_rank + 4,
    )
    return jnp.transpose(blocks_view, order_axes).reshape(
        lead_shape + (rows_here // PATCH * (width_cells // PATCH), PATCH * PATCH * CHANNELS)
    )


def contract(left_mat, right_mat, left_dim, right_dim):
    return lax.dot_general(
        left_mat,
        right_mat,
        (((left_dim,), (right_dim,)), ((), ())),
        preferred_element_type=jnp.float32,
    )


def head_lanes(head):
    return lax.broadcasted_iota(jnp.int32, (1, PAIR), 1) // HD == head


def attend_kernel(chunk, query_ref, key_ref, value_ref, exps_ref, low_ref, mixed_ref, inverse_ref):
    key_total = key_ref.shape[1]
    block_rows = query_ref.shape[1]
    query_pair = query_ref[0]
    mixed_parts = []
    inverse_parts = []
    for head in range(2):
        lanes = head_lanes(head)
        query_head = jnp.where(lanes, query_pair, jnp.zeros_like(query_pair))

        def scores_of(rows):
            return contract(key_ref[0, rows, :], query_head, 1, 1) * SCORE_SCALE

        def add_chunk(rows, scores, total):
            exps = jnp.exp2(scores).astype(jnp.bfloat16)
            exps_ref[0, head, :, rows] = exps.T
            values = value_ref[0, rows, :]
            values = jnp.where(lanes, values, jnp.ones_like(values))
            return total + contract(values, exps, 0, 0)

        zeros = jnp.zeros((PAIR, block_rows), jnp.float32)
        total = zeros
        for start in range(0, key_total, chunk):
            rows = slice(start, start + chunk)
            total = add_chunk(rows, scores_of(rows), total)
        sum_rows = total[(1 - head) * HD : (1 - head) * HD + 8]
        outside = jnp.max(
            jnp.where((sum_rows > TOTAL_LOW) & (sum_rows < TOTAL_HIGH), 0.0, 1.0)
        )

        def shifted(unused):
            def chunk_rows(step):
                return pl.ds(pl.multiple_of(step * chunk, chunk), chunk)

            def highest(step, top):
                return jnp.maximum(
                    top, jnp.max(scores_of(chunk_rows(step)), axis=0, keepdims=True)
                )

            top = lax.fori_loop(
                0, key_total // chunk, highest, jnp.full((1, block_rows), -jnp.inf, jnp.float32)
            )

            def one_chunk(step, total):
                rows = chunk_rows(step)
                return add_chunk(rows, scores_of(rows) - top, total)

            return lax.fori_loop(0, key_total // chunk, one_chunk, zeros)

        total = lax.cond(outside > 0.0, shifted, lambda kept: kept, total)
        inverse = 1.0 / total[(1 - head) * HD : (2 - head) * HD]
        mixed_parts.append(total[head * HD : (head + 1) * HD] * inverse)
        inverse_parts.append(inverse)
    mixed = jnp.concatenate(mixed_parts, axis=0).T
    mixed_ref[0] = mixed
    low_ref[0] = mixed.astype(jnp.bfloat16)
    inverse_ref[0] = jnp.concatenate(inverse_parts, axis=0).T


def attend(query_in, key_value, key_place):
    units, query_total = query_in.shape[:2]
    key_total = key_value.shape[1]
    block_rows = min(1024, query_total)
    chunk = min(1024, key_total)

    def query_map(unit, step):
        return (unit, step, 0)

    query_spec = pl.BlockSpec((1, block_rows, PAIR), query_map)
    shape_rows = (units, query_total, PAIR)
    products = 4 * units * query_total * key_total * PAIR
    return pl.pallas_call(
        partial(attend_kernel, chunk),
        grid=(units, query_total // block_rows),
        in_specs=[
            query_spec,
            pl.BlockSpec((1, key_total, PAIR), lambda unit, step: (unit, 0, key_place)),
            pl.BlockSpec((1, key_total, PAIR), lambda unit, step: (unit, 0, key_place + 1)),
        ],
        out_specs=[
            pl.BlockSpec((1, 2, block_rows, key_total), lambda unit, step: (unit, 0, step, 0)),
            query_spec,
            query_spec,
            query_spec,
        ],
        out_shape=[
            jax.ShapeDtypeStruct((units, 2, query_total, key_total), jnp.bfloat16),
            jax.ShapeDtypeStruct(shape_rows, jnp.bfloat16),
            jax.ShapeDtypeStruct(shape_rows, jnp.float32),
            jax.ShapeDtypeStruct(shape_rows, jnp.float32),
        ],
        cost_estimate=pl.CostEstimate(
            flops=4 * products,
            bytes_accessed=4 * units * query_total * key_total,
            transcendentals=2 * units * query_total * key_total,
        ),
        compiler_params=pltpu.CompilerParams(vmem_limit_bytes=62 << 20),
    )(query_in, key_value, key_value)


def attend_back_kernel(
    chunk,
    exps_ref,
    query_ref,
    key_ref,
    value_ref,
    grad_ref,
    mixed_ref,
    inverse_ref,
    *grads_and_sums,
):
    *grad_refs, key_sums, value_sums = grads_and_sums
    step = pl.program_id(1)
    head = pl.program_id(2)
    key_total = key_ref.shape[1]
    block_rows = query_ref.shape[1]
    lane = lax.broadcasted_iota(jnp.int32, (1, PAIR), 1)
    lanes = head_lanes(head)
    grad_low = jnp.where(lanes, grad_ref[0].astype(jnp.float32) * inverse_ref[0], 0.0).astype(
        jnp.bfloat16
    )
    row_terms = jnp.sum(grad_low.astype(jnp.float32) * mixed_ref[0], axis=1, keepdims=True)
    term_high = row_terms.astype(jnp.bfloat16).astype(jnp.float32)
    term_rest = row_terms - term_high
    term_lanes = jnp.where(lane == 0, -term_high, jnp.where(lane == 1, -term_rest, 0.0))
    grad_wide = jnp.concatenate([grad_low, term_lanes.astype(jnp.bfloat16)], axis=1)
    query_pair = query_ref[0]
    query_columns = jnp.where(lanes, query_pair, jnp.zeros_like(query_pair)).T
    grad_columns = grad_low.T
    term_ones = jnp.broadcast_to(jnp.where(lane < 2, 1.0, 0.0).astype(jnp.bfloat16), (chunk, PAIR))

    @pl.when((step == 0) & (head == 0))
    def start_sums():
        key_sums[...] = jnp.zeros_like(key_sums)
        value_sums[...] = jnp.zeros_like(value_sums)

    grad_query = jnp.zeros((block_rows, PAIR), jnp.float32)
    for start in range(0, key_total, chunk):
        rows = slice(start, start + chunk)
        values_wide = jnp.concatenate([value_ref[0, rows, :], term_ones], axis=1)
        grad_probs = contract(grad_wide, values_wide, 1, 1).astype(jnp.bfloat16)
        exps = exps_ref[0, 0, :, rows]
        grad_scores = exps * grad_probs
        value_sums[:, rows] += contract(grad_columns, exps, 1, 0)
        key_sums[:, rows] += contract(query_columns, grad_scores, 1, 0)
        keys = key_ref[0, rows, :]
        keys = jnp.where(lanes, keys, jnp.zeros_like(keys))
        grad_query = grad_query + contract(grad_scores, keys, 1, 0)
    grad_query_low = (grad_query * HD ** (-0.5)).astype(jnp.bfloat16)

    fused = len(grad_refs) == 1
    first_row = pl.multiple_of(step * block_rows, block_rows) if fused else 0
    query_place = (0, pl.ds(first_row, block_rows), slice(0, PAIR))

    @pl.when(head == 0)
    def first_head():
        grad_refs[0][query_place] = grad_query_low

    @pl.when(head == 1)
    def second_head():
        grad_refs[0][query_place] = jnp.where(lanes, grad_query_low, grad_refs[0][query_place])

    @pl.when((step == pl.num_programs(1) - 1) & (head == 1))
    def write_sums():
        grad_key = (key_sums[...].T * HD ** (-0.5)).astype(jnp.bfloat16)
        grad_value = value_sums[...].T.astype(jnp.bfloat16)
        if fused:
            grad_refs[0][0, :, PAIR : 2 * PAIR] = grad_key
            grad_refs[0][0, :, 2 * PAIR :] = grad_value
        else:
            grad_refs[1][0] = grad_key
            grad_refs[2][0] = grad_value


def attend_back(exps, query_in, key_value, key_place, grad_mixed, mixed, inverse):
    units, query_total = mixed.shape[:2]
    key_total = key_value.shape[1]
    block_rows = min(1024, query_total)
    chunk = min(1024, key_total)
    query_spec = pl.BlockSpec((1, block_rows, PAIR), lambda unit, step, head: (unit, step, 0))
    whole_spec = pl.BlockSpec((1, key_total, PAIR), lambda unit, step, head: (unit, 0, 0))
    if query_total == key_total:
        out_sizes = [(key_total, 3 * PAIR)]
        out_specs = [
            pl.BlockSpec((1, key_total, 3 * PAIR), lambda unit, step, head: (unit, 0, 0))
        ]
    else:
        out_sizes = [(query_total, PAIR), (key_total, PAIR), (key_total, PAIR)]
        out_specs = [query_spec, whole_spec, whole_spec]
    products = 8 * units * query_total * key_total * PAIR
    return pl.pallas_call(
        partial(attend_back_kernel, chunk),
        grid=(units, query_total // block_rows, 2),
        in_specs=[
            pl.BlockSpec(
                (1, 1, block_rows, key_total), lambda unit, step, head: (unit, head, step, 0)
            ),
            query_spec,
            pl.BlockSpec((1, key_total, PAIR), lambda unit, step, head: (unit, 0, key_place)),
            pl.BlockSpec((1, key_total, PAIR), lambda unit, step, head: (unit, 0, key_place + 1)),
            query_spec,
            query_spec,
            query_spec,
        ],
        out_specs=out_specs,
        out_shape=[
            jax.ShapeDtypeStruct((units, rows, columns), jnp.bfloat16)
            for rows, columns in out_sizes
        ],
        scratch_shapes=[pltpu.VMEM((PAIR, key_total), jnp.float32)] * 2,
        cost_estimate=pl.CostEstimate(
            flops=4 * products,
            bytes_accessed=4 * units * query_total * key_total,
            transcendentals=0,
        ),
        compiler_params=pltpu.CompilerParams(vmem_limit_bytes=62 << 20),
    )(exps, query_in, key_value, key_value, grad_mixed, mixed, inverse)


def normalize(rows_in):
    centre = rows_in - jnp.mean(rows_in, axis=-1, keepdims=True)
    spread = jnp.mean(centre * centre, axis=-1, keepdims=True)
    inverse = lax.rsqrt(spread + EPS_NORM)
    return (centre * inverse, inverse)


def normalize_back(normed, inverse, scale_row, grad_out):
    grad_shift = jnp.sum(grad_out, axis=0, keepdims=True)
    grad_scale = jnp.sum(grad_out * normed, axis=0, keepdims=True)
    grad_normed = grad_out * (1.0 + scale_row)
    grad_rows = inverse * (
        grad_normed
        - jnp.mean(grad_normed, axis=-1, keepdims=True)
        - normed * jnp.mean(grad_normed * normed, axis=-1, keepdims=True)
    )
    return (grad_rows, grad_shift, grad_scale)


def mod_row(mods_ref, place, group):
    return mods_ref[pl.ds(group, 1), place * D : (place + 1) * D]


def group_rows(group, rows_group):
    return pl.ds(pl.multiple_of(group * rows_group, rows_group), rows_group)


def open_kernel(patch_ref, embed_ref, mods_ref, weight_ref, rows_ref, normed_ref, send_ref):
    groups = mods_ref.shape[0]
    rows_group = rows_ref.shape[0] // groups

    @pl.when(pl.program_id(0) == 0)
    def embed_rows():
        def one_group(group, unused):
            rows = group_rows(group, rows_group)
            residual = product(patch_ref[rows, :], embed_ref[...])
            rows_ref[rows, :] = residual
            normed, unused_inverse = normalize(residual)
            normed_ref[rows, :] = to_half(
                normed * (1.0 + mod_row(mods_ref, 1, group)) + mod_row(mods_ref, 0, group)
            )
            return unused

        lax.fori_loop(0, groups, one_group, 0, unroll=True)

    columns = send_ref.shape[2]
    for place in range(send_ref.shape[0]):
        send_ref[place] = to_half(
            product(
                normed_ref[...], weight_ref[0, :, place * columns : (place + 1) * columns]
            )
        )


def open_layer(patch_rows, w_embed, mods, w_qkv):
    tokens = patch_rows.shape[0]
    blocks, unused, columns = w_qkv.shape
    per_block = columns // (3 * PAIR)
    whole = pl.BlockSpec((tokens, D), lambda step: (0, 0))
    return pl.pallas_call(
        open_kernel,
        grid=(blocks,),
        in_specs=[
            pl.BlockSpec(patch_rows.shape, lambda step: (0, 0)),
            pl.BlockSpec(w_embed.shape, lambda step: (0, 0)),
            pl.BlockSpec(mods.shape, lambda step: (0, 0)),
            pl.BlockSpec((1, D, columns), lambda step: (step, 0, 0)),
        ],
        out_specs=[
            whole,
            whole,
            pl.BlockSpec((per_block, tokens, 3 * PAIR), lambda step: (step, 0, 0)),
        ],
        out_shape=[
            jax.ShapeDtypeStruct((tokens, D), jnp.float32),
            jax.ShapeDtypeStruct((tokens, D), jnp.bfloat16),
            jax.ShapeDtypeStruct((blocks * per_block, tokens, 3 * PAIR), jnp.bfloat16),
        ],
        cost_estimate=pl.CostEstimate(
            flops=2 * tokens * D * blocks * columns,
            bytes_accessed=2 * blocks * D * columns + 12 * tokens * D,
            transcendentals=0,
        ),
        compiler_params=pltpu.CompilerParams(vmem_limit_bytes=60 << 20),
    )(patch_rows, w_embed, mods, w_qkv)


GELU_RATE = math.sqrt(2.0 / math.pi)
GELU_CUBE = 0.044715


def middle_kernel(
    head_cols,
    hidden_cols,
    mixed_ref,
    rows_ref,
    mods_ref,
    goal_ref,
    coef_ref,
    head_ref,
    weights_hbm,
    normed_hbm,
    act_hbm,
    grad_mlp_hbm,
    grad_hidden_hbm,
    grad_attn_hbm,
    grad_rows_hbm,
    send_ref,
    grad_mods_ref,
    grad_head_ref,
    loss_ref,
    weights,
    normed_low,
    act_low,
    grad_mlp_low,
    grad_hidden_low,
    grad_attn_low,
    grad_rows,
    attn_sum,
    middle,
    mlp_sum,
    slopes,
    out_sems,
    wide_sems,
    act_sems,
    hidden_sems,
    row_sems,
):
    blocks = weights.shape[0]
    groups = mods_ref.shape[0]
    rows_group = rows_ref.shape[0] // groups
    per_block = head_cols // PAIR
    wide = 2 * hidden_cols
    up_columns = slice(0, hidden_cols)
    down_columns = slice(hidden_cols, wide)
    out_columns = slice(wide, wide + head_cols)

    def fetch_out(block):
        return pltpu.make_async_copy(
            weights_hbm.at[block, :, out_columns],
            weights.at[block, :, out_columns],
            out_sems.at[block],
        )

    def fetch_wide(block):
        return pltpu.make_async_copy(
            weights_hbm.at[block, :, 0:wide], weights.at[block, :, 0:wide], wide_sems.at[block]
        )

    def put_act(block):
        columns = pl.ds(pl.multiple_of(block * hidden_cols, hidden_cols), hidden_cols)
        return pltpu.make_async_copy(
            act_low.at[block], act_hbm.at[:, columns], act_sems.at[block]
        )

    def put_hidden(block):
        columns = pl.ds(pl.multiple_of(block * hidden_cols, hidden_cols), hidden_cols)
        return pltpu.make_async_copy(
            grad_hidden_low.at[block], grad_hidden_hbm.at[:, columns], hidden_sems.at[block]
        )

    put_normed = pltpu.make_async_copy(normed_low, normed_hbm, row_sems.at[0])
    put_grad_mlp = pltpu.make_async_copy(grad_mlp_low, grad_mlp_hbm, row_sems.at[1])
    put_grad_attn = pltpu.make_async_copy(grad_attn_low, grad_attn_hbm, row_sems.at[2])
    put_grad_rows = pltpu.make_async_copy(grad_rows, grad_rows_hbm, row_sems.at[3])

    def each_block(one_block):
        def step(block, unused):
            one_block(block)
            return unused

        lax.fori_loop(0, blocks, step, 0)

    def each_group(one_group):
        def step(group, unused):
            one_group(group, group_rows(group, rows_group))
            return unused

        lax.fori_loop(0, groups, step, 0, unroll=True)

    each_block(lambda block: fetch_out(block).start())
    each_block(lambda block: fetch_wide(block).start())
    attn_sum[...] = jnp.zeros_like(attn_sum)
    mlp_sum[...] = jnp.zeros_like(mlp_sum)

    def attn_out(block):
        fetch_out(block).wait()
        mixed = jnp.concatenate(
            [mixed_ref[block * per_block + place] for place in range(per_block)], axis=1
        )
        attn_sum[...] += contract(mixed, weights[block, :, out_columns], 1, 1)

    each_block(attn_out)

    def to_middle(group, rows):
        residual = rows_ref[rows, :] + mod_row(mods_ref, 2, group) * attn_sum[rows, :]
        middle[rows, :] = residual
        normed, unused_inverse = normalize(residual)
        normed_low[rows, :] = to_half(
            normed * (1.0 + mod_row(mods_ref, 4, group)) + mod_row(mods_ref, 3, group)
        )

    each_group(to_middle)
    put_normed.start()

    def forward_mlp(block):
        fetch_wide(block).wait()
        hidden = product(normed_low[...], weights[block, :, up_columns])
        square = hidden * hidden
        bend = jnp.tanh(GELU_RATE * hidden * (1.0 + GELU_CUBE * square))
        half_open = 0.5 * (1.0 + bend)
        act = to_half(hidden * half_open)
        act_low[block] = act
        slope = half_open + 0.5 * hidden * (1.0 - bend * bend) * (
            GELU_RATE * (1.0 + 3.0 * GELU_CUBE * square)
        )
        slopes[block] = to_half(slope)
        put_act(block).start()
        mlp_sum[...] += contract(act, weights[block, :, down_columns], 1, 1)

    each_block(forward_mlp)
    grad_head_ref[...] = jnp.zeros_like(grad_head_ref)
    loss_ref[...] = jnp.zeros_like(loss_ref)

    def turn(group, rows):
        mlp_out = mlp_sum[rows, :]
        gate = mod_row(mods_ref, 5, group)
        normed, inverse = normalize(middle[rows, :] + gate * mlp_out)
        scale_row = mod_row(mods_ref, 7, group)
        final_low = to_half(normed * (1.0 + scale_row) + mod_row(mods_ref, 6, group))
        error_rows = contract(final_low, head_ref[...], 1, 1) - goal_ref[rows, :]
        weighted = coef_ref[pl.ds(group, 1), :] * error_rows
        loss_ref[pl.ds(0, 1), :] += jnp.sum(weighted * error_rows, axis=0, keepdims=True)
        grad_pred = to_half(2.0 * weighted)
        grad_head_ref[...] += contract(grad_pred, final_low, 0, 0)
        grad_final = product(grad_pred, head_ref[...])
        grad_residual, grad_six, grad_seven = normalize_back(
            normed, inverse, scale_row, grad_final
        )
        grad_mods_ref[4, pl.ds(group, 1), :] = grad_six
        grad_mods_ref[5, pl.ds(group, 1), :] = grad_seven
        grad_mods_ref[3, pl.ds(group, 1), :] = jnp.sum(
            mlp_out * grad_residual, axis=0, keepdims=True
        )
        grad_rows[rows, :] = grad_residual
        grad_mlp_low[rows, :] = to_half(gate * grad_residual)

    each_group(turn)
    put_grad_mlp.start()
    mlp_sum[...] = jnp.zeros_like(mlp_sum)

    def backward_mlp(block):
        grad_act = product(grad_mlp_low[...], weights[block, :, down_columns])
        grad_hidden = to_half(grad_act * slopes[block].astype(jnp.float32))
        grad_hidden_low[block] = grad_hidden
        put_hidden(block).start()
        mlp_sum[...] += contract(grad_hidden, weights[block, :, up_columns], 1, 1)

    each_block(backward_mlp)

    def from_middle(group, rows):
        normed, inverse = normalize(middle[rows, :])
        grad_branch, grad_three, grad_four = normalize_back(
            normed, inverse, mod_row(mods_ref, 4, group), mlp_sum[rows, :]
        )
        grad_residual = grad_rows[rows, :] + grad_branch
        grad_mods_ref[1, pl.ds(group, 1), :] = grad_three
        grad_mods_ref[2, pl.ds(group, 1), :] = grad_four
        grad_mods_ref[0, pl.ds(group, 1), :] = jnp.sum(
            attn_sum[rows, :] * grad_residual, axis=0, keepdims=True
        )
        grad_rows[rows, :] = grad_residual
        grad_attn_low[rows, :] = to_half(mod_row(mods_ref, 2, group) * grad_residual)

    each_group(from_middle)
    put_grad_rows.start()
    put_grad_attn.start()

    def to_send(block):
        grad_mixed = to_half(product(grad_attn_low[...], weights[block, :, out_columns]))
        for place in range(per_block):
            send_ref[block * per_block + place] = grad_mixed[
                :, place * PAIR : (place + 1) * PAIR
            ]

    each_block(to_send)
    put_normed.wait()
    put_grad_mlp.wait()
    put_grad_rows.wait()
    put_grad_attn.wait()
    each_block(lambda block: put_act(block).wait())
    each_block(lambda block: put_hidden(block).wait())


def middle_layer(mixed_pairs, rows_in, mods, goal, coef, w_head, weights, head_cols, hidden_cols):
    blocks = weights.shape[0]
    tokens = rows_in.shape[0]
    groups = mods.shape[0]
    in_vmem = pl.BlockSpec(memory_space=pltpu.VMEM)
    in_hbm = pl.BlockSpec(memory_space=pl.ANY)
    rows_low = pltpu.VMEM((tokens, D), jnp.bfloat16)
    rows_full = pltpu.VMEM((tokens, D), jnp.float32)
    wide_low = pltpu.VMEM((blocks, tokens, hidden_cols), jnp.bfloat16)
    block_sems = pltpu.SemaphoreType.DMA((blocks,))
    return pl.pallas_call(
        partial(middle_kernel, head_cols, hidden_cols),
        in_specs=[in_vmem] * 6 + [in_hbm],
        out_specs=[in_hbm] * 6 + [in_vmem] * 4,
        out_shape=[
            jax.ShapeDtypeStruct((tokens, D), jnp.bfloat16),
            jax.ShapeDtypeStruct((tokens, blocks * hidden_cols), jnp.bfloat16),
            jax.ShapeDtypeStruct((tokens, D), jnp.bfloat16),
            jax.ShapeDtypeStruct((tokens, blocks * hidden_cols), jnp.bfloat16),
            jax.ShapeDtypeStruct((tokens, D), jnp.bfloat16),
            jax.ShapeDtypeStruct((tokens, D), jnp.float32),
            jax.ShapeDtypeStruct(mixed_pairs.shape, jnp.bfloat16),
            jax.ShapeDtypeStruct((6, groups, D), jnp.float32),
            jax.ShapeDtypeStruct(w_head.shape, jnp.float32),
            jax.ShapeDtypeStruct((8, PAIR), jnp.float32),
        ],
        scratch_shapes=[
            pltpu.VMEM(weights.shape, jnp.bfloat16),
            rows_low,
            wide_low,
            rows_low,
            wide_low,
            rows_low,
            rows_full,
            rows_full,
            rows_full,
            rows_full,
            wide_low,
            block_sems,
            block_sems,
            block_sems,
            block_sems,
            pltpu.SemaphoreType.DMA((4,)),
        ],
        cost_estimate=pl.CostEstimate(
            flops=4 * tokens * D * blocks * (2 * hidden_cols + head_cols),
            bytes_accessed=2 * weights.size + 30 * tokens * D,
            transcendentals=tokens * blocks * hidden_cols,
        ),
        compiler_params=pltpu.CompilerParams(vmem_limit_bytes=62 << 20),
    )(mixed_pairs, rows_in, mods, goal, coef, w_head, weights)


def close_kernel(
    blocks,
    grad_ref,
    rows_ref,
    grad_rows_ref,
    mods_ref,
    patch_ref,
    weight_ref,
    grad_mods_ref,
    grad_embed_ref,
    total,
):
    step = pl.program_id(0)
    groups = mods_ref.shape[0]
    rows_group = rows_ref.shape[0] // groups
    columns = grad_ref.shape[2]
    part = jnp.zeros(total.shape, jnp.float32)
    for place in range(grad_ref.shape[0]):
        part = part + contract(
            grad_ref[place], weight_ref[0, :, place * columns : (place + 1) * columns], 1, 1
        )

    @pl.when(step == 0)
    def first():
        total[...] = part

    @pl.when(step > 0)
    def later():
        total[...] += part

    @pl.when(step == blocks - 1)
    def finish():
        grad_embed_ref[...] = jnp.zeros_like(grad_embed_ref)

        def one_group(group, unused):
            rows = group_rows(group, rows_group)
            normed, inverse = normalize(rows_ref[rows, :])
            grad_branch, grad_zero, grad_one = normalize_back(
                normed, inverse, mod_row(mods_ref, 1, group), total[rows, :]
            )
            grad_mods_ref[0, pl.ds(group, 1), :] = grad_zero
            grad_mods_ref[1, pl.ds(group, 1), :] = grad_one
            grad_low = to_half(grad_rows_ref[rows, :] + grad_branch)
            grad_embed_ref[...] += contract(patch_ref[rows, :], grad_low, 0, 0)
            return unused

        lax.fori_loop(0, groups, one_group, 0, unroll=True)


def close_layer(grad_pairs, rows_in, grad_rows, mods, patch_rows, w_qkv):
    tokens = rows_in.shape[0]
    groups = mods.shape[0]
    blocks, unused, columns = w_qkv.shape
    per_block = columns // (3 * PAIR)

    def whole(shape):
        return pl.BlockSpec(shape, lambda step: (0,) * len(shape))

    return pl.pallas_call(
        partial(close_kernel, blocks),
        grid=(blocks,),
        in_specs=[
            pl.BlockSpec((per_block, tokens, 3 * PAIR), lambda step: (step, 0, 0)),
            whole(rows_in.shape),
            whole(grad_rows.shape),
            whole(mods.shape),
            whole(patch_rows.shape),
            pl.BlockSpec((1, D, columns), lambda step: (step, 0, 0)),
        ],
        out_specs=[whole((2, groups, D)), whole((PAIR, D))],
        out_shape=[
            jax.ShapeDtypeStruct((2, groups, D), jnp.float32),
            jax.ShapeDtypeStruct((PAIR, D), jnp.float32),
        ],
        scratch_shapes=[pltpu.VMEM((tokens, D), jnp.float32)],
        cost_estimate=pl.CostEstimate(
            flops=2 * tokens * D * blocks * columns,
            bytes_accessed=2 * blocks * D * columns + 16 * tokens * D,
            transcendentals=0,
        ),
        compiler_params=pltpu.CompilerParams(vmem_limit_bytes=60 << 20),
    )(grad_pairs, rows_in, grad_rows, mods, patch_rows, w_qkv)


def weight_kernel(clips, kinds, *refs):
    out = refs[-1]
    column = 0
    for kind in range(kinds):
        lefts = refs[2 * clips * kind : 2 * clips * kind + clips]
        rights = refs[2 * clips * kind + clips : 2 * clips * (kind + 1)]
        paired = len(rights[0].shape) == 3
        pieces = rights[0].shape[0] if paired else rights[0].shape[1] // 512
        width = rights[0].shape[2] if paired else 512
        for piece in range(pieces):
            total = None
            for left, right in zip(lefts, rights):
                block = right[piece] if paired else right[:, piece * width : (piece + 1) * width]
                part = contract(left[...], block, 0, 0)
                total = part if total is None else total + part
            out[0, :, column : column + width] = to_half(total)
            column += width


def weight_grads(blocks, terms):
    clips = len(terms[0][0])
    operands = []
    specs = []
    columns_all = 0
    flops = 0
    for lefts, rights in terms:
        for left in lefts:
            operands.append(left)
            specs.append(pl.BlockSpec(left.shape, lambda step: (0, 0)))
        for right in rights:
            operands.append(right)
            if right.ndim == 3:
                per_block = right.shape[0] // blocks
                specs.append(
                    pl.BlockSpec((per_block,) + right.shape[1:], lambda step: (step, 0, 0))
                )
                columns = per_block * right.shape[2]
            else:
                columns = right.shape[1] // blocks
                specs.append(pl.BlockSpec((right.shape[0], columns), lambda step: (0, step)))
            flops += 2 * right.size * D
        columns_all += columns
    return pl.pallas_call(
        partial(weight_kernel, clips, len(terms)),
        grid=(blocks,),
        in_specs=specs,
        out_specs=pl.BlockSpec((1, D, columns_all), lambda step: (step, 0, 0)),
        out_shape=jax.ShapeDtypeStruct((blocks, D, columns_all), jnp.bfloat16),
        cost_estimate=pl.CostEstimate(
            flops=flops,
            bytes_accessed=2 * blocks * D * columns_all + 2 * sum(op.size for op in operands),
            transcendentals=0,
        ),
        compiler_params=pltpu.CompilerParams(vmem_limit_bytes=62 << 20),
    )(*operands)


def pack_kernel(head_cols, in_ref, outs_ref, qkv_ref, rest_ref):
    pairs = head_cols // PAIR
    for pair in range(pairs):
        for kind in range(3):
            source = (kind * pairs + pair) * PAIR
            place = (pair * 3 + kind) * PAIR
            qkv_ref[:, place : place + PAIR] = to_half(in_ref[:, source : source + PAIR])
    hidden_cols = in_ref.shape[1] - 3 * head_cols
    rest_ref[:, :hidden_cols] = to_half(in_ref[:, 3 * head_cols :])
    columns = to_half(outs_ref[...].T)
    rest_ref[:, hidden_cols : 2 * hidden_cols] = columns[:, head_cols:]
    rest_ref[:, 2 * hidden_cols :] = columns[:, :head_cols]


def pack_weights(w_in, w_outs, head_cols):
    rows = w_in.shape[0]
    hidden_cols = w_in.shape[1] - 3 * head_cols
    return pl.pallas_call(
        partial(pack_kernel, head_cols),
        out_shape=[
            jax.ShapeDtypeStruct((rows, 3 * head_cols), jnp.bfloat16),
            jax.ShapeDtypeStruct((rows, 2 * hidden_cols + head_cols), jnp.bfloat16),
        ],
    )(w_in, w_outs)


def swap_groups(array_in):
    dp_size = lax.axis_size("dp")
    tensor_size = lax.axis_size("tensor")
    pairs = [
        (row * tensor_size + column, column * dp_size + row)
        for row in range(dp_size)
        for column in range(tensor_size)
    ]
    return lax.ppermute(array_in, ("dp", "tensor"), pairs)


MESH_ID = pl.DeviceIdType.MESH


def places():
    dp_size, frame_size, tensor_size = [
        lax.axis_size(axis) for axis in ("dp", "frame", "tensor")
    ]
    here = [lax.axis_index(axis) for axis in ("dp", "frame", "tensor")]
    return (dp_size, frame_size, tensor_size, *here)


def device(row, frame, column):
    return {"dp": row, "frame": frame, "tensor": column}


def greet_plane():
    dp_size, frame_size, tensor_size, row, frame, column = places()
    plane = dp_size * frame_size
    barrier = pltpu.get_barrier_semaphore()
    for shift in range(1, plane):
        other = lax.rem(row * frame_size + frame + shift, plane)
        pl.semaphore_signal(
            barrier,
            inc=1,
            device_id=device(lax.div(other, frame_size), lax.rem(other, frame_size), column),
            device_id_type=MESH_ID,
        )
    pl.semaphore_wait(barrier, plane - 1)


def greet_all():
    dp_size, frame_size, tensor_size, row, frame, column = places()
    plane = dp_size * frame_size
    everyone = plane * tensor_size
    here = (row * frame_size + frame) * tensor_size + column
    barrier = pltpu.get_barrier_semaphore()

    def signal(shift, unused):
        other = lax.rem(here + shift, everyone)
        place = lax.div(other, tensor_size)
        pl.semaphore_signal(
            barrier,
            inc=1,
            device_id=device(
                lax.div(place, frame_size), lax.rem(place, frame_size), lax.rem(other, tensor_size)
            ),
            device_id_type=MESH_ID,
        )
        return unused

    lax.fori_loop(1, everyone, signal, 0)
    pl.semaphore_wait(barrier, everyone - 1)


def send(source, target, send_sem, receive_sem, device_id):
    return pltpu.make_async_remote_copy(
        src_ref=source,
        dst_ref=target,
        send_sem=send_sem,
        recv_sem=receive_sem,
        device_id=device_id,
        device_id_type=MESH_ID,
    )


def plane_copies(source_of, target_of, send_sems, receive_sems):
    dp_size, frame_size, tensor_size, row, frame, column = places()
    plane = dp_size * frame_size
    here = row * frame_size + frame
    copies = []
    for shift in range(1, plane):
        other = lax.rem(here + shift, plane)
        copies.append(
            send(
                source_of(other),
                target_of(here),
                send_sems.at[shift - 1],
                receive_sems.at[shift - 1],
                device(lax.div(other, frame_size), lax.rem(other, frame_size), column),
            )
        )
    return copies


def axis_copies(axis, source_of, target_of, send_sems, receive_sems):
    size = lax.axis_size(axis)
    here = lax.axis_index(axis)
    row, frame, column = [lax.axis_index(name) for name in ("dp", "frame", "tensor")]
    copies = []
    for shift in range(1, size):
        other = lax.rem(here + shift, size)
        target = device(other, frame, column) if axis == "dp" else device(row, frame, other)
        copies.append(
            send(
                source_of(other),
                target_of(here),
                send_sems.at[shift - 1],
                receive_sems.at[shift - 1],
                target,
            )
        )
    return copies


def plane_gather_kernel(count, *refs):
    ins = refs[:count]
    outs = refs[count : 2 * count]
    sems = refs[2 * count :]
    greet_plane()
    here = lax.axis_index("dp") * lax.axis_size("frame") + lax.axis_index("frame")
    copies = []
    for place in range(count):
        copies += plane_copies(
            lambda other, place=place: ins[place],
            lambda own, place=place: outs[place].at[own],
            sems[2 * place],
            sems[2 * place + 1],
        )
    for copy in copies:
        copy.start()
    for place in range(count):
        outs[place][here] = ins[place][...]
    for copy in copies:
        copy.wait()


def remote_call(kernel, collective_id, out_shape, scratch_shapes, operands):
    in_vmem = pl.BlockSpec(memory_space=pltpu.VMEM)
    return pl.pallas_call(
        kernel,
        out_shape=out_shape,
        in_specs=[in_vmem] * len(operands),
        out_specs=[in_vmem] * len(out_shape),
        scratch_shapes=scratch_shapes,
        compiler_params=pltpu.CompilerParams(
            collective_id=collective_id, has_side_effects=True, vmem_limit_bytes=48 << 20
        ),
    )(*operands)


def plane_gather(arrays):
    plane = lax.axis_size("dp") * lax.axis_size("frame")
    return remote_call(
        partial(plane_gather_kernel, len(arrays)),
        0,
        [jax.ShapeDtypeStruct((plane,) + array.shape, array.dtype) for array in arrays],
        [pltpu.SemaphoreType.DMA((plane - 1,))] * (2 * len(arrays)),
        arrays,
    )


def swap_block(block, swapped, send_sem, receive_sem, start):
    row, frame, column = [lax.axis_index(name) for name in ("dp", "frame", "tensor")]
    own = row == column
    copy = send(block, swapped, send_sem, receive_sem, device(column, frame, row))

    @pl.when(jnp.logical_not(own))
    def remote():
        copy.start() if start else copy.wait()

    if start:

        @pl.when(own)
        def keep():
            swapped[...] = block[...]


def mods_kernel(
    parts,
    out,
    received,
    block,
    swapped,
    plane_send,
    plane_receive,
    swap_send,
    swap_receive,
    spread_send,
    spread_receive,
):
    dp_size, frame_size, tensor_size, row, frame, column = places()
    plane = dp_size * frame_size
    here = row * frame_size + frame
    greet_all()
    copies = plane_copies(
        lambda other: parts.at[other], lambda own: received.at[own], plane_send, plane_receive
    )
    for copy in copies:
        copy.start()
    received[here] = parts[here]
    for copy in copies:
        copy.wait()
    total = received[0].astype(jnp.float32)
    for place in range(1, plane):
        total = total + received[place].astype(jnp.float32)
    block[...] = to_half(total)
    swap_block(block, swapped, swap_send.at[0], swap_receive.at[0], True)
    swap_block(block, swapped, swap_send.at[0], swap_receive.at[0], False)
    copies = axis_copies(
        "dp", lambda other: swapped, lambda own: out.at[own], spread_send, spread_receive
    )
    for copy in copies:
        copy.start()
    out[row] = swapped[...]
    for copy in copies:
        copy.wait()


def spread_mods(parts):
    plane, rows, columns = parts.shape
    dma = pltpu.SemaphoreType.DMA
    dp_size = lax.axis_size("dp")
    return remote_call(
        mods_kernel,
        1,
        [jax.ShapeDtypeStruct((dp_size, rows, columns), jnp.bfloat16)],
        [
            pltpu.VMEM(parts.shape, jnp.bfloat16),
            pltpu.VMEM(parts.shape[1:], jnp.bfloat16),
            pltpu.VMEM(parts.shape[1:], jnp.bfloat16),
            dma((plane - 1,)),
            dma((plane - 1,)),
            dma((1,)),
            dma((1,)),
            dma((dp_size - 1,)),
            dma((dp_size - 1,)),
        ],
        [parts],
    )[0]


def cond_kernel(
    mod_parts,
    patch_parts,
    weight,
    mod_all,
    cond_all,
    patch_out,
    mod_received,
    patch_received,
    mod_block,
    patch_block,
    patch_tensor,
    cond_part,
    cond_tensor,
    mod_swapped,
    cond_block,
    swap_send,
    swap_receive,
    dp_send,
    dp_receive,
    patch_send,
    patch_receive,
    spread_send,
    spread_receive,
    patch_tensor_send,
    patch_tensor_receive,
    cond_send,
    cond_receive,
    gather_send,
    gather_receive,
):
    dp_size, frame_size, tensor_size, row, frame, column = places()
    plane = dp_size * frame_size
    here = row * frame_size + frame
    greet_all()
    copies = axis_copies(
        "dp",
        lambda other: mod_parts.at[other],
        lambda own: mod_received.at[own],
        dp_send,
        dp_receive,
    ) + plane_copies(
        lambda other: patch_parts.at[other],
        lambda own: patch_received.at[own],
        patch_send,
        patch_receive,
    )
    for copy in copies:
        copy.start()
    mod_received[row] = mod_parts[row]
    patch_received[here] = patch_parts[here]
    for copy in copies:
        copy.wait()
    total = mod_received[0].astype(jnp.float32)
    for place in range(1, dp_size):
        total = total + mod_received[place].astype(jnp.float32)
    mod_block[...] = to_half(total)
    total = patch_received[0]
    for place in range(1, plane):
        total = total + patch_received[place]
    patch_block[...] = total
    swap_block(mod_block, mod_swapped, swap_send.at[0], swap_receive.at[0], True)
    patch_copies = axis_copies(
        "tensor",
        lambda other: patch_block,
        lambda own: patch_tensor.at[own],
        patch_tensor_send,
        patch_tensor_receive,
    )
    for copy in patch_copies:
        copy.start()
    patch_tensor[column] = patch_block[...]
    swap_block(mod_block, mod_swapped, swap_send.at[0], swap_receive.at[0], False)
    mod_copies = plane_copies(
        lambda other: mod_swapped, lambda own: mod_all.at[own], spread_send, spread_receive
    )
    cond_part[...] = to_half(contract(mod_swapped[...], weight[...], 1, 1))
    cond_copies = axis_copies(
        "tensor",
        lambda other: cond_part,
        lambda own: cond_tensor.at[own],
        cond_send,
        cond_receive,
    )
    for copy in cond_copies + mod_copies:
        copy.start()
    mod_all[here] = mod_swapped[...]
    cond_tensor[column] = cond_part[...]
    for copy in patch_copies + cond_copies:
        copy.wait()
    total = cond_tensor[0].astype(jnp.float32)
    total_patch = patch_tensor[0]
    for place in range(1, tensor_size):
        total = total + cond_tensor[place].astype(jnp.float32)
        total_patch = total_patch + patch_tensor[place]
    patch_out[...] = total_patch
    cond_block[...] = to_half(total)
    gather_copies = plane_copies(
        lambda other: cond_block, lambda own: cond_all.at[own], gather_send, gather_receive
    )
    for copy in gather_copies:
        copy.start()
    cond_all[here] = cond_block[...]
    for copy in gather_copies + mod_copies:
        copy.wait()


def cond_sums(mod_parts, patch_parts, weight):
    dp_size, rows, columns = mod_parts.shape
    plane = patch_parts.shape[0]
    tensor_size = lax.axis_size("tensor")
    features = weight.shape[0]

    def held(*shape):
        return pltpu.VMEM(shape, jnp.float32)

    def low(*shape):
        return pltpu.VMEM(shape, jnp.bfloat16)

    def sems(*counts):
        return [pltpu.SemaphoreType.DMA((count,)) for count in counts]

    patch_shape = patch_parts.shape[1:]
    return remote_call(
        cond_kernel,
        2,
        [
            jax.ShapeDtypeStruct((plane, rows, columns), jnp.bfloat16),
            jax.ShapeDtypeStruct((plane, rows, features), jnp.bfloat16),
            jax.ShapeDtypeStruct(patch_shape, jnp.float32),
        ],
        [
            low(*mod_parts.shape),
            held(*patch_parts.shape),
            low(rows, columns),
            held(*patch_shape),
            held(tensor_size, *patch_shape),
            low(rows, features),
            low(tensor_size, rows, features),
            low(rows, columns),
            low(rows, features),
        ]
        + sems(1, 1, dp_size - 1, dp_size - 1, *[plane - 1] * 4)
        + sems(*[tensor_size - 1] * 4, plane - 1, plane - 1),
        [mod_parts, patch_parts, weight],
    )


def total_kernel(tile, out, received, send_sems, receive_sems):
    dp_size, frame_size, tensor_size, row, frame, column = places()
    everyone = dp_size * frame_size * tensor_size
    here = (row * frame_size + frame) * tensor_size + column
    greet_all()

    def copy_to(shift):
        other = lax.rem(here + shift, everyone)
        place = lax.div(other, tensor_size)
        return send(
            tile,
            received.at[here],
            send_sems.at[shift - 1],
            receive_sems.at[shift - 1],
            device(
                lax.div(place, frame_size), lax.rem(place, frame_size), lax.rem(other, tensor_size)
            ),
        )

    def start(shift, unused):
        copy_to(shift).start()
        return unused

    def finish(shift, unused):
        copy_to(shift).wait()
        return unused

    lax.fori_loop(1, everyone, start, 0)
    received[here] = tile[...]
    lax.fori_loop(1, everyone, finish, 0)
    out[...] = jnp.sum(received[...], axis=0)


def total_over_all(first, second):
    lane = jnp.arange(PAIR)[None, :]
    tile = jnp.where(lane == 0, first, jnp.where(lane == 1, second, 0.0))
    tile = jnp.broadcast_to(tile, (8, PAIR)).astype(jnp.float32)
    everyone = lax.axis_size(EVERY)
    sums = remote_call(
        total_kernel,
        3,
        [jax.ShapeDtypeStruct((8, PAIR), jnp.float32)],
        [
            pltpu.VMEM((everyone, 8, PAIR), jnp.float32),
            pltpu.SemaphoreType.DMA((everyone - 1,)),
            pltpu.SemaphoreType.DMA((everyone - 1,)),
        ],
        [tile],
    )[0]
    return (sums[0, 0], sums[0, 1])


def spread_heads():
    return (D // PAIR) % (lax.axis_size("dp") * lax.axis_size("frame")) == 0


def exchange_axes():
    axes = PLANE if spread_heads() else ("dp",)
    return (axes, math.prod(lax.axis_size(axis) for axis in axes))


def to_heads(pairs_in):
    axes, parts = exchange_axes()
    pairs, tokens, columns = pairs_in.shape
    moved = lax.all_to_all(
        pairs_in.reshape(parts, pairs // parts, tokens, columns), axes, 0, 0, tiled=True
    )
    return jnp.swapaxes(moved, 0, 1).reshape(pairs // parts, parts * tokens, columns)


def to_tokens(units_in):
    axes, parts = exchange_axes()
    units, tokens_all, columns = units_in.shape
    by_place = jnp.swapaxes(units_in.reshape(units, parts, tokens_all // parts, columns), 0, 1)
    moved = lax.all_to_all(by_place, axes, 0, 0, tiled=True)
    return moved.reshape(parts * units, tokens_all // parts, columns)


def gather_blocks(shard):
    whole = lax.all_gather(shard, EVERY, axis=0, tiled=True)
    return whole.reshape(lax.axis_size("tensor"), D, -1)


def scatter_blocks(blocks_in):
    flat = blocks_in.reshape(-1, blocks_in.shape[-1])
    return lax.psum_scatter(flat, EVERY, scatter_dimension=0, tiled=True)


def scatter_stages(blocks_in):
    dp_size, frame_size, tensor_size, row, frame, column = places()
    pairs_dp = dp_size // 2
    side = lax.rem(row, 2)
    columns = blocks_in.shape[-1]
    parted = blocks_in.reshape(tensor_size, pairs_dp, 2, frame_size, -1, columns)

    def of_side(which):
        return lax.dynamic_index_in_dim(parted, which, 2, keepdims=False)

    swaps = [(place, place + 1 - 2 * (place % 2)) for place in range(dp_size)]
    received = lax.ppermute(of_side(1 - side), "dp", swaps)
    halves = to_half(of_side(side).astype(jnp.float32) + received.astype(jnp.float32))
    members = pairs_dp * frame_size
    halves = jnp.moveaxis(halves, 0, 2).reshape(members, tensor_size, -1, columns)
    here = lax.div(row, 2) * frame_size + frame
    total = lax.dynamic_index_in_dim(halves, here, 0, keepdims=False).astype(jnp.float32)
    moved = []
    for shift in range(1, members):
        routes = []
        for source in range(members):
            target = (source + shift) % members
            for core in range(2):
                source_row = source // frame_size * 2 + core
                target_row = target // frame_size * 2 + core
                routes.append(
                    (
                        source_row * frame_size + source % frame_size,
                        target_row * frame_size + target % frame_size,
                    )
                )
        block = lax.dynamic_index_in_dim(
            halves, lax.rem(here + shift, members), 0, keepdims=False
        )
        moved.append(lax.ppermute(block, PLANE, routes))
    for block in moved:
        total = total + block.astype(jnp.float32)
    over_tensor = lax.all_to_all(to_half(total), "tensor", 0, 0, tiled=True)
    return jnp.sum(over_tensor.astype(jnp.float32), axis=0)


def pad_lanes(rows_in, axis):
    widths = [(0, 0)] * rows_in.ndim
    widths[axis] = (0, PAIR - rows_in.shape[axis])
    return jnp.pad(rows_in, widths)


def after(value, *others):
    return lax.optimization_barrier((value,) + others)[0]


def update_part(refs, rows, columns, gradient, rates):
    master_ref, first_ref, second_ref, master_out, first_out, second_out, half_out = refs
    factor, fix_first, fix_second = rates
    place = (Ellipsis, rows, columns)
    master = master_ref[place]
    clipped = gradient * factor
    first_new = BETA_FIRST * first_ref[place] + (1.0 - BETA_FIRST) * clipped
    second_new = BETA_SECOND * second_ref[place] + (1.0 - BETA_SECOND) * clipped * clipped
    step_dir = first_new / fix_first / (jnp.sqrt(second_new / fix_second) + ADAM_EPS)
    master_new = master - LEARN_RATE * (step_dir + WEIGHT_DECAY * master)
    master_out[place] = master_new
    first_out[place] = first_new
    second_out[place] = second_new
    half_out[place] = to_half(master_new)


def update_kernel(head_cols, rates_ref, qkv_ref, rest_ref, cond_ref, time_ref, patch_ref, *refs):
    rates = (rates_ref[0], rates_ref[1], rates_ref[2])
    sets = [refs[which::5] for which in range(5)]
    everything = slice(None)
    pairs = head_cols // PAIR
    for pair in range(pairs):
        for kind in range(3):
            source = (pair * 3 + kind) * PAIR
            place = (kind * pairs + pair) * PAIR
            update_part(
                sets[0],
                everything,
                slice(place, place + PAIR),
                qkv_ref[:, source : source + PAIR].astype(jnp.float32),
                rates,
            )
    qkv_cols = 3 * head_cols
    hidden_cols = sets[0][0].shape[1] - qkv_cols
    for start in range(0, hidden_cols, 256):
        update_part(
            sets[0],
            everything,
            slice(qkv_cols + start, qkv_cols + start + 256),
            rest_ref[:, start : start + 256].astype(jnp.float32),
            rates,
        )
    for start in range(0, hidden_cols + head_cols, 256):
        source = 2 * hidden_cols if start == 0 else hidden_cols + start - head_cols
        gradient = rest_ref[:, source : source + 256].astype(jnp.float32).T
        update_part(sets[1], slice(start, start + 256), everything, gradient, rates)
    for start in range(0, cond_ref.shape[1], 256):
        columns = slice(start, start + 256)
        update_part(sets[2], everything, columns, cond_ref[:, columns], rates)
    for start in range(0, D, 256):
        columns = slice(start, start + 256)
        update_part(sets[3], everything, columns, time_ref[:, columns], rates)
    update_part(sets[4], everything, everything, patch_ref[...], rates)


def update_all(rates, gradients, masters, firsts, seconds, head_cols):
    operands = list(gradients) + list(masters) + list(firsts) + list(seconds)
    shapes = [master.shape for master in masters]
    in_vmem = pl.BlockSpec(memory_space=pltpu.VMEM)
    return pl.pallas_call(
        partial(update_kernel, head_cols),
        in_specs=[pl.BlockSpec(memory_space=pltpu.SMEM)] + [in_vmem] * len(operands),
        out_specs=[in_vmem] * 20,
        out_shape=[jax.ShapeDtypeStruct(shape, jnp.float32) for shape in shapes] * 3
        + [jax.ShapeDtypeStruct(shape, jnp.bfloat16) for shape in shapes],
        compiler_params=pltpu.CompilerParams(vmem_limit_bytes=60 << 20),
    )(rates, *operands)


def shards(
    latent,
    noise_draw,
    levels,
    context,
    step_count,
    w_in,
    w_outs,
    w_cond,
    w_time,
    w_patch,
    m_in,
    m_outs,
    m_cond,
    m_time,
    m_patch,
    v_in,
    v_outs,
    v_cond,
    v_time,
    v_patch,
):
    head_cols = D // lax.axis_size("tensor")
    pairs_block = head_cols // PAIR
    pairs_all = D // PAIR
    masters = (w_in, w_outs, w_cond, w_time, w_patch)
    clips, frames_here, patch_rows, width = latent.shape
    groups = clips * frames_here
    plane_index = lax.axis_index(PLANE)
    half_cond, half_time, half_patch = [to_half(m) for m in masters[2:]]
    hidden_cols = w_in.shape[1] - 3 * head_cols
    shard_qkv, shard_rest = pack_weights(w_in, w_outs, head_cols)

    w_qkv = gather_blocks(shard_qkv)
    level_rows = jnp.pad(
        levels.astype(jnp.float32), ((0, 8 - clips), (0, PAIR - frames_here))
    )
    time_places, patch_places, level_places = plane_gather([half_time, half_patch, level_rows])
    time_whole = time_places.reshape(-1, D)
    patch_whole = jnp.moveaxis(patch_places, 0, 2).reshape(2, PD, D)
    fields = swap_groups(jnp.stack([latent, noise_draw]))
    levels_all = level_places[:, :clips, :frames_here]
    blocks = lax.axis_size("tensor")
    w_first = time_whole[:TEMB]
    w_second = time_whole[TEMB:]
    w_embed = pad_lanes(patch_whole[0], 0)
    w_head = pad_lanes(patch_whole[1], 0)

    token_total = (TOKF * jnp.sum(FRAMES - context)).astype(jnp.float32)
    dp_size = lax.axis_size("dp")
    frame_size = lax.axis_size("frame")
    clip_ids = jnp.arange(dp_size * clips, dtype=jnp.int32).reshape(dp_size, 1, clips, 1)
    frame_ids = jnp.arange(FRAMES, dtype=jnp.int32).reshape(1, frame_size, 1, frames_here)
    clean_all = frame_ids < context[clip_ids]
    level_all = jnp.where(
        clean_all, 0.0, levels_all.reshape(dp_size, frame_size, clips, frames_here)
    )
    embed_low = to_half(frequency_table(level_all.reshape(-1)))
    hidden_time = product(embed_low, w_first)
    first_low = to_half(jax.nn.silu(hidden_time))
    cond_vec = product(first_low, w_second)
    cond_low = to_half(jax.nn.silu(cond_vec))
    frame_index = lax.axis_index("frame")
    tensor_index = lax.axis_index("tensor")
    cond_rows = half_cond.shape[0]
    cond_own = lax.dynamic_slice_in_dim(cond_low, plane_index * cond_rows, cond_rows, 1)
    mod_parts = product(cond_own, half_cond).reshape(dp_size * frame_size, groups, -1)
    def own_part(whole):
        part = lax.dynamic_index_in_dim(whole, tensor_index, 0, keepdims=False)
        return lax.dynamic_index_in_dim(part, frame_index, 0, keepdims=False)

    clean_frames = own_part(clean_all)
    alpha_coef, sigma_coef = noise_terms(own_part(level_all))
    alpha_field = alpha_coef[:, :, None, None]
    sigma_field = sigma_coef[:, :, None, None]
    clean_field = fields[0].astype(jnp.float32)
    noise_field = fields[1].astype(jnp.float32)
    noisy_field = alpha_field * clean_field + sigma_field * noise_field
    target = alpha_field * noise_field - sigma_field * clean_field
    patch_low = pad_lanes(to_half(patchify(noisy_field).reshape(clips, -1, PD)), 2)
    goal_rows = pad_lanes(patchify(target).reshape(clips, -1, PD), 2)
    coef = (1.0 - clean_frames.astype(jnp.float32)) / token_total
    coef_rows = jnp.broadcast_to(coef[:, :, None], (clips, frames_here, PAIR))


    mod_parts, patch_low, goal_rows, coef_rows = lax.optimization_barrier(
        (mod_parts, patch_low, goal_rows, coef_rows)
    )
    modulation = jnp.swapaxes(spread_mods(to_half(mod_parts)), 0, 1).astype(jnp.float32)
    mods = modulation.reshape(clips, frames_here, -1)

    spread = spread_heads()
    each_clip = range(clips)
    opened = [
        open_layer(patch_low[clip], w_embed, mods[clip], w_qkv) for clip in each_clip
    ]
    rows_in = [parts[0] for parts in opened]
    flat_one = [parts[1] for parts in opened]
    kept = []
    mixed_pairs = []
    mixed_lows = []
    for clip in each_clip:
        qkv_send = opened[clip][2]
        if clip > 1:
            qkv_send = after(qkv_send, mixed_lows[clip - 2])
        qkv_heads = to_heads(qkv_send)
        if clip == 0:
            w_rest = gather_blocks(after(shard_rest, qkv_heads, *rows_in[1:]))
            cond_whole = lax.all_gather(after(half_cond, w_rest), PLANE, axis=0, tiled=True)
        else:
            qkv_heads = after(qkv_heads, mixed_lows[clip - 1])
        if spread:
            key_value, key_place = qkv_heads, 1
        else:
            key_value = lax.all_gather(qkv_heads[..., PAIR:], "frame", axis=1, tiled=True)
            key_place = 0
        exps, mixed_low, mixed, inverse = attend(qkv_heads, key_value, key_place)
        kept.append((exps, qkv_heads, key_value, key_place, mixed, inverse))
        mixed_lows.append(mixed_low)
    middles = []
    grad_heads = []
    for clip in each_clip:
        gates = mixed_lows[clip + 1 : clip + 2]
        if not gates and clip > 1:
            gates = [middles[clip - 2][5]]
        mixed_pairs.append(to_tokens(after(mixed_lows[clip], *gates)))
        middles.append(
            middle_layer(
                mixed_pairs[clip],
                rows_in[clip],
                mods[clip],
                goal_rows[clip],
                coef_rows[clip],
                w_head,
                w_rest,
                head_cols,
                hidden_cols,
            )
        )
    flat_two, act_low, grad_mlp, grad_hidden, grad_attn, grad_rows = [
        [parts[place] for parts in middles] for place in range(6)
    ]
    loss_part = sum(jnp.sum(parts[9]) for parts in middles)
    grad_head = sum(parts[8][:PD] for parts in middles)
    grad_heads = [to_heads(after(middles[0][6], middles[1 % clips][5]))]
    flat_two[-1] = after(flat_two[-1], *grad_heads)
    grad_rest = weight_grads(
        blocks,
        [(flat_two, grad_hidden), (grad_mlp, act_low), (grad_attn, mixed_pairs)],
    )
    scattered_rest = scatter_blocks(after(grad_rest, cond_whole))
    if clips > 1:
        sends = after(jnp.concatenate([parts[6] for parts in middles[1:]], axis=1), grad_rest)
        together = to_heads(sends).reshape(
            kept[0][5].shape[0], -1, clips - 1, sends.shape[1] // (clips - 1), PAIR
        )
        grad_heads += [
            together[:, :, clip].reshape(together.shape[0], -1, PAIR) for clip in range(clips - 1)
        ]
    grad_pairs = []
    for clip in each_clip:
        exps, qkv_heads, key_value, key_place, mixed, inverse = kept[clip]
        grad_now = after(grad_heads[clip], grad_rest)
        if clip > 1:
            grad_now = after(grad_now, grad_pairs[clip - 2])
        grads = attend_back(exps, qkv_heads, key_value, key_place, grad_now, mixed, inverse)
        if not spread:
            grads = [grads[0]] + [
                lax.psum_scatter(grad, "frame", scatter_dimension=1, tiled=True)
                for grad in grads[1:]
            ]
        grad_units = grads[0] if len(grads) == 1 else jnp.concatenate(grads, axis=-1)
        grad_pairs.append(to_tokens(grad_units))
    closed = []
    for clip in each_clip:
        if clip == clips - 1:
            grad_pairs[clip] = after(
                grad_pairs[clip], scattered_rest, *[parts[0] for parts in closed]
            )
            grad_wqkv = weight_grads(blocks, [(flat_one, grad_pairs)])
            scattered_qkv = scatter_stages(grad_wqkv)
            grad_pairs[clip] = after(grad_pairs[clip], grad_wqkv)
        closed.append(
            close_layer(
                grad_pairs[clip], rows_in[clip], grad_rows[clip], mods[clip], patch_low[clip], w_qkv
            )
        )
    grad_embed = sum(parts[1][:PD] for parts in closed)
    patch_cols = half_patch.shape[2]
    patch_parts = jnp.swapaxes(
        jnp.concatenate([grad_embed, grad_head], axis=0).reshape(2 * PD, -1, patch_cols), 0, 1
    )
    grad_mod = jnp.stack(
        [jnp.concatenate([closed[clip][0], middles[clip][7]], axis=0) for clip in each_clip]
    )
    mod_parts = jnp.transpose(
        grad_mod.reshape(clips, dp_size, -1, frames_here, D), (1, 0, 3, 2, 4)
    ).reshape(dp_size, groups, -1)
    mod_all, cond_places, patch_block = cond_sums(to_half(mod_parts), patch_parts, cond_whole)
    mod_all = mod_all.reshape(-1, mod_all.shape[-1])
    grad_cond_all = cond_places.reshape(-1, D).astype(jnp.float32)
    final_patch = patch_block.reshape(2, PD, patch_cols)
    final_cond = rows_product(cond_own, mod_all)
    unused, silu_cond = jax.vjp(jax.nn.silu, cond_vec)
    grad_cond_low = to_half(silu_cond(grad_cond_all)[0])
    grad_second = rows_product(first_low, grad_cond_low)
    grad_first_act = cols_product(grad_cond_low, w_second)
    unused, silu_first = jax.vjp(jax.nn.silu, hidden_time)
    grad_hidden_time = to_half(silu_first(grad_first_act)[0])
    grad_first = rows_product(embed_low, grad_hidden_time)
    time_rows = half_time.shape[0]
    final_time = lax.dynamic_slice_in_dim(
        jnp.concatenate([grad_first, grad_second], axis=0), plane_index * time_rows, time_rows, 0
    )
    def square_sum(gradient):
        wide = gradient.astype(jnp.float32)
        return jnp.sum(wide * wide)

    split_square = sum(square_sum(part) for part in (scattered_qkv, scattered_rest, final_cond))
    shared_square = (square_sum(final_time) + square_sum(final_patch)) / blocks
    totals = total_over_all(loss_part, split_square + shared_square)
    loss_value = totals[0]
    grad_norm = jnp.sqrt(totals[1])
    factor = jnp.minimum(1.0, MAX_NORM / (grad_norm + 1e-06))
    steps_done = step_count[0].astype(jnp.float32)
    fix_first = 1.0 - BETA_FIRST**steps_done
    fix_second = 1.0 - BETA_SECOND**steps_done
    results = update_all(
        jnp.stack([factor, fix_first, fix_second]),
        (scattered_qkv, scattered_rest, final_cond, final_time, final_patch),
        masters,
        (m_in, m_outs, m_cond, m_time, m_patch),
        (v_in, v_outs, v_cond, v_time, v_patch),
        head_cols,
    )
    return (loss_value, grad_norm, *results)


def solution(mesh):
    placed = (
        P("dp", "frame", "tensor", None),
        P("dp", "frame", "tensor", None),
        P("dp", "frame"),
        P(),
        P(),
        P(("dp", "frame"), "tensor"),
        P("tensor", ("dp", "frame")),
        P(("dp", "frame"), "tensor"),
        P(("dp", "frame"), None),
        P(None, None, ("dp", "frame")),
        P(("dp", "frame"), "tensor"),
        P("tensor", ("dp", "frame")),
        P(("dp", "frame"), "tensor"),
        P(("dp", "frame"), None),
        P(None, None, ("dp", "frame")),
        P(("dp", "frame"), "tensor"),
        P("tensor", ("dp", "frame")),
        P(("dp", "frame"), "tensor"),
        P(("dp", "frame"), None),
        P(None, None, ("dp", "frame")),
    )
    return jax.shard_map(
        shards,
        mesh=mesh,
        in_specs=placed,
        out_specs=(
            P(),
            P(),
            P(("dp", "frame"), "tensor"),
            P("tensor", ("dp", "frame")),
            P(("dp", "frame"), "tensor"),
            P(("dp", "frame"), None),
            P(None, None, ("dp", "frame")),
            P(("dp", "frame"), "tensor"),
            P("tensor", ("dp", "frame")),
            P(("dp", "frame"), "tensor"),
            P(("dp", "frame"), None),
            P(None, None, ("dp", "frame")),
            P(("dp", "frame"), "tensor"),
            P("tensor", ("dp", "frame")),
            P(("dp", "frame"), "tensor"),
            P(("dp", "frame"), None),
            P(None, None, ("dp", "frame")),
            P(("dp", "frame"), "tensor"),
            P("tensor", ("dp", "frame")),
            P(("dp", "frame"), "tensor"),
            P(("dp", "frame"), None),
            P(None, None, ("dp", "frame")),
        ),
        check_vma=False,
    )
```
